512 devices in a mesh: gx: 32 (over y, x), gy: 16 (over z, core).
Axes of the slice: x: 4, y: 8, z: 8, core: 2. Of those that a mesh axis runs over, the one named last changes fastest.
Arguments:
- source: float32 [4, 2048, 4096], P(None, 'gx', 'gy'), may hold values from -8 to 8
- reaction: float32 [2048, 4096], P('gx', 'gy'), may hold values from 0.001 to 0.06
- coupling: float32 [4, 4], replicated, may hold values from -0.025 to 0.015
- solid0: int32 [2048, 4096], P('gx', 'gy'), may hold values 0 or 1
- solid1: int32 [1024, 2048], P('gx', 'gy'), may hold values 0 or 1
- solid2: int32 [512, 1024], P('gx', 'gy'), may hold values 0 or 1
- solid3: int32 [256, 512], P('gx', 'gy'), may hold values 0 or 1
Outputs:
- displacement: float32 [4, 2048, 4096], P(None, 'gx', 'gy')
- residual: float32 [4, 2048, 4096], P(None, 'gx', 'gy')
The draws below stay inside these ranges and needn't reach their ends.
All inputs are finite; a program needn't handle non-finite values. No bound on the sum of `solid0` or of `solid1` or of `solid2` or of `solid3` on one device may be relied on, other than what follows from the above.
Results may differ from the reference program's by a relative error of at most 0.0003.
Values sent between devices are 32-bit elements; how exact they have to be, the bound alone decides.
No kernel may reach another device: no remote copies, remote signals or barrier semaphores. Data moves between devices by JAX's collectives and lax.ppermute only.
A program may use at most 128 MiB of HBM per device.

```python
import math
import jax
import jax.numpy as jnp
from jax import lax

FIELDS = 4
CYCLES = 2
SWEEPS = 2
COARSE_SWEEPS = 6
NX = 2048
NY = 4096


def draw_source(key, part):
    key = jax.random.fold_in(key, 11)
    values = jnp.clip(jax.random.normal(key, (FIELDS, NX, NY), jnp.float32), -8.0, 8.0)
    return values


def draw_reaction(key, part):
    key = jax.random.fold_in(key, 23)
    lower = math.log(0.002)
    upper = math.log(0.06)
    return jnp.exp(jax.random.uniform(key, (NX, NY), jnp.float32, lower, upper))


def draw_coupling(key, part):
    key = jax.random.fold_in(key, 37)
    values = jax.random.uniform(key, (FIELDS, FIELDS), jnp.float32, -0.015, 0.015)
    return values


def plant(result, own_key, smallest, high):
    index_at = [jax.random.randint(jax.random.fold_in(own_key, axis), (), 0, length) for axis, length in enumerate(result.shape)]
    widest = result.shape.index(max(result.shape))
    beside = index_at[:widest] + [(index_at[widest] + 1) % result.shape[widest]] + index_at[widest + 1:]
    return result.at[tuple(index_at)].set(smallest).at[tuple(beside)].set(high)


def setup_inputs(seed: int = 0) -> dict:
    key_of = jax.random.split(jax.random.key(seed), 8)
    source = draw_source(jax.random.fold_in(key_of[7], 71), 0)
    reaction = draw_reaction(jax.random.fold_in(key_of[7], 71), 0)
    coupling = draw_coupling(jax.random.fold_in(key_of[7], 71), 0)
    solid0 = plant((jax.random.randint(key_of[3], (NX, NY), 0, 50) < 49).astype(jnp.int32), jax.random.fold_in(key_of[3], 1), 0, 1)
    solid1 = plant((jax.random.randint(key_of[4], (NX // 2, NY // 2), 0, 50) < 49).astype(jnp.int32), jax.random.fold_in(key_of[4], 1), 0, 1)
    solid2 = plant((jax.random.randint(key_of[5], (NX // 4, NY // 4), 0, 50) < 49).astype(jnp.int32), jax.random.fold_in(key_of[5], 1), 0, 1)
    solid3 = plant((jax.random.randint(key_of[6], (NX // 8, NY // 8), 0, 50) < 49).astype(jnp.int32), jax.random.fold_in(key_of[6], 1), 0, 1)
    return {"source": source, "reaction": reaction, "coupling": coupling, "solid0": solid0, "solid1": solid1, "solid2": solid2, "solid3": solid3}


OMEGA = 0.6


def neighbours(masked):
    padded = jnp.pad(masked, ((0, 0), (1, 1), (1, 1)))
    return padded[:, 2:, 1:-1] + padded[:, :-2, 1:-1] + padded[:, 1:-1, 2:] + padded[:, 1:-1, :-2]


def apply_level(field, solid, react, coupling, scale):
    masked = solid * field
    mixed = jnp.einsum("ab,bxy->axy", coupling, field, precision=lax.Precision.HIGHEST)
    return scale * (4.0 * field - solid * neighbours(masked)) + react * field + mixed


def coarsen(values):
    lead, rows, cols = values.shape
    return values.reshape(lead, rows // 2, 2, cols // 2, 2).mean(axis=(2, 4))


def refine(values):
    return jnp.repeat(jnp.repeat(values, 2, axis=1), 2, axis=2)


def cycle(level, rhs, field, levels, coupling):
    solid, react, scale, divisor = levels[level]

    def sweep(current):
        return current + OMEGA * (rhs - apply_level(current, solid, react, coupling, scale)) / divisor

    if level == 3:
        for index in range(COARSE_SWEEPS):
            field = sweep(field)
        leftover = rhs - apply_level(field, solid, react, coupling, scale)
        full_div = divisor + jnp.zeros_like(field)
        field = field + jnp.sum(leftover, axis=1, keepdims=True) / jnp.sum(full_div, axis=1, keepdims=True)
        return field
    for index in range(SWEEPS):
        field = sweep(field)
    error = rhs - apply_level(field, solid, react, coupling, scale)
    coarse_rhs = coarsen(error)
    correction = cycle(level + 1, coarse_rhs, jnp.zeros_like(coarse_rhs), levels, coupling)
    field = field + refine(correction)
    for index in range(SWEEPS):
        field = sweep(field)
    return field


def reference(source, reaction, coupling, solid0, solid1, solid2, solid3):
    masks = [solid0, solid1, solid2, solid3]
    react = reaction[None]
    levels = []
    for level in range(4):
        solid = masks[level].astype(jnp.float32)[None]
        scale = 4.0 ** (-level)
        divisor = 4.0 * scale + react + jnp.diagonal(coupling)[:, None, None]
        levels.append((solid, react, scale, divisor))
        react = coarsen(react)
    field = jnp.zeros_like(source)
    for index in range(CYCLES):
        field = cycle(0, source, field, levels, coupling)
    residual = source - apply_level(field, levels[0][0], levels[0][1], coupling, 1.0)
    return field, residual
```

```python
import functools

import jax
import jax.numpy as jnp
from jax import lax
from jax.experimental import pallas as pl
from jax.experimental.pallas import tpu as pltpu
from jax.sharding import PartitionSpec as P


F = 4
ROWS = (8, 4, 2)
COLS = (4, 2, 1)
SCALE = (1.0, 0.25, 0.0625, 0.015625)
OMEGA = 0.6
TILES = 102
XTILES = 64
F32 = jnp.float32
BF16 = jnp.bfloat16


def lanes(shape):
    return lax.broadcasted_iota(jnp.int32, shape, len(shape) - 1)


def sublanes(shape):
    return lax.broadcasted_iota(jnp.int32, shape, len(shape) - 2)


def roll(value, shift, axis):
    size = value.shape[axis]
    shift = shift % size
    return value if shift == 0 else pltpu.roll(value, shift, axis)


def three(value):
    high = value.astype(BF16)
    rest = value - high.astype(F32)
    mid = rest.astype(BF16)
    low = (rest - mid.astype(F32)).astype(BF16)
    return high, mid, low


def exact_dot(value, matrix):
    parts = [jnp.dot(part, matrix, preferred_element_type=F32) for part in three(value)]
    return parts[0] + (parts[1] + parts[2])


def split_matrix(size, stride):
    c = lax.broadcasted_iota(jnp.int32, (size, size), 0)
    o = lax.broadcasted_iota(jnp.int32, (size, size), 1)
    return jnp.where(o == (c % stride) * (size // stride) + c // stride, 1.0, 0.0).astype(BF16)


def join_matrix(size, stride):
    o = lax.broadcasted_iota(jnp.int32, (size, size), 0)
    c = lax.broadcasted_iota(jnp.int32, (size, size), 1)
    return jnp.where(o == (c % stride) * (size // stride) + c // stride, 1.0, 0.0).astype(BF16)


def pack_rows(own, up, dn, count):
    low = sublanes((8, 128)) < 4

    def body(n, _):
        a = own[2 * n]
        b = own[2 * n + 1]
        up[n] = jnp.where(low, a, roll(b, 4, 0))
        dn[n] = jnp.where(low, roll(a, 4, 0), b)
        return _

    lax.fori_loop(0, count // 2, body, 0, unroll=3 if count % 6 == 0 else 4)


def outer_rows(up, dn, n, odd):
    low = sublanes((8, 128)) < 4
    if odd:
        return jnp.where(low, roll(up[n], 4, 0), dn[n])
    return jnp.where(low, up[n], roll(dn[n], 4, 0))


def pack_kernel(source, reaction, solid0, solid1, solid2, solid3, own, up, dn, stage, small):
    matrix = split_matrix(256, 4)
    for a in range(6):
        if a < 4:
            value = exact_dot(source[a], matrix)
        elif a == 4:
            value = exact_dot(reaction[...], matrix)
        else:
            value = jnp.dot(
                solid0[...].astype(F32).astype(BF16), matrix, preferred_element_type=F32
            )
        for h in range(2):
            stage[a, h] = value[:, 128 * h : 128 * h + 128]
    for a in range(6):
        for q in range(8):
            for h in range(2):
                own[a * 16 + q * 2 + h] = stage[a, h, pl.ds(q, 8, stride=8), :]
    small[...] = jnp.dot(
        solid1[...].astype(F32).astype(BF16),
        split_matrix(128, 2),
        preferred_element_type=F32,
    )
    for q in range(4):
        own[96 + q] = small[pl.ds(q, 8, stride=4), :]
    c = lax.broadcasted_iota(jnp.int32, (64, 128), 0)
    o = lax.broadcasted_iota(jnp.int32, (64, 128), 1)
    wide = jnp.where(o % 64 == c, 1.0, 0.0).astype(BF16)
    small[pl.ds(0, 16), :] = jnp.dot(
        solid2[...].astype(F32).astype(BF16), wide, preferred_element_type=F32
    )
    own[100] = jnp.where(
        lanes((8, 128)) < 64,
        small[pl.ds(0, 8, stride=2), :],
        small[pl.ds(1, 8, stride=2), :],
    )
    c = lax.broadcasted_iota(jnp.int32, (32, 128), 0)
    o = lax.broadcasted_iota(jnp.int32, (32, 128), 1)
    twice = jnp.where((o % 64) // 2 == c, 1.0, 0.0)
    own[101] = jnp.dot(
        solid3[...].astype(F32), twice, preferred_element_type=F32,
        precision=lax.Precision.HIGHEST,
    )
    pack_rows(own, up, dn, TILES)


def side_kernel(count, own, up, dn, right, left):
    lane = lanes((8, 128)) % 64

    def group(g, members):
        for v in range(2):
            tiles = []
            for t in range(members):
                index = 3 * g + t
                if v == 0:
                    tiles.append(own[index])
                else:
                    n = index // 2
                    low = sublanes((8, 128)) < 4
                    turn = lax.broadcast(index % 2, (8, 128)) == 1
                    a, b = up[n], dn[n]
                    even = jnp.where(low, a, roll(b, 4, 0))
                    odd = jnp.where(low, roll(a, 4, 0), b)
                    tiles.append(jnp.where(turn, odd, even))
            r, l = tiles[0], tiles[0]
            for t in range(1, members):
                r = jnp.where(lane < 64 - 20 * t, roll(tiles[t], -20 * t, 1), r)
                l = jnp.where(lane >= 20 * t, roll(tiles[t], 20 * t, 1), l)
            right[g, v] = r
            left[g, v] = l

    def body(g, _):
        group(g, 3)
        return _

    lax.fori_loop(0, count // 3, body, 0, unroll=2)
    if count % 3:
        group(jnp.int32(count // 3), count % 3)


def widen(own, up, dn, right, left, index):
    lane = lanes((8, 128))
    g, t = index // 3, index % 3
    out = [[], []]
    for v in range(2):
        mine = own[index] if v == 0 else outer_rows(up, dn, index // 2, index % 2)
        r, l = right[g, v], left[g, v]
        for h in range(2):
            centre = roll(mine, 64 * h, 1)
            before = roll(r, 64 + 20 * t + 64 * h, 1)
            after = roll(l, 64 - 20 * t + 64 * h, 1)
            tile = jnp.where(lane < 64, centre, jnp.where(lane < 84, after, 0.0))
            out[h].append(jnp.where(lane >= 108, before, tile))
    return [jnp.concatenate(pair, axis=0) for pair in out]


def fix_ends(masked, level):
    R, C = ROWS[level], COLS[level]
    for f in range(F):
        for p in range(C):
            masked[f, 0, p + 1] = roll(masked[f, R, p + 1], 1, 0)
            masked[f, R + 1, p + 1] = roll(masked[f, 1, p + 1], -1, 0)


def put_masked(masked, level, f, q, p, value):
    C = COLS[level]
    masked[f, q + 1, p + 1] = value
    if p == 0:
        masked[f, q + 1, C + 1] = roll(value, -1, 1)
    if p == C - 1:
        masked[f, q + 1, 0] = roll(value, 1, 1)


def each_row(count, body):
    if count > 4:
        def step(q, _):
            body(q)
            return _

        lax.fori_loop(0, count, step, 0)
    else:
        for q in range(count):
            body(q)


def drive(level, K, x, masked, rhs, solid, q, p, rows=slice(None)):
    xs = [x[f, q, p, rows] for f in range(F)]
    weight = solid[q, p, rows]
    if level:
        weight = weight * SCALE[level]
    out = []
    for f in range(F):
        near = (masked[f, q, p + 1, rows] + masked[f, q + 2, p + 1, rows]) + (
            masked[f, q + 1, p, rows] + masked[f, q + 1, p + 2, rows]
        )
        total = rhs[f, q, p, rows] + weight * near
        mixed = None
        for b in range(F):
            if b != f:
                term = K[f, b] * xs[b]
                mixed = term if mixed is None else mixed + term
        out.append(total - mixed)
    return out, xs


def sweep(level, K, x, masked, target, rhs, solid, inverse, last=False):
    R, C = ROWS[level], COLS[level]

    def body(q):
        for p in range(C):
            drives, xs = drive(level, K, x, masked, rhs, solid, q, p)
            m = solid[q, p]
            for f in range(F):
                new = (1.0 - OMEGA) * xs[f] + inverse[f, q, p] * drives[f]
                x[f, q, p] = new
                if not last:
                    put_masked(target, level, f, q, p, m * new)

    each_row(R, body)
    if not last:
        fix_ends(target, level)


def first(level, x, masked, rhs, solid, inverse):
    def body(q):
        for p in range(COLS[level]):
            m = solid[q, p]
            for f in range(F):
                new = inverse[f, q, p] * rhs[f, q, p]
                x[f, q, p] = new
                put_masked(masked, level, f, q, p, m * new)

    each_row(ROWS[level], body)
    fix_ends(masked, level)


def mask(level, x, masked, solid):
    def body(q):
        for p in range(COLS[level]):
            m = solid[q, p]
            for f in range(F):
                put_masked(masked, level, f, q, p, m * x[f, q, p])

    each_row(ROWS[level], body)
    fix_ends(masked, level)


def restrict(level, K, x, masked, rhs, solid, react, coarse):
    R, C = ROWS[level], COLS[level]
    wide = 2 if C > 1 else 1

    def body(half):
        for P_ in range(C // wide):
            sums = [None] * F
            for dq in range(2):
                for dp in range(wide):
                    q, p = 2 * half + dq, wide * P_ + dp
                    drives, xs = drive(level, K, x, masked, rhs, solid, q, p)
                    s = react[q, p]
                    for f in range(F):
                        e = drives[f] - (s + (4.0 * SCALE[level] + K[f, f])) * xs[f]
                        sums[f] = e if sums[f] is None else sums[f] + e
            for f in range(F):
                coarse[f, half, P_] = sums[f] * (0.5 / wide)

    each_row(R // 2, body)


def prolong(level, x, masked, solid, source):
    def body(half):
        for dq in range(2):
            q = 2 * half + dq
            for p in range(COLS[level]):
                m = solid[q, p]
                for f in range(F):
                    new = x[f, q, p] + source[f, half, p // 2]
                    x[f, q, p] = new
                    put_masked(masked, level, f, q, p, m * new)

    each_row(ROWS[level] // 2, body)
    fix_ends(masked, level)


def invert(level, K, react, inverse):
    def body(q):
        for p in range(COLS[level]):
            s = react[q, p]
            for f in range(F):
                inverse[f, q, p] = OMEGA / (s + (4.0 * SCALE[level] + K[f, f]))

    each_row(ROWS[level], body)


def decimate():
    k = lax.broadcasted_iota(jnp.int32, (128, 128), 0)
    o = lax.broadcasted_iota(jnp.int32, (128, 128), 1)
    return jnp.where(o == (k // 2 + 10) % 64, 0.5, 0.0).astype(BF16)


def spread(half):
    o = lax.broadcasted_iota(jnp.int32, (128, 128), 0)
    k = lax.broadcasted_iota(jnp.int32, (128, 128), 1)
    return jnp.where(o == (k // 2 + 10) % 64 + 64 * half, 1.0, 0.0).astype(BF16)


def half_pair(a, b):
    return jnp.where(lanes((8, 128)) < 64, a, roll(b, 64, 1))


def descend(K, X, M, RHS, SOLID, REACT, INV):
    for level in range(3):
        a, b = M[level]
        if level:
            first(level, X[level], a, RHS[level], SOLID[level], INV[level])
            sweep(level, K, X[level], a, b, RHS[level], SOLID[level], INV[level])
        if level < 2:
            restrict(
                level, K, X[level], b, RHS[level], SOLID[level], REACT[level], RHS[level + 1]
            )


def coarse_rhs(K, X, M, RHS, SOLID, REACT, three_rhs):
    restrict(2, K, X[2], M[2][1], RHS[2], SOLID[2], REACT[2], three_rhs)
    return [three_rhs[f, 0, 0, 0:8] for f in range(F)]


def down_one(
    K, own, up, dn, right, left,
    x0, r0, s0, m0, i0, x1, r1, s1, m1, i1, x2, r2, s2, m2, i2, payload,
    ma0, mb0, ma1, mb1, ma2, mb2, three_rhs,
):
    for a in range(6):
        for q in range(8):
            for h in range(2):
                pair = widen(own, up, dn, right, left, a * 16 + q * 2 + h)
                for e in range(2):
                    if a < 4:
                        r0[a, q, 2 * h + e] = pair[e]
                    elif a == 4:
                        s0[q, 2 * h + e] = pair[e]
                    else:
                        m0[q, 2 * h + e] = pair[e]
    for q in range(4):
        pair = widen(own, up, dn, right, left, 96 + q)
        m1[q, 0], m1[q, 1] = pair
    pair = widen(own, up, dn, right, left, 100)
    m2[0, 0], m2[1, 0] = pair
    m3 = widen(own, up, dn, right, left, 101)[0]
    for q in range(4):
        for p in range(2):
            s1[q, p] = 0.25 * (
                (s0[2 * q, 2 * p] + s0[2 * q, 2 * p + 1])
                + (s0[2 * q + 1, 2 * p] + s0[2 * q + 1, 2 * p + 1])
            )
    for q in range(2):
        s2[q, 0] = 0.25 * (
            (s1[2 * q, 0] + s1[2 * q, 1]) + (s1[2 * q + 1, 0] + s1[2 * q + 1, 1])
        )
    X, RHS, SOLID, REACT, INV = (x0, x1, x2), (r0, r1, r2), (m0, m1, m2), (s0, s1, s2), (i0, i1, i2)
    M = ((ma0, mb0), (ma1, mb1), (ma2, mb2))
    for level in range(3):
        invert(level, K, REACT[level], INV[level])
    first(0, x0, ma0, r0, m0, i0)
    sweep(0, K, x0, ma0, mb0, r0, m0, i0)
    descend(K, X, M, RHS, SOLID, REACT, INV)
    rest = coarse_rhs(K, X, M, RHS, SOLID, REACT, three_rhs)
    s3 = 0.5 * (s2[0, 0, 0:8] + s2[1, 0, 0:8])
    y = exact_dot(jnp.concatenate(rest + [m3[0:8], s3], axis=0), decimate())
    y = [y[8 * n : 8 * n + 8] for n in range(6)]
    tiles = [half_pair(y[0], y[1]), half_pair(y[2], y[3]), half_pair(y[4], y[5])]
    for d in range(payload.shape[0]):
        for n in range(3):
            payload[d, n] = tiles[n]


def down_two(
    K, own, up, dn, right, left, r0, s0, m0, i0, s1, m1, i1, s2, m2, i2,
    x0, x1, r1, x2, r2, payload,
    ma0, mb0, ma1, mb1, ma2, mb2, three_rhs,
):
    for a in range(F):
        for q in range(8):
            for h in range(2):
                pair = widen(own, up, dn, right, left, a * 16 + q * 2 + h)
                for e in range(2):
                    x0[a, q, 2 * h + e] = pair[e]
    X, RHS, SOLID, REACT, INV = (x0, x1, x2), (r0, r1, r2), (m0, m1, m2), (s0, s1, s2), (i0, i1, i2)
    M = ((ma0, mb0), (ma1, mb1), (ma2, mb2))
    mask(0, x0, mb0, m0)
    sweep(0, K, x0, mb0, ma0, r0, m0, i0)
    sweep(0, K, x0, ma0, mb0, r0, m0, i0)
    descend(K, X, M, RHS, SOLID, REACT, INV)
    rest = coarse_rhs(K, X, M, RHS, SOLID, REACT, three_rhs)
    y = exact_dot(jnp.concatenate(rest + rest[0:2], axis=0), decimate())
    y = [y[8 * n : 8 * n + 8] for n in range(4)]
    tiles = [half_pair(y[0], y[1]), half_pair(y[2], y[3])]
    for d in range(payload.shape[0]):
        for n in range(2):
            payload[d, n] = tiles[n]


def solve_coarsest(K, gathered, statics, natural, x, ma, mb, rhs, solid, react, inverse, wide, correct):
    low = lanes((8, 128)) < 64
    top = sublanes((8, 128)) == 0
    bottom = sublanes((8, 128)) == 7
    c = SCALE[3]
    blocks = gathered.shape[0]
    for d in range(blocks):
        natural[0, pl.ds(8 * d, 8), :] = gathered[d, 0]
        natural[1, pl.ds(8 * d, 8), :] = gathered[d, 1]
        natural[2, pl.ds(8 * d, 8), :] = statics[d, 2]
    diagonal = [jnp.where(low, 4.0 * c + K[2 * n, 2 * n], 4.0 * c + K[2 * n + 1, 2 * n + 1]) for n in range(2)]
    weights = [
        (jnp.where(low, K[0, 1], K[1, 0]), jnp.where(low, K[0, 2], K[1, 3]), jnp.where(low, K[0, 3], K[1, 2])),
        (jnp.where(low, K[2, 3], K[3, 2]), jnp.where(low, K[2, 0], K[3, 1]), jnp.where(low, K[2, 1], K[3, 0])),
    ]
    for t in range(blocks):
        pick = pl.ds(t, 8, stride=blocks)
        both = natural[2, pick, :]
        turned = roll(both, 64, 1)
        m = jnp.where(low, both, turned)
        s = jnp.where(low, turned, both)
        solid[t] = m
        react[t] = s
        for n in range(2):
            r = natural[n, pick, :]
            i = OMEGA / (s + diagonal[n])
            rhs[n, t] = r
            inverse[n, t] = i
            x[n, t] = i * r
            ma[n, t + 1] = m * (i * r)

    def ends(masked):
        for n in range(2):
            masked[n, 0] = jnp.where(top, 0.0, roll(masked[n, blocks], 1, 0))
            masked[n, blocks + 1] = jnp.where(bottom, 0.0, roll(masked[n, 1], -1, 0))

    def drives(t, masked):
        weight = c * solid[t]
        xs = [x[0, t], x[1, t]]
        turned = [roll(v, 64, 1) for v in xs]
        out = []
        for n in range(2):
            here = masked[n, t + 1]
            near = (masked[n, t] + masked[n, t + 2]) + (roll(here, 1, 1) + roll(here, -1, 1))
            u, v, w = weights[n]
            mixed = u * turned[n] + v * xs[1 - n] + w * turned[1 - n]
            out.append(rhs[n, t] + weight * near - mixed)
        return out, xs

    ends(ma)
    for index in range(5):
        source, target = (ma, mb) if index % 2 == 0 else (mb, ma)

        def body(t, _):
            out, xs = drives(t, source)
            m = solid[t]
            for n in range(2):
                new = (1.0 - OMEGA) * xs[n] + inverse[n, t] * out[n]
                x[n, t] = new
                target[n, t + 1] = m * new
            return _

        lax.fori_loop(0, blocks, body, 0, unroll=4)
        ends(target)

    def gather_sums(t, sums):
        out, xs = drives(t, mb)
        s = react[t]
        sums = list(sums)
        for n in range(2):
            g = s + diagonal[n]
            sums[n] = sums[n] + (out[n] - g * xs[n])
            sums[2 + n] = sums[2 + n] + g
        return tuple(sums)

    zero = jnp.zeros((8, 128), F32)
    sums = lax.fori_loop(0, blocks, gather_sums, (zero,) * 4, unroll=4)
    sums = [jnp.sum(v, axis=0, keepdims=True) for v in sums]
    for n in range(2):
        wide[n, pl.ds(0, 8), :] = zero
        wide[n, pl.ds(8 * blocks + 8, 8), :] = zero
        mean = sums[n] / sums[2 + n]
        for t in range(blocks):
            wide[n, pl.ds(8 + t, 8, stride=blocks), :] = x[n, t] + mean
    start = pl.multiple_of(lax.axis_index("gx") * 8, 8)
    rows = []
    for n in range(2):
        rows.append(wide[n, pl.ds(start + 8, 8), :])
        rows.append(
            jnp.where(
                sublanes((8, 128)) < 4,
                wide[n, pl.ds(start + 16, 8), :],
                wide[n, pl.ds(start, 8), :],
            )
        )
    rows = jnp.concatenate(rows, axis=0)
    for half in range(2):
        y = exact_dot(rows, spread(half))
        correct[half, 0, 0] = y[0:16]
        correct[2 + half, 0, 0] = y[16:32]


def ascend(K, X, M, RHS, SOLID, INV, correct, last):
    source = correct
    for level in (2, 1, 0):
        a, b = M[level]
        prolong(level, X[level], a, SOLID[level], source)
        sweep(level, K, X[level], a, b, RHS[level], SOLID[level], INV[level])
        sweep(
            level, K, X[level], b, a, RHS[level], SOLID[level], INV[level],
            last=level > 0 or not last,
        )
        source = X[level]


def copy_state(sources, targets):
    for source, target in zip(sources, targets):
        target[...] = source[...]


def up_one(
    K, gathered, x0i, r0, m0, i0, x1i, r1, m1, i1, x2i, r2, m2, i2,
    own, up, dn,
    x0, x1, x2, ma0, mb0, ma1, mb1, ma2, mb2,
    natural, x3, ma3, mb3, r3, m3, s3, i3, wide, correct,
):
    copy_state((x0i, x1i, x2i), (x0, x1, x2))
    solve_coarsest(K, gathered, gathered, natural, x3, ma3, mb3, r3, m3, s3, i3, wide, correct)
    M = ((ma0, mb0), (ma1, mb1), (ma2, mb2))
    ascend(K, (x0, x1, x2), M, (r0, r1, r2), (m0, m1, m2), (i0, i1, i2), correct, False)
    for f in range(F):
        for q in range(8):
            for h in range(2):
                own[f * 16 + q * 2 + h] = half_pair(
                    x0[f, q, 2 * h, 0:8], x0[f, q, 2 * h + 1, 0:8]
                )
    pack_rows(own, up, dn, XTILES)


def up_two(
    K, gathered, statics, x0i, r0, s0, m0, i0, x1i, r1, m1, i1, x2i, r2, m2, i2,
    displacement, residual,
    x0, x1, x2, ma0, mb0, ma1, mb1, ma2, mb2,
    natural, x3, ma3, mb3, r3, m3, s3, i3, wide, correct, stage,
):
    copy_state((x0i, x1i, x2i), (x0, x1, x2))
    solve_coarsest(K, gathered, statics, natural, x3, ma3, mb3, r3, m3, s3, i3, wide, correct)
    M = ((ma0, mb0), (ma1, mb1), (ma2, mb2))
    ascend(K, (x0, x1, x2), M, (r0, r1, r2), (m0, m1, m2), (i0, i1, i2), correct, True)
    mine = slice(0, 8)
    for q in range(8):
        for h in range(2):
            outs = []
            for p in (2 * h, 2 * h + 1):
                drives, xs = drive(0, K, x0, ma0, r0, m0, q, p, mine)
                s = s0[q, p, mine]
                rest = [drives[f] - (s + (4.0 + K[f, f])) * xs[f] for f in range(F)]
                outs.append(xs + rest)
            for a in range(2 * F):
                stage[a, h, pl.ds(q, 8, stride=8), :] = half_pair(outs[0][a], outs[1][a])
    matrix = join_matrix(256, 4)
    for f in range(F):
        for out, a in ((displacement, f), (residual, F + f)):
            out[f] = exact_dot(jnp.concatenate([stage[a, 0], stage[a, 1]], axis=1), matrix)


def sds(*shape):
    return jax.ShapeDtypeStruct(shape, F32)


def field(level):
    return (F, ROWS[level], COLS[level], 16, 128)


def plane(level):
    return (ROWS[level], COLS[level], 16, 128)


def masked_scratch():
    out = []
    for level in range(3):
        shape = (F, ROWS[level] + 2, COLS[level] + 2, 16, 128)
        out += [pltpu.VMEM(shape, F32), pltpu.VMEM(shape, F32)]
    return out


def coarsest_scratch(blocks):
    return [
        pltpu.VMEM((3, 8 * blocks, 128), F32),
        pltpu.VMEM((2, blocks, 8, 128), F32),
        pltpu.VMEM((2, blocks + 2, 8, 128), F32),
        pltpu.VMEM((2, blocks + 2, 8, 128), F32),
        pltpu.VMEM((2, blocks, 8, 128), F32),
        pltpu.VMEM((blocks, 8, 128), F32),
        pltpu.VMEM((blocks, 8, 128), F32),
        pltpu.VMEM((2, blocks, 8, 128), F32),
        pltpu.VMEM((2, 8 * blocks + 16, 128), F32),
        pltpu.VMEM((F, 1, 1, 16, 128), F32),
    ]


def call(body, outs, scratch, args, smem=True):
    specs = [pl.BlockSpec(memory_space=pltpu.VMEM)] * len(args)
    if smem:
        specs[0] = pl.BlockSpec(memory_space=pltpu.SMEM)
    return pl.pallas_call(
        body,
        out_shape=outs,
        in_specs=specs,
        out_specs=[pl.BlockSpec(memory_space=pltpu.VMEM)] * len(outs),
        scratch_shapes=scratch,
        compiler_params=pltpu.CompilerParams(vmem_limit_bytes=30 * 1024 * 1024),
    )(*args)


def along(axis, down_message, up_message):
    count = lax.axis_size(axis)
    forward = [(i, i + 1) for i in range(count - 1)]
    backward = [(target, source) for source, target in forward]
    return lax.ppermute(down_message, axis, forward), lax.ppermute(up_message, axis, backward)


def exchange(own, up, dn):
    count = own.shape[0]
    dn, up = along("gx", dn, up)
    groups = -(-count // 3)
    right, left = call(
        functools.partial(side_kernel, count),
        [sds(groups, 2, 8, 128)] * 2,
        [],
        (own, up, dn),
        smem=False,
    )
    right, left = along("gy", right, left)
    return own, up, dn, right, left


def shards(source, reaction, coupling, solid0, solid1, solid2, solid3):
    blocks = lax.axis_size("gx")
    packed = call(
        pack_kernel,
        [sds(TILES, 8, 128), sds(TILES // 2, 8, 128), sds(TILES // 2, 8, 128)],
        [pltpu.VMEM((6, 2, 64, 128), F32), pltpu.VMEM((32, 128), F32)],
        (source, reaction, solid0, solid1, solid2, solid3),
        smem=False,
    )
    halo = exchange(*packed)
    shapes = []
    for level in range(3):
        shapes += [sds(*field(level))] * 2 + [sds(*plane(level))] * 2 + [sds(*field(level))]
    state = call(
        down_one,
        shapes + [sds(blocks, 3, 8, 128)],
        masked_scratch() + [pltpu.VMEM((F, 1, 1, 16, 128), F32)],
        (coupling,) + halo,
    )
    x0, r0, s0, m0, i0, x1, r1, s1, m1, i1, x2, r2, s2, m2, i2, payload = state
    statics = lax.all_to_all(payload, "gx", 0, 0)
    inner = [pltpu.VMEM(field(level), F32) for level in range(3)]
    packed = call(
        up_one,
        [sds(XTILES, 8, 128), sds(XTILES // 2, 8, 128), sds(XTILES // 2, 8, 128)],
        inner + masked_scratch() + coarsest_scratch(blocks),
        (coupling, statics, x0, r0, m0, i0, x1, r1, m1, i1, x2, r2, m2, i2),
    )
    halo = exchange(*packed)
    x0, x1, r1, x2, r2, payload = call(
        down_two,
        [sds(*field(0)), sds(*field(1)), sds(*field(1)), sds(*field(2)), sds(*field(2)),
         sds(blocks, 2, 8, 128)],
        masked_scratch() + [pltpu.VMEM((F, 1, 1, 16, 128), F32)],
        (coupling,) + halo + (r0, s0, m0, i0, s1, m1, i1, s2, m2, i2),
    )
    gathered = lax.all_to_all(payload, "gx", 0, 0)
    displacement, residual = call(
        up_two,
        [sds(F, 64, 256), sds(F, 64, 256)],
        inner + masked_scratch() + coarsest_scratch(blocks)
        + [pltpu.VMEM((2 * F, 2, 64, 128), F32)],
        (coupling, gathered, statics, x0, r0, s0, m0, i0, x1, r1, m1, i1, x2, r2, m2, i2),
    )
    return displacement, residual


def solution(mesh):
    placed = (
        P(None, "gx", "gy"),
        P("gx", "gy"),
        P(),
        P("gx", "gy"),
        P("gx", "gy"),
        P("gx", "gy"),
        P("gx", "gy"),
    )
    return jax.shard_map(
        shards,
        mesh=mesh,
        in_specs=placed,
        out_specs=(P(None, "gx", "gy"), P(None, "gx", "gy")),
        check_vma=False,
    )
```

```python
import functools

import jax
import jax.numpy as jnp
from jax import lax
from jax.experimental import pallas as pl
from jax.experimental.pallas import tpu as pltpu
from jax.sharding import PartitionSpec as P


F = 4
ROWS = (8, 4, 2)
COLS = (4, 2, 1)
SCALE = (1.0, 0.25, 0.0625, 0.015625)
OMEGA = 0.6
TILES = 102
XTILES = 64
F32 = jnp.float32
BF16 = jnp.bfloat16


def lanes(shape):
    return lax.broadcasted_iota(jnp.int32, shape, len(shape) - 1)


def sublanes(shape):
    return lax.broadcasted_iota(jnp.int32, shape, len(shape) - 2)


def roll(value, shift, axis):
    size = value.shape[axis]
    shift = shift % size
    return value if shift == 0 else pltpu.roll(value, shift, axis)


def three(value):
    high = value.astype(BF16)
    rest = value - high.astype(F32)
    mid = rest.astype(BF16)
    low = (rest - mid.astype(F32)).astype(BF16)
    return high, mid, low


def exact_dot(value, matrix):
    parts = [jnp.dot(part, matrix, preferred_element_type=F32) for part in three(value)]
    return parts[0] + (parts[1] + parts[2])


def split_matrix(size, stride):
    c = lax.broadcasted_iota(jnp.int32, (size, size), 0)
    o = lax.broadcasted_iota(jnp.int32, (size, size), 1)
    return jnp.where(o == (c % stride) * (size // stride) + c // stride, 1.0, 0.0).astype(BF16)


def join_matrix(size, stride):
    o = lax.broadcasted_iota(jnp.int32, (size, size), 0)
    c = lax.broadcasted_iota(jnp.int32, (size, size), 1)
    return jnp.where(o == (c % stride) * (size // stride) + c // stride, 1.0, 0.0).astype(BF16)


def pack_rows(own, up, dn, count):
    low = sublanes((8, 128)) < 4

    def body(n, _):
        a = own[2 * n]
        b = own[2 * n + 1]
        up[n] = jnp.where(low, a, roll(b, 4, 0))
        dn[n] = jnp.where(low, roll(a, 4, 0), b)
        return _

    lax.fori_loop(0, count // 2, body, 0, unroll=3 if count % 6 == 0 else 4)


def outer_rows(up, dn, n, odd):
    low = sublanes((8, 128)) < 4
    if odd:
        return jnp.where(low, roll(up[n], 4, 0), dn[n])
    return jnp.where(low, up[n], roll(dn[n], 4, 0))


def pack_kernel(
    source_in, reaction_in, solid0_in, solid1_in, solid2_in, solid3_in, own, up, dn,
    source, reaction, solid0, solid1, solid2, solid3, stage, small, arrived,
):
    moves = [
        pltpu.make_async_copy(there, here, arrived.at[n])
        for n, (there, here) in enumerate(
            (
                (source_in, source),
                (reaction_in, reaction),
                (solid0_in, solid0),
                (solid1_in, solid1),
                (solid2_in, solid2),
                (solid3_in, solid3),
            )
        )
    ]
    for move in moves:
        move.start()
    matrix = split_matrix(256, 4)
    for move in moves:
        move.wait()
    for a in range(6):
        if a < 4:
            value = exact_dot(source[a], matrix)
        elif a == 4:
            value = exact_dot(reaction[...], matrix)
        else:
            value = jnp.dot(
                solid0[...].astype(F32).astype(BF16), matrix, preferred_element_type=F32
            )
        for h in range(2):
            stage[a, h] = value[:, 128 * h : 128 * h + 128]
    for a in range(6):
        for q in range(8):
            for h in range(2):
                own[a * 16 + q * 2 + h] = stage[a, h, pl.ds(q, 8, stride=8), :]
    small[...] = jnp.dot(
        solid1[...].astype(F32).astype(BF16),
        split_matrix(128, 2),
        preferred_element_type=F32,
    )
    for q in range(4):
        own[96 + q] = small[pl.ds(q, 8, stride=4), :]
    c = lax.broadcasted_iota(jnp.int32, (64, 128), 0)
    o = lax.broadcasted_iota(jnp.int32, (64, 128), 1)
    wide = jnp.where(o % 64 == c, 1.0, 0.0).astype(BF16)
    small[pl.ds(0, 16), :] = jnp.dot(
        solid2[...].astype(F32).astype(BF16), wide, preferred_element_type=F32
    )
    own[100] = jnp.where(
        lanes((8, 128)) < 64,
        small[pl.ds(0, 8, stride=2), :],
        small[pl.ds(1, 8, stride=2), :],
    )
    c = lax.broadcasted_iota(jnp.int32, (32, 128), 0)
    o = lax.broadcasted_iota(jnp.int32, (32, 128), 1)
    twice = jnp.where((o % 64) // 2 == c, 1.0, 0.0)
    own[101] = jnp.dot(
        solid3[...].astype(F32), twice, preferred_element_type=F32,
        precision=lax.Precision.HIGHEST,
    )
    pack_rows(own, up, dn, TILES)


def side_kernel(count, own, up, dn, right, left):
    lane = lanes((8, 128)) % 64

    def group(g, members):
        for v in range(2):
            tiles = []
            for t in range(members):
                index = 3 * g + t
                if v == 0:
                    tiles.append(own[index])
                else:
                    n = index // 2
                    low = sublanes((8, 128)) < 4
                    turn = lax.broadcast(index % 2, (8, 128)) == 1
                    a, b = up[n], dn[n]
                    even = jnp.where(low, a, roll(b, 4, 0))
                    odd = jnp.where(low, roll(a, 4, 0), b)
                    tiles.append(jnp.where(turn, odd, even))
            r, l = tiles[0], tiles[0]
            for t in range(1, members):
                r = jnp.where(lane < 64 - 20 * t, roll(tiles[t], -20 * t, 1), r)
                l = jnp.where(lane >= 20 * t, roll(tiles[t], 20 * t, 1), l)
            right[g, v] = r
            left[g, v] = l

    def body(g, _):
        group(g, 3)
        return _

    lax.fori_loop(0, count // 3, body, 0, unroll=2)
    if count % 3:
        group(jnp.int32(count // 3), count % 3)


def widen(own, up, dn, right, left, index):
    lane = lanes((8, 128))
    g, t = index // 3, index % 3
    out = [[], []]
    for v in range(2):
        mine = own[index] if v == 0 else outer_rows(up, dn, index // 2, index % 2)
        r, l = right[g, v], left[g, v]
        for h in range(2):
            centre = roll(mine, 64 * h, 1)
            before = roll(r, 64 + 20 * t + 64 * h, 1)
            after = roll(l, 64 - 20 * t + 64 * h, 1)
            tile = jnp.where(lane < 64, centre, jnp.where(lane < 84, after, 0.0))
            out[h].append(jnp.where(lane >= 108, before, tile))
    return [jnp.concatenate(pair, axis=0) for pair in out]


def fix_ends(masked, level):
    R, C = ROWS[level], COLS[level]
    for f in range(F):
        for p in range(C):
            masked[f, 0, p + 1] = roll(masked[f, R, p + 1], 1, 0)
            masked[f, R + 1, p + 1] = roll(masked[f, 1, p + 1], -1, 0)
        for q in range(R):
            masked[f, q + 1, 0] = roll(masked[f, q + 1, C], 1, 1)
            masked[f, q + 1, C + 1] = roll(masked[f, q + 1, 1], -1, 1)


def put_masked(masked, level, f, q, p, value):
    masked[f, q + 1, p + 1] = value


def each_row(count, body):
    if count > 4:
        def step(q, _):
            body(q)
            return _

        lax.fori_loop(0, count, step, 0, unroll=count)
    else:
        for q in range(count):
            body(q)


def drive(level, K, x, masked, rhs, solid, q, p, rows=slice(None)):
    xs = [x[f, q, p, rows] for f in range(F)]
    weight = solid[q, p, rows]
    if level:
        weight = weight * SCALE[level]
    out = []
    for f in range(F):
        near = (masked[f, q, p + 1, rows] + masked[f, q + 2, p + 1, rows]) + (
            masked[f, q + 1, p, rows] + masked[f, q + 1, p + 2, rows]
        )
        total = rhs[f, q, p, rows] + weight * near
        mixed = None
        for b in range(F):
            if b != f:
                term = K[f, b] * xs[b]
                mixed = term if mixed is None else mixed + term
        out.append(total - mixed)
    return out, xs


def sweep(level, K, x, masked, target, rhs, solid, inverse, last=False):
    R, C = ROWS[level], COLS[level]

    def body(q):
        news = []
        for p in range(C):
            drives, xs = drive(level, K, x, masked, rhs, solid, q, p)
            news.append(
                [(1.0 - OMEGA) * xs[f] + inverse[f, q, p] * drives[f] for f in range(F)]
            )
        for p in range(C):
            m = None if last else solid[q, p]
            for f in range(F):
                x[f, q, p] = news[p][f]
                if not last:
                    put_masked(target, level, f, q, p, m * news[p][f])

    each_row(R, body)
    if not last:
        fix_ends(target, level)


def first(level, x, masked, rhs, solid, inverse):
    def body(q):
        for p in range(COLS[level]):
            m = solid[q, p]
            for f in range(F):
                new = inverse[f, q, p] * rhs[f, q, p]
                x[f, q, p] = new
                put_masked(masked, level, f, q, p, m * new)

    each_row(ROWS[level], body)
    fix_ends(masked, level)


def mask(level, x, masked, solid):
    def body(q):
        for p in range(COLS[level]):
            m = solid[q, p]
            for f in range(F):
                put_masked(masked, level, f, q, p, m * x[f, q, p])

    each_row(ROWS[level], body)
    fix_ends(masked, level)


def restrict(level, K, x, masked, rhs, solid, react, coarse):
    R, C = ROWS[level], COLS[level]
    wide = 2 if C > 1 else 1

    def body(half):
        for P_ in range(C // wide):
            sums = [None] * F
            for dq in range(2):
                for dp in range(wide):
                    q, p = 2 * half + dq, wide * P_ + dp
                    drives, xs = drive(level, K, x, masked, rhs, solid, q, p)
                    s = react[q, p]
                    for f in range(F):
                        e = drives[f] - (s + (4.0 * SCALE[level] + K[f, f])) * xs[f]
                        sums[f] = e if sums[f] is None else sums[f] + e
            for f in range(F):
                coarse[f, half, P_] = sums[f] * (0.5 / wide)

    each_row(R // 2, body)


def prolong(level, x, masked, solid, source):
    def body(half):
        for dq in range(2):
            q = 2 * half + dq
            for p in range(COLS[level]):
                m = solid[q, p]
                for f in range(F):
                    new = x[f, q, p] + source[f, half, p // 2]
                    x[f, q, p] = new
                    put_masked(masked, level, f, q, p, m * new)

    each_row(ROWS[level] // 2, body)
    fix_ends(masked, level)


def invert(level, K, react, inverse):
    def body(q):
        for p in range(COLS[level]):
            s = react[q, p]
            for f in range(F):
                inverse[f, q, p] = OMEGA / (s + (4.0 * SCALE[level] + K[f, f]))

    each_row(ROWS[level], body)


def decimate():
    k = lax.broadcasted_iota(jnp.int32, (128, 128), 0)
    o = lax.broadcasted_iota(jnp.int32, (128, 128), 1)
    return jnp.where(o == (k // 2 + 10) % 64, 0.5, 0.0).astype(BF16)


def spread(half):
    o = lax.broadcasted_iota(jnp.int32, (128, 128), 0)
    k = lax.broadcasted_iota(jnp.int32, (128, 128), 1)
    return jnp.where(o == (k // 2 + 10) % 64 + 64 * half, 1.0, 0.0).astype(BF16)


def half_pair(a, b):
    return jnp.where(lanes((8, 128)) < 64, a, roll(b, 64, 1))


def descend(K, X, M, RHS, SOLID, REACT, INV):
    for level in range(3):
        a, b = M[level]
        if level:
            first(level, X[level], a, RHS[level], SOLID[level], INV[level])
            sweep(level, K, X[level], a, b, RHS[level], SOLID[level], INV[level])
        if level < 2:
            restrict(
                level, K, X[level], b, RHS[level], SOLID[level], REACT[level], RHS[level + 1]
            )


def coarse_rhs(K, X, M, RHS, SOLID, REACT, three_rhs):
    restrict(2, K, X[2], M[2][1], RHS[2], SOLID[2], REACT[2], three_rhs)
    return [three_rhs[f, 0, 0, 0:8] for f in range(F)]


def down_one(
    K, own, up, dn, right, left,
    x0, r0, s0, m0, i0, x1, r1, s1, m1, i1, x2, r2, s2, m2, i2, payload,
    ma0, mb0, ma1, mb1, ma2, mb2, three_rhs,
):
    for a in range(6):
        for q in range(8):
            for h in range(2):
                pair = widen(own, up, dn, right, left, a * 16 + q * 2 + h)
                for e in range(2):
                    if a < 4:
                        r0[a, q, 2 * h + e] = pair[e]
                    elif a == 4:
                        s0[q, 2 * h + e] = pair[e]
                    else:
                        m0[q, 2 * h + e] = pair[e]
    for q in range(4):
        pair = widen(own, up, dn, right, left, 96 + q)
        m1[q, 0], m1[q, 1] = pair
    pair = widen(own, up, dn, right, left, 100)
    m2[0, 0], m2[1, 0] = pair
    m3 = widen(own, up, dn, right, left, 101)[0]
    for q in range(4):
        for p in range(2):
            s1[q, p] = 0.25 * (
                (s0[2 * q, 2 * p] + s0[2 * q, 2 * p + 1])
                + (s0[2 * q + 1, 2 * p] + s0[2 * q + 1, 2 * p + 1])
            )
    for q in range(2):
        s2[q, 0] = 0.25 * (
            (s1[2 * q, 0] + s1[2 * q, 1]) + (s1[2 * q + 1, 0] + s1[2 * q + 1, 1])
        )
    X, RHS, SOLID, REACT, INV = (x0, x1, x2), (r0, r1, r2), (m0, m1, m2), (s0, s1, s2), (i0, i1, i2)
    M = ((ma0, mb0), (ma1, mb1), (ma2, mb2))
    for level in range(3):
        invert(level, K, REACT[level], INV[level])
    first(0, x0, ma0, r0, m0, i0)
    sweep(0, K, x0, ma0, mb0, r0, m0, i0)
    descend(K, X, M, RHS, SOLID, REACT, INV)
    rest = coarse_rhs(K, X, M, RHS, SOLID, REACT, three_rhs)
    s3 = 0.5 * (s2[0, 0, 0:8] + s2[1, 0, 0:8])
    y = exact_dot(jnp.concatenate(rest + [m3[0:8], s3], axis=0), decimate())
    y = [y[8 * n : 8 * n + 8] for n in range(6)]
    tiles = [half_pair(y[0], y[1]), half_pair(y[2], y[3]), half_pair(y[4], y[5])]
    for d in range(payload.shape[0]):
        for n in range(3):
            payload[d, n] = tiles[n]


def down_two(
    K, own, up, dn, right, left, r0, s0, m0, i0, s1, m1, i1, s2, m2, i2,
    x0, x1, r1, x2, r2, payload,
    ma0, mb0, ma1, mb1, ma2, mb2, three_rhs,
):
    for a in range(F):
        for q in range(8):
            for h in range(2):
                pair = widen(own, up, dn, right, left, a * 16 + q * 2 + h)
                for e in range(2):
                    x0[a, q, 2 * h + e] = pair[e]
    X, RHS, SOLID, REACT, INV = (x0, x1, x2), (r0, r1, r2), (m0, m1, m2), (s0, s1, s2), (i0, i1, i2)
    M = ((ma0, mb0), (ma1, mb1), (ma2, mb2))
    mask(0, x0, mb0, m0)
    sweep(0, K, x0, mb0, ma0, r0, m0, i0)
    sweep(0, K, x0, ma0, mb0, r0, m0, i0)
    descend(K, X, M, RHS, SOLID, REACT, INV)
    rest = coarse_rhs(K, X, M, RHS, SOLID, REACT, three_rhs)
    y = exact_dot(jnp.concatenate(rest + rest[0:2], axis=0), decimate())
    y = [y[8 * n : 8 * n + 8] for n in range(4)]
    tiles = [half_pair(y[0], y[1]), half_pair(y[2], y[3])]
    for d in range(payload.shape[0]):
        for n in range(2):
            payload[d, n] = tiles[n]


def solve_coarsest(K, gathered, statics, natural, x, ma, mb, rhs, solid, react, inverse, wide, correct):
    low = lanes((8, 128)) < 64
    top = sublanes((8, 128)) == 0
    bottom = sublanes((8, 128)) == 7
    c = SCALE[3]
    blocks = gathered.shape[0]
    for d in range(blocks):
        natural[0, pl.ds(8 * d, 8), :] = gathered[d, 0]
        natural[1, pl.ds(8 * d, 8), :] = gathered[d, 1]
        natural[2, pl.ds(8 * d, 8), :] = statics[d, 2]
    diagonal = [jnp.where(low, 4.0 * c + K[2 * n, 2 * n], 4.0 * c + K[2 * n + 1, 2 * n + 1]) for n in range(2)]
    weights = [
        (jnp.where(low, K[0, 1], K[1, 0]), jnp.where(low, K[0, 2], K[1, 3]), jnp.where(low, K[0, 3], K[1, 2])),
        (jnp.where(low, K[2, 3], K[3, 2]), jnp.where(low, K[2, 0], K[3, 1]), jnp.where(low, K[2, 1], K[3, 0])),
    ]
    for t in range(blocks):
        pick = pl.ds(t, 8, stride=blocks)
        both = natural[2, pick, :]
        turned = roll(both, 64, 1)
        m = jnp.where(low, both, turned)
        s = jnp.where(low, turned, both)
        solid[t] = m
        react[t] = s
        for n in range(2):
            r = natural[n, pick, :]
            i = OMEGA / (s + diagonal[n])
            rhs[n, t] = r
            inverse[n, t] = i
            x[n, t] = i * r
            ma[n, t + 1] = m * (i * r)

    def ends(masked):
        for n in range(2):
            masked[n, 0] = jnp.where(top, 0.0, roll(masked[n, blocks], 1, 0))
            masked[n, blocks + 1] = jnp.where(bottom, 0.0, roll(masked[n, 1], -1, 0))

    def drives(t, masked):
        weight = c * solid[t]
        xs = [x[0, t], x[1, t]]
        turned = [roll(v, 64, 1) for v in xs]
        out = []
        for n in range(2):
            here = masked[n, t + 1]
            near = (masked[n, t] + masked[n, t + 2]) + (roll(here, 1, 1) + roll(here, -1, 1))
            u, v, w = weights[n]
            mixed = u * turned[n] + v * xs[1 - n] + w * turned[1 - n]
            out.append(rhs[n, t] + weight * near - mixed)
        return out, xs

    ends(ma)
    for index in range(5):
        source, target = (ma, mb) if index % 2 == 0 else (mb, ma)

        def body(t, _):
            out, xs = drives(t, source)
            m = solid[t]
            for n in range(2):
                new = (1.0 - OMEGA) * xs[n] + inverse[n, t] * out[n]
                x[n, t] = new
                target[n, t + 1] = m * new
            return _

        lax.fori_loop(0, blocks, body, 0, unroll=blocks)
        ends(target)

    def gather_sums(t, sums):
        out, xs = drives(t, mb)
        s = react[t]
        sums = list(sums)
        for n in range(2):
            g = s + diagonal[n]
            sums[n] = sums[n] + (out[n] - g * xs[n])
            sums[2 + n] = sums[2 + n] + g
        return tuple(sums)

    zero = jnp.zeros((8, 128), F32)
    sums = lax.fori_loop(0, blocks, gather_sums, (zero,) * 4, unroll=blocks)
    sums = [jnp.sum(v, axis=0, keepdims=True) for v in sums]
    for n in range(2):
        wide[n, pl.ds(0, 8), :] = zero
        wide[n, pl.ds(8 * blocks + 8, 8), :] = zero
        mean = sums[n] / sums[2 + n]
        for t in range(blocks):
            wide[n, pl.ds(8 + t, 8, stride=blocks), :] = x[n, t] + mean
    start = pl.multiple_of(lax.axis_index("gx") * 8, 8)
    rows = []
    for n in range(2):
        rows.append(wide[n, pl.ds(start + 8, 8), :])
        rows.append(
            jnp.where(
                sublanes((8, 128)) < 4,
                wide[n, pl.ds(start + 16, 8), :],
                wide[n, pl.ds(start, 8), :],
            )
        )
    rows = jnp.concatenate(rows, axis=0)
    for half in range(2):
        y = exact_dot(rows, spread(half))
        correct[half, 0, 0] = y[0:16]
        correct[2 + half, 0, 0] = y[16:32]


def ascend(K, X, M, RHS, SOLID, INV, correct, last):
    source = correct
    for level in (2, 1, 0):
        a, b = M[level]
        prolong(level, X[level], a, SOLID[level], source)
        sweep(level, K, X[level], a, b, RHS[level], SOLID[level], INV[level])
        sweep(
            level, K, X[level], b, a, RHS[level], SOLID[level], INV[level],
            last=level > 0 or not last,
        )
        source = X[level]


def copy_state(sources, targets):
    for source, target in zip(sources, targets):
        target[...] = source[...]


def up_one(
    K, gathered, x0i, r0, m0, i0, x1i, r1, m1, i1, x2i, r2, m2, i2,
    own, up, dn,
    x0, x1, x2, ma0, mb0, ma1, mb1, ma2, mb2,
    natural, x3, ma3, mb3, r3, m3, s3, i3, wide, correct,
):
    copy_state((x0i, x1i, x2i), (x0, x1, x2))
    solve_coarsest(K, gathered, gathered, natural, x3, ma3, mb3, r3, m3, s3, i3, wide, correct)
    M = ((ma0, mb0), (ma1, mb1), (ma2, mb2))
    ascend(K, (x0, x1, x2), M, (r0, r1, r2), (m0, m1, m2), (i0, i1, i2), correct, False)
    for f in range(F):
        for q in range(8):
            for h in range(2):
                own[f * 16 + q * 2 + h] = half_pair(
                    x0[f, q, 2 * h, 0:8], x0[f, q, 2 * h + 1, 0:8]
                )
    pack_rows(own, up, dn, XTILES)


def up_two(
    K, gathered, statics, x0i, r0, s0, m0, i0, x1i, r1, m1, i1, x2i, r2, m2, i2,
    displacement, residual,
    x0, x1, x2, ma0, mb0, ma1, mb1, ma2, mb2,
    natural, x3, ma3, mb3, r3, m3, s3, i3, wide, correct, stage,
):
    copy_state((x0i, x1i, x2i), (x0, x1, x2))
    solve_coarsest(K, gathered, statics, natural, x3, ma3, mb3, r3, m3, s3, i3, wide, correct)
    M = ((ma0, mb0), (ma1, mb1), (ma2, mb2))
    ascend(K, (x0, x1, x2), M, (r0, r1, r2), (m0, m1, m2), (i0, i1, i2), correct, True)
    mine = slice(0, 8)
    for q in range(8):
        for h in range(2):
            outs = []
            for p in (2 * h, 2 * h + 1):
                drives, xs = drive(0, K, x0, ma0, r0, m0, q, p, mine)
                s = s0[q, p, mine]
                rest = [drives[f] - (s + (4.0 + K[f, f])) * xs[f] for f in range(F)]
                outs.append(xs + rest)
            for a in range(2 * F):
                stage[a, h, pl.ds(q, 8, stride=8), :] = half_pair(outs[0][a], outs[1][a])
    matrix = join_matrix(256, 4)
    for f in range(F):
        for out, a in ((displacement, f), (residual, F + f)):
            out[f] = exact_dot(jnp.concatenate([stage[a, 0], stage[a, 1]], axis=1), matrix)


def sds(*shape):
    return jax.ShapeDtypeStruct(shape, F32)


def field(level):
    return (F, ROWS[level], COLS[level], 16, 128)


def plane(level):
    return (ROWS[level], COLS[level], 16, 128)


def masked_scratch():
    out = []
    for level in range(3):
        shape = (F, ROWS[level] + 2, COLS[level] + 2, 16, 128)
        out += [pltpu.VMEM(shape, F32), pltpu.VMEM(shape, F32)]
    return out


def coarsest_scratch(blocks):
    return [
        pltpu.VMEM((3, 8 * blocks, 128), F32),
        pltpu.VMEM((2, blocks, 8, 128), F32),
        pltpu.VMEM((2, blocks + 2, 8, 128), F32),
        pltpu.VMEM((2, blocks + 2, 8, 128), F32),
        pltpu.VMEM((2, blocks, 8, 128), F32),
        pltpu.VMEM((blocks, 8, 128), F32),
        pltpu.VMEM((blocks, 8, 128), F32),
        pltpu.VMEM((2, blocks, 8, 128), F32),
        pltpu.VMEM((2, 8 * blocks + 16, 128), F32),
        pltpu.VMEM((F, 1, 1, 16, 128), F32),
    ]


def call(body, outs, scratch, args, smem=True, space=pltpu.VMEM):
    specs = [pl.BlockSpec(memory_space=space)] * len(args)
    if smem:
        specs[0] = pl.BlockSpec(memory_space=pltpu.SMEM)
    return pl.pallas_call(
        body,
        out_shape=outs,
        in_specs=specs,
        out_specs=[pl.BlockSpec(memory_space=pltpu.VMEM)] * len(outs),
        scratch_shapes=scratch,
        compiler_params=pltpu.CompilerParams(vmem_limit_bytes=30 * 1024 * 1024),
    )(*args)


def along(axis, down_message, up_message):
    count = lax.axis_size(axis)
    forward = [(i, i + 1) for i in range(count - 1)]
    backward = [(target, source) for source, target in forward]
    return lax.ppermute(down_message, axis, forward), lax.ppermute(up_message, axis, backward)


def exchange(own, up, dn):
    count = own.shape[0]
    dn, up = along("gx", dn, up)
    groups = -(-count // 3)
    right, left = call(
        functools.partial(side_kernel, count),
        [sds(groups, 2, 8, 128)] * 2,
        [],
        (own, up, dn),
        smem=False,
    )
    right, left = along("gy", right, left)
    return own, up, dn, right, left


def shards(source, reaction, coupling, solid0, solid1, solid2, solid3):
    blocks = lax.axis_size("gx")
    arrays = (source, reaction, solid0, solid1, solid2, solid3)
    packed = call(
        pack_kernel,
        [sds(TILES, 8, 128), sds(TILES // 2, 8, 128), sds(TILES // 2, 8, 128)],
        [pltpu.VMEM(array.shape, array.dtype) for array in arrays]
        + [
            pltpu.VMEM((6, 2, 64, 128), F32),
            pltpu.VMEM((32, 128), F32),
            pltpu.SemaphoreType.DMA((6,)),
        ],
        tuple(pltpu.with_memory_space_constraint(array, pltpu.HBM) for array in arrays),
        smem=False,
        space=pltpu.HBM,
    )
    halo = exchange(*packed)
    shapes = []
    for level in range(3):
        shapes += [sds(*field(level))] * 2 + [sds(*plane(level))] * 2 + [sds(*field(level))]
    state = call(
        down_one,
        shapes + [sds(blocks, 3, 8, 128)],
        masked_scratch() + [pltpu.VMEM((F, 1, 1, 16, 128), F32)],
        (coupling,) + halo,
    )
    x0, r0, s0, m0, i0, x1, r1, s1, m1, i1, x2, r2, s2, m2, i2, payload = state
    statics = lax.all_to_all(payload, "gx", 0, 0)
    inner = [pltpu.VMEM(field(level), F32) for level in range(3)]
    packed = call(
        up_one,
        [sds(XTILES, 8, 128), sds(XTILES // 2, 8, 128), sds(XTILES // 2, 8, 128)],
        inner + masked_scratch() + coarsest_scratch(blocks),
        (coupling, statics, x0, r0, m0, i0, x1, r1, m1, i1, x2, r2, m2, i2),
    )
    halo = exchange(*packed)
    x0, x1, r1, x2, r2, payload = call(
        down_two,
        [sds(*field(0)), sds(*field(1)), sds(*field(1)), sds(*field(2)), sds(*field(2)),
         sds(blocks, 2, 8, 128)],
        masked_scratch() + [pltpu.VMEM((F, 1, 1, 16, 128), F32)],
        (coupling,) + halo + (r0, s0, m0, i0, s1, m1, i1, s2, m2, i2),
    )
    gathered = lax.all_to_all(payload, "gx", 0, 0)
    displacement, residual = call(
        up_two,
        [sds(F, 64, 256), sds(F, 64, 256)],
        inner + masked_scratch() + coarsest_scratch(blocks)
        + [pltpu.VMEM((2 * F, 2, 64, 128), F32)],
        (coupling, gathered, statics, x0, r0, s0, m0, i0, x1, r1, m1, i1, x2, r2, m2, i2),
    )
    return displacement, residual


def solution(mesh):
    placed = (
        P(None, "gx", "gy"),
        P("gx", "gy"),
        P(),
        P("gx", "gy"),
        P("gx", "gy"),
        P("gx", "gy"),
        P("gx", "gy"),
    )
    return jax.shard_map(
        shards,
        mesh=mesh,
        in_specs=placed,
        out_specs=(P(None, "gx", "gy"), P(None, "gx", "gy")),
        check_vma=False,
    )
```

```python
import functools

import jax
import jax.numpy as jnp
from jax import lax
from jax.experimental import pallas as pl
from jax.experimental.pallas import tpu as pltpu
from jax.sharding import PartitionSpec as P


F = 4
ROWS = (8, 4, 2)
COLS = (4, 2, 1)
SCALE = (1.0, 0.25, 0.0625, 0.015625)
OMEGA = 0.6
TILES = 102
XTILES = 64
MIDDLE = 100
F32 = jnp.float32
BF16 = jnp.bfloat16


def lanes(shape):
    return lax.broadcasted_iota(jnp.int32, shape, len(shape) - 1)


def sublanes(shape):
    return lax.broadcasted_iota(jnp.int32, shape, len(shape) - 2)


def roll(value, shift, axis):
    size = value.shape[axis]
    shift = shift % size
    return value if shift == 0 else pltpu.roll(value, shift, axis)


def three(value):
    high = value.astype(BF16)
    rest = value - high.astype(F32)
    mid = rest.astype(BF16)
    low = (rest - mid.astype(F32)).astype(BF16)
    return high, mid, low


def exact_dot(value, matrix):
    parts = [jnp.dot(part, matrix, preferred_element_type=F32) for part in three(value)]
    return parts[0] + (parts[1] + parts[2])


def split_matrix(size, stride):
    c = lax.broadcasted_iota(jnp.int32, (size, size), 0)
    o = lax.broadcasted_iota(jnp.int32, (size, size), 1)
    return jnp.where(o == (c % stride) * (size // stride) + c // stride, 1.0, 0.0).astype(BF16)


def join_matrix(size, stride):
    o = lax.broadcasted_iota(jnp.int32, (size, size), 0)
    c = lax.broadcasted_iota(jnp.int32, (size, size), 1)
    return jnp.where(o == (c % stride) * (size // stride) + c // stride, 1.0, 0.0).astype(BF16)


def is_even(axis):
    return lax.broadcast(lax.rem(lax.axis_index(axis), 2), (8, 128)) == 0


def meet(after, before, even):
    return jnp.where(even, after, before), jnp.where(even, before, after)


def pack_rows(own, one, two, count):
    low = sublanes((8, 128)) < 4
    even = is_even("gx")

    def body(n, _):
        a = own[2 * n]
        b = own[2 * n + 1]
        up = jnp.where(low, a, roll(b, 4, 0))
        dn = jnp.where(low, roll(a, 4, 0), b)
        one[n], two[n] = meet(dn, up, even)
        return _

    lax.fori_loop(0, count // 2, body, 0, unroll=3)


def outer_rows(one, two, n, odd, even):
    low = sublanes((8, 128)) < 4
    up, dn = meet(one[n], two[n], even)
    if odd:
        return jnp.where(low, roll(up, 4, 0), dn)
    return jnp.where(low, up, roll(dn, 4, 0))


def pack_kernel(
    source_in, reaction_in, solid0_in, solid1_in, solid2_in, solid3_in, own, one, two,
    source, reaction, solid0, solid1, solid2, solid3, stage, small, arrived,
):
    moves = [
        pltpu.make_async_copy(there, here, arrived.at[n])
        for n, (there, here) in enumerate(
            (
                (source_in, source),
                (reaction_in, reaction),
                (solid0_in, solid0),
                (solid1_in, solid1),
                (solid2_in, solid2),
                (solid3_in, solid3),
            )
        )
    ]
    for move in moves:
        move.start()
    matrix = split_matrix(256, 4)
    for move in moves:
        move.wait()
    for a in range(6):
        if a < 4:
            value = exact_dot(source[a], matrix)
        elif a == 4:
            value = exact_dot(reaction[...], matrix)
        else:
            value = jnp.dot(
                solid0[...].astype(F32).astype(BF16), matrix, preferred_element_type=F32
            )
        for h in range(2):
            stage[a, h] = value[:, 128 * h : 128 * h + 128]
    for a in range(6):
        for q in range(8):
            for h in range(2):
                own[a * 16 + q * 2 + h] = stage[a, h, pl.ds(q, 8, stride=8), :]
    small[...] = jnp.dot(
        solid1[...].astype(F32).astype(BF16),
        split_matrix(128, 2),
        preferred_element_type=F32,
    )
    for q in range(4):
        own[96 + q] = small[pl.ds(q, 8, stride=4), :]
    c = lax.broadcasted_iota(jnp.int32, (64, 128), 0)
    o = lax.broadcasted_iota(jnp.int32, (64, 128), 1)
    wide = jnp.where(o % 64 == c, 1.0, 0.0).astype(BF16)
    small[pl.ds(0, 16), :] = jnp.dot(
        solid2[...].astype(F32).astype(BF16), wide, preferred_element_type=F32
    )
    own[100] = jnp.where(
        lanes((8, 128)) < 64,
        small[pl.ds(0, 8, stride=2), :],
        small[pl.ds(1, 8, stride=2), :],
    )
    c = lax.broadcasted_iota(jnp.int32, (32, 128), 0)
    o = lax.broadcasted_iota(jnp.int32, (32, 128), 1)
    twice = jnp.where((o % 64) // 2 == c, 1.0, 0.0)
    own[101] = jnp.dot(
        solid3[...].astype(F32), twice, preferred_element_type=F32,
        precision=lax.Precision.HIGHEST,
    )
    pack_rows(own, one, two, TILES)


def pack_sides(pick, count, one, two, even):
    lane = lanes((8, 128)) % 64
    for g in range(-(-count // 3)):
        members = min(3, count - 3 * g)
        for v in range(2):
            tiles = [pick(3 * g + t, v) for t in range(members)]
            r, l = tiles[0], tiles[0]
            for t in range(1, members):
                r = jnp.where(lane < 64 - 20 * t, roll(tiles[t], -20 * t, 1), r)
                l = jnp.where(lane >= 20 * t, roll(tiles[t], 20 * t, 1), l)
            one[g, v], two[g, v] = meet(r, l, even)


def side_kernel(count, own, up_one, up_two, one, two):
    even = is_even("gx")

    def pick(index, v):
        if v == 0:
            return own[index]
        return outer_rows(up_one, up_two, index // 2, index % 2, even)

    pack_sides(pick, count, one, two, is_even("gy"))


def sides(one, two, index, v, even):
    g, t = index // 3, index % 3
    l, r = meet(one[g, v], two[g, v], even)
    return [
        (roll(r, 64 + 20 * t + 64 * h, 1), roll(l, 64 - 20 * t + 64 * h, 1)) for h in range(2)
    ]


def with_sides(centre, before, after):
    lane = lanes((8, 128))
    tile = jnp.where(lane < 64, centre, jnp.where(lane < 84, after, 0.0))
    return jnp.where(lane >= 108, before, tile)


def widen(own, row_one, row_two, one, two, index, even_x, even_y):
    out = [[], []]
    for v in range(2):
        if v == 0:
            mine = own[index]
        else:
            mine = outer_rows(row_one, row_two, index // 2, index % 2, even_x)
        halo = sides(one, two, index, v, even_y)
        for h in range(2):
            out[h].append(with_sides(roll(mine, 64 * h, 1), *halo[h]))
    return [jnp.concatenate(pair, axis=0) for pair in out]


def fix_ends(masked, level):
    R, C = ROWS[level], COLS[level]
    for f in range(F):
        for p in range(C):
            masked[f, 0, p + 1] = roll(masked[f, R, p + 1], 1, 0)
            masked[f, R + 1, p + 1] = roll(masked[f, 1, p + 1], -1, 0)
        for q in range(R):
            masked[f, q + 1, 0] = roll(masked[f, q + 1, C], 1, 1)
            masked[f, q + 1, C + 1] = roll(masked[f, q + 1, 1], -1, 1)


def put_masked(masked, level, f, q, p, value):
    masked[f, q + 1, p + 1] = value


def each_row(count, body):
    if count > 4:
        def step(q, _):
            body(q)
            return _

        lax.fori_loop(0, count, step, 0, unroll=count)
    else:
        for q in range(count):
            body(q)


def drive(level, K, x, masked, rhs, solid, q, p, rows=slice(None)):
    xs = [x[f, q, p, rows] for f in range(F)]
    weight = solid[q, p, rows]
    if level:
        weight = weight * SCALE[level]
    out = []
    for f in range(F):
        near = (masked[f, q, p + 1, rows] + masked[f, q + 2, p + 1, rows]) + (
            masked[f, q + 1, p, rows] + masked[f, q + 1, p + 2, rows]
        )
        total = rhs[f, q, p, rows] + weight * near
        mixed = None
        for b in range(F):
            if b != f:
                term = K[f, b] * xs[b]
                mixed = term if mixed is None else mixed + term
        out.append(total - mixed)
    return out, xs


def sweep(level, K, x, masked, target, rhs, solid, inverse, last=False):
    R, C = ROWS[level], COLS[level]

    def body(q):
        news = []
        for p in range(C):
            drives, xs = drive(level, K, x, masked, rhs, solid, q, p)
            news.append(
                [(1.0 - OMEGA) * xs[f] + inverse[f, q, p] * drives[f] for f in range(F)]
            )
        for p in range(C):
            m = None if last else solid[q, p]
            for f in range(F):
                x[f, q, p] = news[p][f]
                if not last:
                    put_masked(target, level, f, q, p, m * news[p][f])

    each_row(R, body)
    if not last:
        fix_ends(target, level)


def first(level, x, masked, rhs, solid, inverse):
    def body(q):
        for p in range(COLS[level]):
            m = solid[q, p]
            for f in range(F):
                new = inverse[f, q, p] * rhs[f, q, p]
                x[f, q, p] = new
                put_masked(masked, level, f, q, p, m * new)

    each_row(ROWS[level], body)
    fix_ends(masked, level)


def mask(level, x, masked, solid):
    def body(q):
        for p in range(COLS[level]):
            m = solid[q, p]
            for f in range(F):
                put_masked(masked, level, f, q, p, m * x[f, q, p])

    each_row(ROWS[level], body)
    fix_ends(masked, level)


def restrict(level, K, x, masked, rhs, solid, react, coarse):
    R, C = ROWS[level], COLS[level]
    wide = 2 if C > 1 else 1

    def body(half):
        for P_ in range(C // wide):
            sums = [None] * F
            for dq in range(2):
                for dp in range(wide):
                    q, p = 2 * half + dq, wide * P_ + dp
                    drives, xs = drive(level, K, x, masked, rhs, solid, q, p)
                    s = react[q, p]
                    for f in range(F):
                        e = drives[f] - (s + (4.0 * SCALE[level] + K[f, f])) * xs[f]
                        sums[f] = e if sums[f] is None else sums[f] + e
            for f in range(F):
                coarse[f, half, P_] = sums[f] * (0.5 / wide)

    each_row(R // 2, body)


def near_rows(value):
    outer = jnp.where(sublanes((8, 128)) < 4, value[8:16], value[16:24])
    return jnp.concatenate([value[0:8], outer], axis=0)


def prolong(level, x, masked, solid, source):
    def body(half):
        for dq in range(2):
            q = 2 * half + dq
            for p in range(COLS[level]):
                m = solid[q, p]
                for f in range(F):
                    fix = source[f, half, p // 2]
                    if fix.shape[0] == 24 and m.shape[0] == 16:
                        fix = near_rows(fix)
                    new = x[f, q, p] + fix
                    x[f, q, p] = new
                    put_masked(masked, level, f, q, p, m * new)

    each_row(ROWS[level] // 2, body)
    fix_ends(masked, level)


def invert(level, K, react, inverse):
    def body(q):
        for p in range(COLS[level]):
            s = react[q, p]
            for f in range(F):
                inverse[f, q, p] = OMEGA / (s + (4.0 * SCALE[level] + K[f, f]))

    each_row(ROWS[level], body)


def decimate():
    k = lax.broadcasted_iota(jnp.int32, (128, 128), 0)
    o = lax.broadcasted_iota(jnp.int32, (128, 128), 1)
    return jnp.where(o == (k // 2 + 10) % 64, 0.5, 0.0).astype(BF16)


def spread(half):
    o = lax.broadcasted_iota(jnp.int32, (128, 128), 0)
    k = lax.broadcasted_iota(jnp.int32, (128, 128), 1)
    return jnp.where(o == (k // 2 + 10) % 64 + 64 * half, 1.0, 0.0).astype(BF16)


def half_pair(a, b):
    return jnp.where(lanes((8, 128)) < 64, a, roll(b, 64, 1))


def descend(K, X, M, RHS, SOLID, REACT, INV):
    for level in range(3):
        a, b = M[level]
        if level:
            first(level, X[level], a, RHS[level], SOLID[level], INV[level])
            sweep(level, K, X[level], a, b, RHS[level], SOLID[level], INV[level])
        if level < 2:
            restrict(
                level, K, X[level], b, RHS[level], SOLID[level], REACT[level], RHS[level + 1]
            )


def coarse_rhs(K, X, M, RHS, SOLID, REACT, three_rhs):
    restrict(2, K, X[2], M[2][1], RHS[2], SOLID[2], REACT[2], three_rhs)
    return [three_rhs[f, 0, 0, 0:8] for f in range(F)]


def middle_tiles(x1, r1, s1, m1, x2, r2, s2, m2):
    for level, (x, r, s, m) in ((1, (x1, r1, s1, m1)), (2, (x2, r2, s2, m2))):
        for q in range(ROWS[level]):
            for p in range(COLS[level]):
                for f in range(F):
                    yield x[f, q, p]
                    yield r[f, q, p]
                yield s[q, p]
                yield m[q, p]


def down_one(
    K, own, row_one, row_two, one, two,
    x0, r0, s0, m0, i0, x1, r1, s1, m1, i1, x2, r2, s2, m2, i2, middle, payload,
    ma0, mb0, ma1, mb1, ma2, mb2, three_rhs,
):
    halo = (own, row_one, row_two, one, two)
    even = (is_even("gx"), is_even("gy"))
    for a in range(6):
        for q in range(8):
            for h in range(2):
                pair = widen(*halo, a * 16 + q * 2 + h, *even)
                for e in range(2):
                    if a < 4:
                        r0[a, q, 2 * h + e] = pair[e]
                    elif a == 4:
                        s0[q, 2 * h + e] = pair[e]
                    else:
                        m0[q, 2 * h + e] = pair[e]
    for q in range(4):
        pair = widen(*halo, 96 + q, *even)
        m1[q, 0], m1[q, 1] = pair
    pair = widen(*halo, 100, *even)
    m2[0, 0], m2[1, 0] = pair
    m3 = widen(*halo, 101, *even)[0]
    for q in range(4):
        for p in range(2):
            s1[q, p] = 0.25 * (
                (s0[2 * q, 2 * p] + s0[2 * q, 2 * p + 1])
                + (s0[2 * q + 1, 2 * p] + s0[2 * q + 1, 2 * p + 1])
            )
    for q in range(2):
        s2[q, 0] = 0.25 * (
            (s1[2 * q, 0] + s1[2 * q, 1]) + (s1[2 * q + 1, 0] + s1[2 * q + 1, 1])
        )
    X, RHS, SOLID, REACT, INV = (x0, x1, x2), (r0, r1, r2), (m0, m1, m2), (s0, s1, s2), (i0, i1, i2)
    M = ((ma0, mb0), (ma1, mb1), (ma2, mb2))
    for level in range(3):
        invert(level, K, REACT[level], INV[level])
    first(0, x0, ma0, r0, m0, i0)
    sweep(0, K, x0, ma0, mb0, r0, m0, i0)
    descend(K, X, M, RHS, SOLID, REACT, INV)
    for n, tile in enumerate(middle_tiles(x1, r1, s1, m1, x2, r2, s2, m2)):
        middle[n] = tile[0:8]
    rest = coarse_rhs(K, X, M, RHS, SOLID, REACT, three_rhs)
    s3 = 0.5 * (s2[0, 0, 0:8] + s2[1, 0, 0:8])
    y = exact_dot(jnp.concatenate(rest + [m3[0:8], s3], axis=0), decimate())
    y = [y[8 * n : 8 * n + 8] for n in range(6)]
    tiles = [half_pair(y[0], y[1]), half_pair(y[2], y[3]), half_pair(y[4], y[5])]
    for d in range(payload.shape[0]):
        for n in range(3):
            payload[d, n] = tiles[n]


def down_two(
    K, x0i, one, two, r0, s0, m0, i0, s1, m1, i1, s2, m2, i2,
    x0, x1, r1, x2, r2, payload,
    ma0, mb0, ma1, mb1, ma2, mb2, three_rhs,
):
    even = is_even("gy")
    for a in range(F):
        for q in range(8):
            for h in range(2):
                halo = [sides(one, two, a * 16 + q * 2 + h, v, even) for v in range(2)]
                for e in range(2):
                    mine = x0i[a, q, 2 * h + e]
                    x0[a, q, 2 * h + e] = jnp.concatenate(
                        [with_sides(mine[8 * v : 8 * v + 8], *halo[v][e]) for v in range(2)],
                        axis=0,
                    )
    X, RHS, SOLID, REACT, INV = (x0, x1, x2), (r0, r1, r2), (m0, m1, m2), (s0, s1, s2), (i0, i1, i2)
    M = ((ma0, mb0), (ma1, mb1), (ma2, mb2))
    mask(0, x0, mb0, m0)
    sweep(0, K, x0, mb0, ma0, r0, m0, i0)
    sweep(0, K, x0, ma0, mb0, r0, m0, i0)
    descend(K, X, M, RHS, SOLID, REACT, INV)
    rest = coarse_rhs(K, X, M, RHS, SOLID, REACT, three_rhs)
    y = exact_dot(jnp.concatenate(rest + rest[0:2], axis=0), decimate())
    y = [y[8 * n : 8 * n + 8] for n in range(4)]
    tiles = [half_pair(y[0], y[1]), half_pair(y[2], y[3])]
    for d in range(payload.shape[0]):
        for n in range(2):
            payload[d, n] = tiles[n]


def solve_coarsest(K, gathered, statics, natural, x, ma, mb, rhs, solid, react, inverse, wide, correct):
    low = lanes((8, 128)) < 64
    top = sublanes((8, 128)) == 0
    bottom = sublanes((8, 128)) == 7
    c = SCALE[3]
    blocks = gathered.shape[0]
    for d in range(blocks):
        natural[0, pl.ds(8 * d, 8), :] = gathered[d, 0]
        natural[1, pl.ds(8 * d, 8), :] = gathered[d, 1]
        natural[2, pl.ds(8 * d, 8), :] = statics[d, 2]
    diagonal = [jnp.where(low, 4.0 * c + K[2 * n, 2 * n], 4.0 * c + K[2 * n + 1, 2 * n + 1]) for n in range(2)]
    weights = [
        (jnp.where(low, K[0, 1], K[1, 0]), jnp.where(low, K[0, 2], K[1, 3]), jnp.where(low, K[0, 3], K[1, 2])),
        (jnp.where(low, K[2, 3], K[3, 2]), jnp.where(low, K[2, 0], K[3, 1]), jnp.where(low, K[2, 1], K[3, 0])),
    ]
    for t in range(blocks):
        pick = pl.ds(t, 8, stride=blocks)
        both = natural[2, pick, :]
        turned = roll(both, 64, 1)
        m = jnp.where(low, both, turned)
        s = jnp.where(low, turned, both)
        solid[t] = m
        react[t] = s
        for n in range(2):
            r = natural[n, pick, :]
            i = OMEGA / (s + diagonal[n])
            rhs[n, t] = r
            inverse[n, t] = i
            x[n, t] = i * r
            ma[n, t + 1] = m * (i * r)

    def ends(masked):
        for n in range(2):
            masked[n, 0] = jnp.where(top, 0.0, roll(masked[n, blocks], 1, 0))
            masked[n, blocks + 1] = jnp.where(bottom, 0.0, roll(masked[n, 1], -1, 0))

    def drives(t, masked):
        weight = c * solid[t]
        xs = [x[0, t], x[1, t]]
        turned = [roll(v, 64, 1) for v in xs]
        out = []
        for n in range(2):
            here = masked[n, t + 1]
            near = (masked[n, t] + masked[n, t + 2]) + (roll(here, 1, 1) + roll(here, -1, 1))
            u, v, w = weights[n]
            mixed = u * turned[n] + v * xs[1 - n] + w * turned[1 - n]
            out.append(rhs[n, t] + weight * near - mixed)
        return out, xs

    ends(ma)
    for index in range(5):
        source, target = (ma, mb) if index % 2 == 0 else (mb, ma)

        def body(t, _):
            out, xs = drives(t, source)
            m = solid[t]
            for n in range(2):
                new = (1.0 - OMEGA) * xs[n] + inverse[n, t] * out[n]
                x[n, t] = new
                target[n, t + 1] = m * new
            return _

        lax.fori_loop(0, blocks, body, 0, unroll=blocks)
        ends(target)

    def gather_sums(t, sums):
        out, xs = drives(t, mb)
        s = react[t]
        sums = list(sums)
        for n in range(2):
            g = s + diagonal[n]
            sums[n] = sums[n] + (out[n] - g * xs[n])
            sums[2 + n] = sums[2 + n] + g
        return tuple(sums)

    zero = jnp.zeros((8, 128), F32)
    sums = lax.fori_loop(0, blocks, gather_sums, (zero,) * 4, unroll=blocks)
    sums = [jnp.sum(v, axis=0, keepdims=True) for v in sums]
    for n in range(2):
        wide[n, pl.ds(0, 8), :] = zero
        wide[n, pl.ds(8 * blocks + 8, 8), :] = zero
        mean = sums[n] / sums[2 + n]
        for t in range(blocks):
            wide[n, pl.ds(8 + t, 8, stride=blocks), :] = x[n, t] + mean
    start = pl.multiple_of(lax.axis_index("gx") * 8, 8)
    low = sublanes((8, 128)) < 4
    height = correct.shape[-2]
    rows = []
    for n in range(2):
        mine = wide[n, pl.ds(start + 8, 8), :]
        after = wide[n, pl.ds(start + 16, 8), :]
        before = wide[n, pl.ds(start, 8), :]
        rows += [mine, after, before] if height == 24 else [mine, jnp.where(low, after, before)]
    rows = jnp.concatenate(rows, axis=0)
    for half in range(2):
        y = exact_dot(rows, spread(half))
        correct[half, 0, 0] = y[0:height]
        correct[2 + half, 0, 0] = y[height : 2 * height]


def ascend(K, X, M, RHS, SOLID, INV, correct, last):
    source = correct
    for level in (2, 1, 0):
        a, b = M[level]
        prolong(level, X[level], a, SOLID[level], source)
        sweep(level, K, X[level], a, b, RHS[level], SOLID[level], INV[level])
        sweep(
            level, K, X[level], b, a, RHS[level], SOLID[level], INV[level],
            last=level > 0 or not last,
        )
        source = X[level]


def copy_state(sources, targets):
    for source, target in zip(sources, targets):
        target[...] = source[...]


def up_one(
    K, gathered, mine, from_one, from_two, x0i, r0, m0, i0,
    x0, one, two,
    x1, r1, s1, m1, i1, x2, r2, s2, m2, i2, ma0, mb0, ma1, mb1, ma2, mb2,
    natural, x3, ma3, mb3, r3, m3, s3, i3, wide, correct,
):
    even = is_even("gx")
    n = 0

    def tall():
        nonlocal n
        after, before = meet(from_one[n], from_two[n], even)
        tile = jnp.concatenate([mine[n], after, before], axis=0)
        n += 1
        return tile

    for level, (x, r, s, m) in ((1, (x1, r1, s1, m1)), (2, (x2, r2, s2, m2))):
        for q in range(ROWS[level]):
            for p in range(COLS[level]):
                for f in range(F):
                    x[f, q, p] = tall()
                    r[f, q, p] = tall()
                s[q, p] = tall()
                m[q, p] = tall()
    invert(1, K, s1, i1)
    invert(2, K, s2, i2)
    x0[...] = x0i[...]
    solve_coarsest(K, gathered, gathered, natural, x3, ma3, mb3, r3, m3, s3, i3, wide, correct)
    M = ((ma0, mb0), (ma1, mb1), (ma2, mb2))
    ascend(K, (x0, x1, x2), M, (r0, r1, r2), (m0, m1, m2), (i0, i1, i2), correct, False)

    def pick(index, v):
        f, q, h = index // 16, index // 2 % 8, index % 2
        part = slice(8 * v, 8 * v + 8)
        return half_pair(x0[f, q, 2 * h, part], x0[f, q, 2 * h + 1, part])

    pack_sides(pick, XTILES, one, two, is_even("gy"))


def up_two(
    K, gathered, statics, x0i, r0, s0, m0, i0, x1i, r1, m1, i1, x2i, r2, m2, i2,
    displacement, residual,
    x0, x1, x2, ma0, mb0, ma1, mb1, ma2, mb2,
    natural, x3, ma3, mb3, r3, m3, s3, i3, wide, correct, stage,
):
    copy_state((x0i, x1i, x2i), (x0, x1, x2))
    solve_coarsest(K, gathered, statics, natural, x3, ma3, mb3, r3, m3, s3, i3, wide, correct)
    M = ((ma0, mb0), (ma1, mb1), (ma2, mb2))
    ascend(K, (x0, x1, x2), M, (r0, r1, r2), (m0, m1, m2), (i0, i1, i2), correct, True)
    mine = slice(0, 8)
    for q in range(8):
        for h in range(2):
            outs = []
            for p in (2 * h, 2 * h + 1):
                drives, xs = drive(0, K, x0, ma0, r0, m0, q, p, mine)
                s = s0[q, p, mine]
                rest = [drives[f] - (s + (4.0 + K[f, f])) * xs[f] for f in range(F)]
                outs.append(xs + rest)
            for a in range(2 * F):
                stage[a, h, pl.ds(q, 8, stride=8), :] = half_pair(outs[0][a], outs[1][a])
    matrix = join_matrix(256, 4)
    for f in range(F):
        for out, a in ((displacement, f), (residual, F + f)):
            out[f] = exact_dot(jnp.concatenate([stage[a, 0], stage[a, 1]], axis=1), matrix)


def sds(*shape):
    return jax.ShapeDtypeStruct(shape, F32)


def field(level, height=16):
    return (F, ROWS[level], COLS[level], height, 128)


def plane(level, height=16):
    return (ROWS[level], COLS[level], height, 128)


def masked_scratch(height=16):
    out = []
    for level in range(3):
        tall = height if level else 16
        shape = (F, ROWS[level] + 2, COLS[level] + 2, tall, 128)
        out += [pltpu.VMEM(shape, F32), pltpu.VMEM(shape, F32)]
    return out


def coarsest_scratch(blocks, height=16):
    return [
        pltpu.VMEM((3, 8 * blocks, 128), F32),
        pltpu.VMEM((2, blocks, 8, 128), F32),
        pltpu.VMEM((2, blocks + 2, 8, 128), F32),
        pltpu.VMEM((2, blocks + 2, 8, 128), F32),
        pltpu.VMEM((2, blocks, 8, 128), F32),
        pltpu.VMEM((blocks, 8, 128), F32),
        pltpu.VMEM((blocks, 8, 128), F32),
        pltpu.VMEM((2, blocks, 8, 128), F32),
        pltpu.VMEM((2, 8 * blocks + 16, 128), F32),
        pltpu.VMEM((F, 1, 1, height, 128), F32),
    ]


def call(body, outs, scratch, args, smem=True, space=pltpu.VMEM):
    specs = [pl.BlockSpec(memory_space=space)] * len(args)
    if smem:
        specs[0] = pl.BlockSpec(memory_space=pltpu.SMEM)
    return pl.pallas_call(
        body,
        out_shape=outs,
        in_specs=specs,
        out_specs=[pl.BlockSpec(memory_space=pltpu.VMEM)] * len(outs),
        scratch_shapes=scratch,
        compiler_params=pltpu.CompilerParams(vmem_limit_bytes=30 * 1024 * 1024),
    )(*args)


def swap(axis, first, second):
    count = lax.axis_size(axis)
    near = [(i, i ^ 1) for i in range(count) if i ^ 1 < count]
    far = [(i, ((i - 1) ^ 1) + 1) for i in range(1, count) if ((i - 1) ^ 1) + 1 < count]
    return lax.ppermute(first, axis, near), lax.ppermute(second, axis, far)


def shards(source, reaction, coupling, solid0, solid1, solid2, solid3):
    blocks = lax.axis_size("gx")
    arrays = (source, reaction, solid0, solid1, solid2, solid3)
    packed = call(
        pack_kernel,
        [sds(TILES, 8, 128), sds(TILES // 2, 8, 128), sds(TILES // 2, 8, 128)],
        [pltpu.VMEM(array.shape, array.dtype) for array in arrays]
        + [
            pltpu.VMEM((6, 2, 64, 128), F32),
            pltpu.VMEM((32, 128), F32),
            pltpu.SemaphoreType.DMA((6,)),
        ],
        tuple(pltpu.with_memory_space_constraint(array, pltpu.HBM) for array in arrays),
        smem=False,
        space=pltpu.HBM,
    )
    own, one, two = packed
    rows = swap("gx", one, two)
    side = call(
        functools.partial(side_kernel, TILES),
        [sds(TILES // 3, 2, 8, 128)] * 2,
        [],
        (own,) + rows,
        smem=False,
    )
    halo = (own,) + rows + swap("gy", *side)
    shapes = []
    for level in range(3):
        shapes += [sds(*field(level))] * 2 + [sds(*plane(level))] * 2 + [sds(*field(level))]
    state = call(
        down_one,
        shapes + [sds(MIDDLE, 8, 128), sds(blocks, 3, 8, 128)],
        masked_scratch() + [pltpu.VMEM((F, 1, 1, 16, 128), F32)],
        (coupling,) + halo,
    )
    x0, r0, s0, m0, i0, x1, r1, s1, m1, i1, x2, r2, s2, m2, i2, middle, payload = state
    near, far = swap("gx", middle, middle)
    statics = lax.all_to_all(payload, "gx", 0, 0)
    inner = [pltpu.VMEM(field(level), F32) for level in range(3)]
    tall = []
    for level in (1, 2):
        tall += [pltpu.VMEM(field(level, 24), F32)] * 2
        tall += [pltpu.VMEM(plane(level, 24), F32)] * 2
        tall += [pltpu.VMEM(field(level, 24), F32)]
    x0, one, two = call(
        up_one,
        [sds(*field(0))] + [sds(-(-XTILES // 3), 2, 8, 128)] * 2,
        tall + masked_scratch(24) + coarsest_scratch(blocks, 24),
        (coupling, statics, middle, near, far, x0, r0, m0, i0),
    )
    x0, x1, r1, x2, r2, payload = call(
        down_two,
        [sds(*field(0)), sds(*field(1)), sds(*field(1)), sds(*field(2)), sds(*field(2)),
         sds(blocks, 2, 8, 128)],
        masked_scratch() + [pltpu.VMEM((F, 1, 1, 16, 128), F32)],
        (coupling, x0) + swap("gy", one, two) + (r0, s0, m0, i0, s1, m1, i1, s2, m2, i2),
    )
    gathered = lax.all_to_all(payload, "gx", 0, 0)
    displacement, residual = call(
        up_two,
        [sds(F, 64, 256), sds(F, 64, 256)],
        inner + masked_scratch() + coarsest_scratch(blocks)
        + [pltpu.VMEM((2 * F, 2, 64, 128), F32)],
        (coupling, gathered, statics, x0, r0, s0, m0, i0, x1, r1, m1, i1, x2, r2, m2, i2),
    )
    return displacement, residual


def solution(mesh):
    placed = (
        P(None, "gx", "gy"),
        P("gx", "gy"),
        P(),
        P("gx", "gy"),
        P("gx", "gy"),
        P("gx", "gy"),
        P("gx", "gy"),
    )
    return jax.shard_map(
        shards,
        mesh=mesh,
        in_specs=placed,
        out_specs=(P(None, "gx", "gy"), P(None, "gx", "gy")),
        check_vma=False,
    )
```

```python
import functools

import jax
import jax.numpy as jnp
from jax import lax
from jax.experimental import pallas as pl
from jax.experimental.pallas import tpu as pltpu
from jax.sharding import PartitionSpec as P


F = 4
ROWS = (8, 4, 2)
COLS = (4, 2, 1)
SCALE = (1.0, 0.25, 0.0625, 0.015625)
OMEGA = 0.6
TILES = 102
XTILES = 64
MIDDLE = 30
STATE = 15
F32 = jnp.float32
BF16 = jnp.bfloat16


def lanes(shape):
    return lax.broadcasted_iota(jnp.int32, shape, len(shape) - 1)


def sublanes(shape):
    return lax.broadcasted_iota(jnp.int32, shape, len(shape) - 2)


def roll(value, shift, axis):
    size = value.shape[axis]
    shift = shift % size
    return value if shift == 0 else pltpu.roll(value, shift, axis)


def three(value):
    high = value.astype(BF16)
    rest = value - high.astype(F32)
    mid = rest.astype(BF16)
    low = (rest - mid.astype(F32)).astype(BF16)
    return high, mid, low


def exact_dot(value, matrix):
    parts = [jnp.dot(part, matrix, preferred_element_type=F32) for part in three(value)]
    return parts[0] + (parts[1] + parts[2])


def split_matrix(size, stride):
    c = lax.broadcasted_iota(jnp.int32, (size, size), 0)
    o = lax.broadcasted_iota(jnp.int32, (size, size), 1)
    return jnp.where(o == (c % stride) * (size // stride) + c // stride, 1.0, 0.0).astype(BF16)


def join_matrix(size, stride):
    o = lax.broadcasted_iota(jnp.int32, (size, size), 0)
    c = lax.broadcasted_iota(jnp.int32, (size, size), 1)
    return jnp.where(o == (c % stride) * (size // stride) + c // stride, 1.0, 0.0).astype(BF16)


def is_even(axis):
    return lax.broadcast(lax.rem(lax.axis_index(axis), 2), (8, 128)) == 0


def meet(after, before, even):
    return jnp.where(even, after, before), jnp.where(even, before, after)


def pack_rows(own, one, two, count):
    low = sublanes((8, 128)) < 4
    even = is_even("gx")

    def body(n, _):
        a = own[2 * n]
        b = own[2 * n + 1]
        up = jnp.where(low, a, roll(b, 4, 0))
        dn = jnp.where(low, roll(a, 4, 0), b)
        one[n], two[n] = meet(dn, up, even)
        return _

    lax.fori_loop(0, count // 2, body, 0, unroll=3)


def outer_rows(one, two, n, odd, even):
    low = sublanes((8, 128)) < 4
    up, dn = meet(one[n], two[n], even)
    if odd:
        return jnp.where(low, roll(up, 4, 0), dn)
    return jnp.where(low, up, roll(dn, 4, 0))


def pack_kernel(
    source_in, reaction_in, solid0_in, solid1_in, solid2_in, solid3_in, own, one, two,
    source, reaction, solid0, solid1, solid2, solid3, stage, small, arrived,
):
    moves = [
        pltpu.make_async_copy(there, here, arrived.at[n])
        for n, (there, here) in enumerate(
            (
                (source_in, source),
                (reaction_in, reaction),
                (solid0_in, solid0),
                (solid1_in, solid1),
                (solid2_in, solid2),
                (solid3_in, solid3),
            )
        )
    ]
    for move in moves:
        move.start()
    matrix = split_matrix(256, 4)
    for move in moves:
        move.wait()
    for a in range(6):
        if a < 4:
            value = exact_dot(source[a], matrix)
        elif a == 4:
            value = exact_dot(reaction[...], matrix)
        else:
            value = jnp.dot(
                solid0[...].astype(F32).astype(BF16), matrix, preferred_element_type=F32
            )
        for h in range(2):
            stage[a, h] = value[:, 128 * h : 128 * h + 128]
    for a in range(6):
        for q in range(8):
            for h in range(2):
                own[a * 16 + q * 2 + h] = stage[a, h, pl.ds(q, 8, stride=8), :]
    small[...] = jnp.dot(
        solid1[...].astype(F32).astype(BF16),
        split_matrix(128, 2),
        preferred_element_type=F32,
    )
    for q in range(4):
        own[96 + q] = small[pl.ds(q, 8, stride=4), :]
    c = lax.broadcasted_iota(jnp.int32, (64, 128), 0)
    o = lax.broadcasted_iota(jnp.int32, (64, 128), 1)
    wide = jnp.where(o % 64 == c, 1.0, 0.0).astype(BF16)
    small[pl.ds(0, 16), :] = jnp.dot(
        solid2[...].astype(F32).astype(BF16), wide, preferred_element_type=F32
    )
    own[100] = jnp.where(
        lanes((8, 128)) < 64,
        small[pl.ds(0, 8, stride=2), :],
        small[pl.ds(1, 8, stride=2), :],
    )
    c = lax.broadcasted_iota(jnp.int32, (32, 128), 0)
    o = lax.broadcasted_iota(jnp.int32, (32, 128), 1)
    twice = jnp.where((o % 64) // 2 == c, 1.0, 0.0)
    own[101] = jnp.dot(
        solid3[...].astype(F32), twice, preferred_element_type=F32,
        precision=lax.Precision.HIGHEST,
    )
    pack_rows(own, one, two, TILES)


def pack_sides(pick, count, one, two, even):
    lane = lanes((8, 128)) % 64
    for g in range(-(-count // 3)):
        members = min(3, count - 3 * g)
        for v in range(2):
            tiles = [pick(3 * g + t, v) for t in range(members)]
            r, l = tiles[0], tiles[0]
            for t in range(1, members):
                r = jnp.where(lane < 64 - 20 * t, roll(tiles[t], -20 * t, 1), r)
                l = jnp.where(lane >= 20 * t, roll(tiles[t], 20 * t, 1), l)
            one[g, v], two[g, v] = meet(r, l, even)


def side_kernel(count, own, up_one, up_two, one, two):
    even = is_even("gx")

    def pick(index, v):
        if v == 0:
            return own[index]
        return outer_rows(up_one, up_two, index // 2, index % 2, even)

    pack_sides(pick, count, one, two, is_even("gy"))


def sides(one, two, index, v, even):
    g, t = index // 3, index % 3
    l, r = meet(one[g, v], two[g, v], even)
    return [
        (roll(r, 64 + 20 * t + 64 * h, 1), roll(l, 64 - 20 * t + 64 * h, 1)) for h in range(2)
    ]


def with_sides(centre, before, after):
    lane = lanes((8, 128))
    tile = jnp.where(lane < 64, centre, jnp.where(lane < 84, after, 0.0))
    return jnp.where(lane >= 108, before, tile)


def widen(own, row_one, row_two, one, two, index, even_x, even_y):
    out = [[], []]
    for v in range(2):
        if v == 0:
            mine = own[index]
        else:
            mine = outer_rows(row_one, row_two, index // 2, index % 2, even_x)
        halo = sides(one, two, index, v, even_y)
        for h in range(2):
            out[h].append(with_sides(roll(mine, 64 * h, 1), *halo[h]))
    return [jnp.concatenate(pair, axis=0) for pair in out]


def fix_ends(masked, level):
    R, C = ROWS[level], COLS[level]
    for f in range(F):
        for p in range(C):
            masked[f, 0, p + 1] = roll(masked[f, R, p + 1], 1, 0)
            masked[f, R + 1, p + 1] = roll(masked[f, 1, p + 1], -1, 0)
        for q in range(R):
            masked[f, q + 1, 0] = roll(masked[f, q + 1, C], 1, 1)
            masked[f, q + 1, C + 1] = roll(masked[f, q + 1, 1], -1, 1)


def put_masked(masked, level, f, q, p, value):
    masked[f, q + 1, p + 1] = value


def each_row(count, body):
    if count > 4:
        def step(q, _):
            body(q)
            return _

        lax.fori_loop(0, count, step, 0, unroll=count)
    else:
        for q in range(count):
            body(q)


def drive(level, K, x, masked, rhs, solid, q, p, rows=slice(None)):
    xs = [x[f, q, p, rows] for f in range(F)]
    weight = solid[q, p, rows]
    if level:
        weight = weight * SCALE[level]
    out = []
    for f in range(F):
        near = (masked[f, q, p + 1, rows] + masked[f, q + 2, p + 1, rows]) + (
            masked[f, q + 1, p, rows] + masked[f, q + 1, p + 2, rows]
        )
        total = rhs[f, q, p, rows] + weight * near
        mixed = None
        for b in range(F):
            if b != f:
                term = K[f, b] * xs[b]
                mixed = term if mixed is None else mixed + term
        out.append(total - mixed)
    return out, xs


def sweep(level, K, x, masked, target, rhs, solid, inverse, last=False):
    R, C = ROWS[level], COLS[level]

    def body(q):
        news = []
        for p in range(C):
            drives, xs = drive(level, K, x, masked, rhs, solid, q, p)
            news.append(
                [(1.0 - OMEGA) * xs[f] + inverse[f, q, p] * drives[f] for f in range(F)]
            )
        for p in range(C):
            m = None if last else solid[q, p]
            for f in range(F):
                x[f, q, p] = news[p][f]
                if not last:
                    put_masked(target, level, f, q, p, m * news[p][f])

    each_row(R, body)
    if not last:
        fix_ends(target, level)


def first(level, x, masked, rhs, solid, inverse):
    def body(q):
        for p in range(COLS[level]):
            m = solid[q, p]
            for f in range(F):
                new = inverse[f, q, p] * rhs[f, q, p]
                x[f, q, p] = new
                put_masked(masked, level, f, q, p, m * new)

    each_row(ROWS[level], body)
    fix_ends(masked, level)


def mask(level, x, masked, solid):
    def body(q):
        for p in range(COLS[level]):
            m = solid[q, p]
            for f in range(F):
                put_masked(masked, level, f, q, p, m * x[f, q, p])

    each_row(ROWS[level], body)
    fix_ends(masked, level)


def restrict(level, K, x, masked, rhs, solid, react, coarse):
    R, C = ROWS[level], COLS[level]
    wide = 2 if C > 1 else 1

    def body(half):
        for P_ in range(C // wide):
            sums = [None] * F
            for dq in range(2):
                for dp in range(wide):
                    q, p = 2 * half + dq, wide * P_ + dp
                    drives, xs = drive(level, K, x, masked, rhs, solid, q, p)
                    s = react[q, p]
                    for f in range(F):
                        e = drives[f] - (s + (4.0 * SCALE[level] + K[f, f])) * xs[f]
                        sums[f] = e if sums[f] is None else sums[f] + e
            for f in range(F):
                coarse[f, half, P_] = sums[f] * (0.5 / wide)

    each_row(R // 2, body)


def near_rows(value):
    outer = jnp.where(sublanes((8, 128)) < 4, value[8:16], value[16:24])
    return jnp.concatenate([value[0:8], outer], axis=0)


def prolong(level, x, masked, solid, source):
    def body(half):
        for dq in range(2):
            q = 2 * half + dq
            for p in range(COLS[level]):
                m = solid[q, p]
                for f in range(F):
                    fix = source[f, half, p // 2]
                    if fix.shape[0] == 24 and m.shape[0] == 16:
                        fix = near_rows(fix)
                    new = x[f, q, p] + fix
                    x[f, q, p] = new
                    put_masked(masked, level, f, q, p, m * new)

    each_row(ROWS[level] // 2, body)
    fix_ends(masked, level)


def invert(level, K, react, inverse):
    def body(q):
        for p in range(COLS[level]):
            s = react[q, p]
            for f in range(F):
                inverse[f, q, p] = OMEGA / (s + (4.0 * SCALE[level] + K[f, f]))

    each_row(ROWS[level], body)


def decimate():
    k = lax.broadcasted_iota(jnp.int32, (128, 128), 0)
    o = lax.broadcasted_iota(jnp.int32, (128, 128), 1)
    return jnp.where(o == (k // 2 + 10) % 64, 0.5, 0.0).astype(BF16)


def spread(half):
    o = lax.broadcasted_iota(jnp.int32, (128, 128), 0)
    k = lax.broadcasted_iota(jnp.int32, (128, 128), 1)
    return jnp.where(o == (k // 2 + 10) % 64 + 64 * half, 1.0, 0.0).astype(BF16)


def half_pair(a, b):
    return jnp.where(lanes((8, 128)) < 64, a, roll(b, 64, 1))


def descend(K, X, M, RHS, SOLID, REACT, INV):
    for level in range(3):
        a, b = M[level]
        if level:
            first(level, X[level], a, RHS[level], SOLID[level], INV[level])
            sweep(level, K, X[level], a, b, RHS[level], SOLID[level], INV[level])
        if level < 2:
            restrict(
                level, K, X[level], b, RHS[level], SOLID[level], REACT[level], RHS[level + 1]
            )


def coarse_rhs(K, X, M, RHS, SOLID, REACT, three_rhs):
    restrict(2, K, X[2], M[2][1], RHS[2], SOLID[2], REACT[2], three_rhs)
    return [three_rhs[f, 0, 0, 0:8] for f in range(F)]


def levels_one_two(state_one, state_two):
    out = []
    for level, (x, r, s, m) in ((1, state_one), (2, state_two)):
        keys = []
        for q in range(ROWS[level]):
            for p in range(COLS[level]):
                for f in range(F):
                    keys.append((x, (f, q, p)))
                    keys.append((r, (f, q, p)))
                keys.append((s, (q, p)))
                keys.append((m, (q, p)))
        out.append(keys)
    return out


TAKE = ((3, 2), (2, 4))


def pack_middle(keys, middle):
    sub = sublanes((8, 128))
    place = 0
    for (start, size), members in zip(TAKE, keys):
        each = 8 // size
        for g in range(0, len(members), each):
            tile = None
            for u in range(each):
                ref, index = members[g + u]
                part = roll(ref[index][0:8], size * u - start, 0)
                tile = part if tile is None else jnp.where(sub >= size * u, part, tile)
            middle[place] = tile
            place += 1


def grow(keys, tall_keys, near, far, even):
    sub = sublanes((8, 128))
    place = 0
    for (start, size), members, targets in zip(TAKE, keys, tall_keys):
        each = 8 // size
        for g in range(0, len(members), each):
            after, before = meet(near[place], far[place], even)
            for u in range(each):
                ref, index = members[g + u]
                tile = ref[index]
                inner, outer = tile[0:8], tile[8:16]
                later = roll(after, start - size * u, 0)
                sooner = roll(before, start - size * u, 0)
                later = jnp.where(sub < start, outer, jnp.where(sub < start + size, later, 0.0))
                sooner = jnp.where(
                    sub >= start + size, outer, jnp.where(sub >= start, sooner, 0.0)
                )
                target, index = targets[g + u]
                target[index] = jnp.concatenate([inner, later, sooner], axis=0)
            place += 1


def down_one(K, own, row_one, row_two, one, two, *refs):
    there, payload = refs[: STATE + 1], refs[STATE + 1]
    here = refs[STATE + 2 : 2 * STATE + 3]
    ma0, mb0, ma1, mb1, ma2, mb2, three_rhs, tile, sent, spread_sent = refs[2 * STATE + 3 :]
    x0, r0, s0, m0, i0, x1, r1, s1, m1, i1, x2, r2, s2, m2, i2, middle = here
    moves = []

    def send(*which):
        for n in which:
            move = pltpu.make_async_copy(here[n], there[n], sent.at[n])
            move.start()
            moves.append(move)

    halo = (own, row_one, row_two, one, two)
    even = (is_even("gx"), is_even("gy"))
    for a in range(6):
        for q in range(8):
            for h in range(2):
                pair = widen(*halo, a * 16 + q * 2 + h, *even)
                for e in range(2):
                    if a < 4:
                        r0[a, q, 2 * h + e] = pair[e]
                    elif a == 4:
                        s0[q, 2 * h + e] = pair[e]
                    else:
                        m0[q, 2 * h + e] = pair[e]
    send(1, 2, 3)
    for q in range(4):
        m1[q, 0], m1[q, 1] = widen(*halo, 96 + q, *even)
    m2[0, 0], m2[1, 0] = widen(*halo, 100, *even)
    m3 = widen(*halo, 101, *even)[0]
    for q in range(4):
        for p in range(2):
            s1[q, p] = 0.25 * (
                (s0[2 * q, 2 * p] + s0[2 * q, 2 * p + 1])
                + (s0[2 * q + 1, 2 * p] + s0[2 * q + 1, 2 * p + 1])
            )
    for q in range(2):
        s2[q, 0] = 0.25 * (
            (s1[2 * q, 0] + s1[2 * q, 1]) + (s1[2 * q + 1, 0] + s1[2 * q + 1, 1])
        )
    X, RHS, SOLID, REACT, INV = (x0, x1, x2), (r0, r1, r2), (m0, m1, m2), (s0, s1, s2), (i0, i1, i2)
    M = ((ma0, mb0), (ma1, mb1), (ma2, mb2))
    for level in range(3):
        invert(level, K, REACT[level], INV[level])
    send(4, 7, 8, 9, 12, 13, 14)
    first(0, x0, ma0, r0, m0, i0)
    sweep(0, K, x0, ma0, mb0, r0, m0, i0)
    send(0)
    descend(K, X, M, RHS, SOLID, REACT, INV)
    pack_middle(levels_one_two((x1, r1, s1, m1), (x2, r2, s2, m2)), middle)
    send(15, 5, 6, 10, 11)
    rest = coarse_rhs(K, X, M, RHS, SOLID, REACT, three_rhs)
    s3 = 0.5 * (s2[0, 0, 0:8] + s2[1, 0, 0:8])
    y = exact_dot(jnp.concatenate(rest + [m3[0:8], s3], axis=0), decimate())
    y = [y[8 * n : 8 * n + 8] for n in range(6)]
    for n in range(3):
        tile[n] = half_pair(y[2 * n], y[2 * n + 1])
    for d in range(payload.shape[0]):
        move = pltpu.make_async_copy(tile, payload.at[d], spread_sent.at[d])
        move.start()
        moves.append(move)
    for move in moves:
        move.wait()


def down_two(
    K, x0i, one, two, r0, s0, m0, i0, s1, m1, i1, s2, m2, i2,
    x0, x1, r1, x2, r2, payload,
    ma0, mb0, ma1, mb1, ma2, mb2, three_rhs,
):
    even = is_even("gy")
    for a in range(F):
        for q in range(8):
            for h in range(2):
                halo = [sides(one, two, a * 16 + q * 2 + h, v, even) for v in range(2)]
                for e in range(2):
                    mine = x0i[a, q, 2 * h + e]
                    x0[a, q, 2 * h + e] = jnp.concatenate(
                        [with_sides(mine[8 * v : 8 * v + 8], *halo[v][e]) for v in range(2)],
                        axis=0,
                    )
    X, RHS, SOLID, REACT, INV = (x0, x1, x2), (r0, r1, r2), (m0, m1, m2), (s0, s1, s2), (i0, i1, i2)
    M = ((ma0, mb0), (ma1, mb1), (ma2, mb2))
    mask(0, x0, mb0, m0)
    sweep(0, K, x0, mb0, ma0, r0, m0, i0)
    sweep(0, K, x0, ma0, mb0, r0, m0, i0)
    descend(K, X, M, RHS, SOLID, REACT, INV)
    rest = coarse_rhs(K, X, M, RHS, SOLID, REACT, three_rhs)
    y = exact_dot(jnp.concatenate(rest + rest[0:2], axis=0), decimate())
    y = [y[8 * n : 8 * n + 8] for n in range(4)]
    tiles = [half_pair(y[0], y[1]), half_pair(y[2], y[3])]
    for d in range(payload.shape[0]):
        for n in range(2):
            payload[d, n] = tiles[n]


def solve_coarsest(K, gathered, statics, natural, x, ma, mb, rhs, solid, react, inverse, wide, correct):
    low = lanes((8, 128)) < 64
    top = sublanes((8, 128)) == 0
    bottom = sublanes((8, 128)) == 7
    c = SCALE[3]
    blocks = gathered.shape[0]
    for d in range(blocks):
        natural[0, pl.ds(8 * d, 8), :] = gathered[d, 0]
        natural[1, pl.ds(8 * d, 8), :] = gathered[d, 1]
        natural[2, pl.ds(8 * d, 8), :] = statics[d, 2]
    diagonal = [jnp.where(low, 4.0 * c + K[2 * n, 2 * n], 4.0 * c + K[2 * n + 1, 2 * n + 1]) for n in range(2)]
    weights = [
        (jnp.where(low, K[0, 1], K[1, 0]), jnp.where(low, K[0, 2], K[1, 3]), jnp.where(low, K[0, 3], K[1, 2])),
        (jnp.where(low, K[2, 3], K[3, 2]), jnp.where(low, K[2, 0], K[3, 1]), jnp.where(low, K[2, 1], K[3, 0])),
    ]
    for t in range(blocks):
        pick = pl.ds(t, 8, stride=blocks)
        both = natural[2, pick, :]
        turned = roll(both, 64, 1)
        m = jnp.where(low, both, turned)
        s = jnp.where(low, turned, both)
        solid[t] = m
        react[t] = s
        for n in range(2):
            r = natural[n, pick, :]
            i = OMEGA / (s + diagonal[n])
            rhs[n, t] = r
            inverse[n, t] = i
            x[n, t] = i * r
            ma[n, t + 1] = m * (i * r)

    def ends(masked):
        for n in range(2):
            masked[n, 0] = jnp.where(top, 0.0, roll(masked[n, blocks], 1, 0))
            masked[n, blocks + 1] = jnp.where(bottom, 0.0, roll(masked[n, 1], -1, 0))

    def drives(t, masked):
        weight = c * solid[t]
        xs = [x[0, t], x[1, t]]
        turned = [roll(v, 64, 1) for v in xs]
        out = []
        for n in range(2):
            here = masked[n, t + 1]
            near = (masked[n, t] + masked[n, t + 2]) + (roll(here, 1, 1) + roll(here, -1, 1))
            u, v, w = weights[n]
            mixed = u * turned[n] + v * xs[1 - n] + w * turned[1 - n]
            out.append(rhs[n, t] + weight * near - mixed)
        return out, xs

    ends(ma)
    for index in range(5):
        source, target = (ma, mb) if index % 2 == 0 else (mb, ma)

        def body(t, _):
            out, xs = drives(t, source)
            m = solid[t]
            for n in range(2):
                new = (1.0 - OMEGA) * xs[n] + inverse[n, t] * out[n]
                x[n, t] = new
                target[n, t + 1] = m * new
            return _

        lax.fori_loop(0, blocks, body, 0, unroll=blocks)
        ends(target)

    def gather_sums(t, sums):
        out, xs = drives(t, mb)
        s = react[t]
        sums = list(sums)
        for n in range(2):
            g = s + diagonal[n]
            sums[n] = sums[n] + (out[n] - g * xs[n])
            sums[2 + n] = sums[2 + n] + g
        return tuple(sums)

    zero = jnp.zeros((8, 128), F32)
    sums = lax.fori_loop(0, blocks, gather_sums, (zero,) * 4, unroll=blocks)
    sums = [jnp.sum(v, axis=0, keepdims=True) for v in sums]
    for n in range(2):
        wide[n, pl.ds(0, 8), :] = zero
        wide[n, pl.ds(8 * blocks + 8, 8), :] = zero
        mean = sums[n] / sums[2 + n]
        for t in range(blocks):
            wide[n, pl.ds(8 + t, 8, stride=blocks), :] = x[n, t] + mean
    start = pl.multiple_of(lax.axis_index("gx") * 8, 8)
    low = sublanes((8, 128)) < 4
    height = correct.shape[-2]
    rows = []
    for n in range(2):
        mine = wide[n, pl.ds(start + 8, 8), :]
        after = wide[n, pl.ds(start + 16, 8), :]
        before = wide[n, pl.ds(start, 8), :]
        rows += [mine, after, before] if height == 24 else [mine, jnp.where(low, after, before)]
    rows = jnp.concatenate(rows, axis=0)
    for half in range(2):
        y = exact_dot(rows, spread(half))
        correct[half, 0, 0] = y[0:height]
        correct[2 + half, 0, 0] = y[height : 2 * height]


def ascend(K, X, M, RHS, SOLID, INV, correct, last):
    source = correct
    for level in (2, 1, 0):
        a, b = M[level]
        prolong(level, X[level], a, SOLID[level], source)
        sweep(level, K, X[level], a, b, RHS[level], SOLID[level], INV[level])
        sweep(
            level, K, X[level], b, a, RHS[level], SOLID[level], INV[level],
            last=level > 0 or not last,
        )
        source = X[level]


def copy_state(sources, targets):
    for source, target in zip(sources, targets):
        target[...] = source[...]


def up_one(K, gathered, *refs):
    there = refs[:14]
    x0, one, two = refs[14:17]
    here = (x0,) + refs[17:30]
    x1, r1, s1, m1, i1, x2, r2, s2, m2, i2, ma0, mb0, ma1, mb1, ma2, mb2 = refs[30:46]
    natural, x3, ma3, mb3, r3, m3, s3, i3, wide, correct, arrived = refs[46:]
    moves = [
        pltpu.make_async_copy(there[n], here[n], arrived.at[n]) for n in range(len(there))
    ]
    for move in moves:
        move.start()
    x0, r0, m0, i0, x1s, r1s, s1s, m1s, x2s, r2s, s2s, m2s, near, far = here
    solve_coarsest(K, gathered, gathered, natural, x3, ma3, mb3, r3, m3, s3, i3, wide, correct)
    for move in moves:
        move.wait()
    grow(
        levels_one_two((x1s, r1s, s1s, m1s), (x2s, r2s, s2s, m2s)),
        levels_one_two((x1, r1, s1, m1), (x2, r2, s2, m2)),
        near, far, is_even("gx"),
    )
    invert(1, K, s1, i1)
    invert(2, K, s2, i2)
    M = ((ma0, mb0), (ma1, mb1), (ma2, mb2))
    ascend(K, (x0, x1, x2), M, (r0, r1, r2), (m0, m1, m2), (i0, i1, i2), correct, False)

    def pick(index, v):
        f, q, h = index // 16, index // 2 % 8, index % 2
        part = slice(8 * v, 8 * v + 8)
        return half_pair(x0[f, q, 2 * h, part], x0[f, q, 2 * h + 1, part])

    pack_sides(pick, XTILES, one, two, is_even("gy"))


def up_two(
    K, gathered, statics, x0i, r0, s0, m0, i0, x1i, r1, m1, i1, x2i, r2, m2, i2,
    displacement, residual,
    x0, x1, x2, ma0, mb0, ma1, mb1, ma2, mb2,
    natural, x3, ma3, mb3, r3, m3, s3, i3, wide, correct, stage,
):
    copy_state((x0i, x1i, x2i), (x0, x1, x2))
    solve_coarsest(K, gathered, statics, natural, x3, ma3, mb3, r3, m3, s3, i3, wide, correct)
    M = ((ma0, mb0), (ma1, mb1), (ma2, mb2))
    ascend(K, (x0, x1, x2), M, (r0, r1, r2), (m0, m1, m2), (i0, i1, i2), correct, True)
    mine = slice(0, 8)
    for q in range(8):
        for h in range(2):
            outs = []
            for p in (2 * h, 2 * h + 1):
                drives, xs = drive(0, K, x0, ma0, r0, m0, q, p, mine)
                s = s0[q, p, mine]
                rest = [drives[f] - (s + (4.0 + K[f, f])) * xs[f] for f in range(F)]
                outs.append(xs + rest)
            for a in range(2 * F):
                stage[a, h, pl.ds(q, 8, stride=8), :] = half_pair(outs[0][a], outs[1][a])
    matrix = join_matrix(256, 4)
    for f in range(F):
        for out, a in ((displacement, f), (residual, F + f)):
            out[f] = exact_dot(jnp.concatenate([stage[a, 0], stage[a, 1]], axis=1), matrix)


def sds(*shape):
    return jax.ShapeDtypeStruct(shape, F32)


def field(level, height=16):
    return (F, ROWS[level], COLS[level], height, 128)


def plane(level, height=16):
    return (ROWS[level], COLS[level], height, 128)


def masked_scratch(height=16):
    out = []
    for level in range(3):
        tall = height if level else 16
        shape = (F, ROWS[level] + 2, COLS[level] + 2, tall, 128)
        out += [pltpu.VMEM(shape, F32), pltpu.VMEM(shape, F32)]
    return out


def coarsest_scratch(blocks, height=16):
    return [
        pltpu.VMEM((3, 8 * blocks, 128), F32),
        pltpu.VMEM((2, blocks, 8, 128), F32),
        pltpu.VMEM((2, blocks + 2, 8, 128), F32),
        pltpu.VMEM((2, blocks + 2, 8, 128), F32),
        pltpu.VMEM((2, blocks, 8, 128), F32),
        pltpu.VMEM((blocks, 8, 128), F32),
        pltpu.VMEM((blocks, 8, 128), F32),
        pltpu.VMEM((2, blocks, 8, 128), F32),
        pltpu.VMEM((2, 8 * blocks + 16, 128), F32),
        pltpu.VMEM((F, 1, 1, height, 128), F32),
    ]


def call(body, outs, scratch, args, smem=True, hbm=0):
    specs = [pl.BlockSpec(memory_space=pltpu.VMEM)] * (len(args) - hbm)
    specs += [pl.BlockSpec(memory_space=pltpu.HBM)] * hbm
    if smem:
        specs[0] = pl.BlockSpec(memory_space=pltpu.SMEM)
    args = args[: len(args) - hbm] + tuple(
        pltpu.with_memory_space_constraint(array, pltpu.HBM) for array in args[len(args) - hbm :]
    )
    kept = [isinstance(out, jax.ShapeDtypeStruct) for out in outs]
    return pl.pallas_call(
        body,
        out_shape=outs,
        in_specs=specs,
        out_specs=[
            pl.BlockSpec(memory_space=pltpu.VMEM if inside else pltpu.HBM) for inside in kept
        ],
        scratch_shapes=scratch,
        compiler_params=pltpu.CompilerParams(vmem_limit_bytes=30 * 1024 * 1024),
    )(*args)


def swap(axis, first, second):
    count = lax.axis_size(axis)
    near = [(i, i ^ 1) for i in range(count) if i ^ 1 < count]
    far = [(i, ((i - 1) ^ 1) + 1) for i in range(1, count) if ((i - 1) ^ 1) + 1 < count]
    return lax.ppermute(first, axis, near), lax.ppermute(second, axis, far)


def shards(source, reaction, coupling, solid0, solid1, solid2, solid3):
    blocks = lax.axis_size("gx")
    arrays = (source, reaction, solid0, solid1, solid2, solid3)
    packed = call(
        pack_kernel,
        [sds(TILES, 8, 128), sds(TILES // 2, 8, 128), sds(TILES // 2, 8, 128)],
        [pltpu.VMEM(array.shape, array.dtype) for array in arrays]
        + [
            pltpu.VMEM((6, 2, 64, 128), F32),
            pltpu.VMEM((32, 128), F32),
            pltpu.SemaphoreType.DMA((6,)),
        ],
        arrays,
        smem=False,
        hbm=6,
    )
    own, one, two = packed
    rows = swap("gx", one, two)
    side = call(
        functools.partial(side_kernel, TILES),
        [sds(TILES // 3, 2, 8, 128)] * 2,
        [],
        (own,) + rows,
        smem=False,
    )
    halo = (own,) + rows + swap("gy", *side)
    shapes = []
    for level in range(3):
        shapes += [field(level)] * 2 + [plane(level)] * 2 + [field(level)]
    shapes.append((MIDDLE, 8, 128))
    state = call(
        down_one,
        [pltpu.HBM(shape, F32) for shape in shapes + [(blocks, 3, 8, 128)]],
        [pltpu.VMEM(shape, F32) for shape in shapes]
        + masked_scratch()
        + [
            pltpu.VMEM((F, 1, 1, 16, 128), F32),
            pltpu.VMEM((3, 8, 128), F32),
            pltpu.SemaphoreType.DMA((STATE + 1,)),
            pltpu.SemaphoreType.DMA((blocks,)),
        ],
        (coupling,) + halo,
    )
    x0, r0, s0, m0, i0, x1, r1, s1, m1, i1, x2, r2, s2, m2, i2, middle, payload = state
    near, far = swap("gx", middle, middle)
    statics = lax.all_to_all(payload, "gx", 0, 0)
    inner = [pltpu.VMEM(field(level), F32) for level in range(3)]
    tall = []
    for level in (1, 2):
        tall += [pltpu.VMEM(field(level, 24), F32)] * 2
        tall += [pltpu.VMEM(plane(level, 24), F32)] * 2
        tall += [pltpu.VMEM(field(level, 24), F32)]
    given = (x0, r0, m0, i0, x1, r1, s1, m1, x2, r2, s2, m2, near, far)
    x0, one, two = call(
        up_one,
        [sds(*field(0))] + [sds(-(-XTILES // 3), 2, 8, 128)] * 2,
        [pltpu.VMEM(array.shape, F32) for array in given[1:]]
        + tall
        + masked_scratch(24)
        + coarsest_scratch(blocks, 24)
        + [pltpu.SemaphoreType.DMA((len(given),))],
        (coupling, statics) + given,
        hbm=len(given),
    )
    x0, x1, r1, x2, r2, payload = call(
        down_two,
        [sds(*field(0)), sds(*field(1)), sds(*field(1)), sds(*field(2)), sds(*field(2)),
         sds(blocks, 2, 8, 128)],
        masked_scratch() + [pltpu.VMEM((F, 1, 1, 16, 128), F32)],
        (coupling, x0) + swap("gy", one, two) + (r0, s0, m0, i0, s1, m1, i1, s2, m2, i2),
    )
    gathered = lax.all_to_all(payload, "gx", 0, 0)
    displacement, residual = call(
        up_two,
        [sds(F, 64, 256), sds(F, 64, 256)],
        inner + masked_scratch() + coarsest_scratch(blocks)
        + [pltpu.VMEM((2 * F, 2, 64, 128), F32)],
        (coupling, gathered, statics, x0, r0, s0, m0, i0, x1, r1, m1, i1, x2, r2, m2, i2),
    )
    return displacement, residual


def solution(mesh):
    placed = (
        P(None, "gx", "gy"),
        P("gx", "gy"),
        P(),
        P("gx", "gy"),
        P("gx", "gy"),
        P("gx", "gy"),
        P("gx", "gy"),
    )
    return jax.shard_map(
        shards,
        mesh=mesh,
        in_specs=placed,
        out_specs=(P(None, "gx", "gy"), P(None, "gx", "gy")),
        check_vma=False,
    )
```

```python
import functools

import jax
import jax.numpy as jnp
from jax import lax
from jax.experimental import pallas as pl
from jax.experimental.pallas import tpu as pltpu
from jax.sharding import PartitionSpec as P


F = 4
ROWS = (8, 4, 2)
COLS = (4, 2, 1)
SCALE = (1.0, 0.25, 0.0625, 0.015625)
OMEGA = 0.6
TILES = 102
XTILES = 64
MIDDLE = 30
STATE = 15
GIVEN = 17
KEPT = 11
F32 = jnp.float32
BF16 = jnp.bfloat16


def lanes(shape):
    return lax.broadcasted_iota(jnp.int32, shape, len(shape) - 1)


def sublanes(shape):
    return lax.broadcasted_iota(jnp.int32, shape, len(shape) - 2)


def roll(value, shift, axis):
    size = value.shape[axis]
    shift = shift % size
    return value if shift == 0 else pltpu.roll(value, shift, axis)


def three(value):
    high = value.astype(BF16)
    rest = value - high.astype(F32)
    mid = rest.astype(BF16)
    low = (rest - mid.astype(F32)).astype(BF16)
    return high, mid, low


def exact_dot(value, matrix):
    parts = [jnp.dot(part, matrix, preferred_element_type=F32) for part in three(value)]
    return parts[0] + (parts[1] + parts[2])


def split_matrix(size, stride):
    c = lax.broadcasted_iota(jnp.int32, (size, size), 0)
    o = lax.broadcasted_iota(jnp.int32, (size, size), 1)
    return jnp.where(o == (c % stride) * (size // stride) + c // stride, 1.0, 0.0).astype(BF16)


def join_matrix(size, stride):
    o = lax.broadcasted_iota(jnp.int32, (size, size), 0)
    c = lax.broadcasted_iota(jnp.int32, (size, size), 1)
    return jnp.where(o == (c % stride) * (size // stride) + c // stride, 1.0, 0.0).astype(BF16)


def is_even(axis):
    return lax.broadcast(lax.rem(lax.axis_index(axis), 2), (8, 128)) == 0


def meet(after, before, even):
    return jnp.where(even, after, before), jnp.where(even, before, after)


def pack_rows(own, one, two, count):
    low = sublanes((8, 128)) < 4
    even = is_even("gx")

    def body(n, _):
        a = own[2 * n]
        b = own[2 * n + 1]
        up = jnp.where(low, a, roll(b, 4, 0))
        dn = jnp.where(low, roll(a, 4, 0), b)
        one[n], two[n] = meet(dn, up, even)
        return _

    lax.fori_loop(0, count // 2, body, 0, unroll=3)


def outer_rows(one, two, n, odd, even):
    low = sublanes((8, 128)) < 4
    up, dn = meet(one[n], two[n], even)
    if odd:
        return jnp.where(low, roll(up, 4, 0), dn)
    return jnp.where(low, up, roll(dn, 4, 0))


def pack_kernel(
    source_in, reaction_in, solid0_in, solid1_in, solid2_in, solid3_in, own, one, two,
    source, reaction, solid0, solid1, solid2, solid3, stage, small, arrived,
):
    moves = [
        pltpu.make_async_copy(there, here, arrived.at[n])
        for n, (there, here) in enumerate(
            (
                (source_in, source),
                (reaction_in, reaction),
                (solid0_in, solid0),
                (solid1_in, solid1),
                (solid2_in, solid2),
                (solid3_in, solid3),
            )
        )
    ]
    for move in moves:
        move.start()
    matrix = split_matrix(256, 4)
    for move in moves:
        move.wait()
    for a in range(6):
        if a < 4:
            value = exact_dot(source[a], matrix)
        elif a == 4:
            value = exact_dot(reaction[...], matrix)
        else:
            value = jnp.dot(
                solid0[...].astype(F32).astype(BF16), matrix, preferred_element_type=F32
            )
        for h in range(2):
            stage[a, h] = value[:, 128 * h : 128 * h + 128]
    for a in range(6):
        for q in range(8):
            for h in range(2):
                own[a * 16 + q * 2 + h] = stage[a, h, pl.ds(q, 8, stride=8), :]
    small[...] = jnp.dot(
        solid1[...].astype(F32).astype(BF16),
        split_matrix(128, 2),
        preferred_element_type=F32,
    )
    for q in range(4):
        own[96 + q] = small[pl.ds(q, 8, stride=4), :]
    c = lax.broadcasted_iota(jnp.int32, (64, 128), 0)
    o = lax.broadcasted_iota(jnp.int32, (64, 128), 1)
    wide = jnp.where(o % 64 == c, 1.0, 0.0).astype(BF16)
    small[pl.ds(0, 16), :] = jnp.dot(
        solid2[...].astype(F32).astype(BF16), wide, preferred_element_type=F32
    )
    own[100] = jnp.where(
        lanes((8, 128)) < 64,
        small[pl.ds(0, 8, stride=2), :],
        small[pl.ds(1, 8, stride=2), :],
    )
    c = lax.broadcasted_iota(jnp.int32, (32, 128), 0)
    o = lax.broadcasted_iota(jnp.int32, (32, 128), 1)
    twice = jnp.where((o % 64) // 2 == c, 1.0, 0.0)
    own[101] = jnp.dot(
        solid3[...].astype(F32), twice, preferred_element_type=F32,
        precision=lax.Precision.HIGHEST,
    )
    pack_rows(own, one, two, TILES)


def pack_sides(pick, count, one, two, even):
    lane = lanes((8, 128)) % 64
    for g in range(-(-count // 3)):
        members = min(3, count - 3 * g)
        for v in range(2):
            tiles = [pick(3 * g + t, v) for t in range(members)]
            r, l = tiles[0], tiles[0]
            for t in range(1, members):
                r = jnp.where(lane < 64 - 20 * t, roll(tiles[t], -20 * t, 1), r)
                l = jnp.where(lane >= 20 * t, roll(tiles[t], 20 * t, 1), l)
            one[g, v], two[g, v] = meet(r, l, even)


def side_kernel(count, own, up_one, up_two, one, two):
    even = is_even("gx")

    def pick(index, v):
        if v == 0:
            return own[index]
        return outer_rows(up_one, up_two, index // 2, index % 2, even)

    pack_sides(pick, count, one, two, is_even("gy"))


def sides(one, two, index, v, even):
    g, t = index // 3, index % 3
    l, r = meet(one[g, v], two[g, v], even)
    return [
        (roll(r, 64 + 20 * t + 64 * h, 1), roll(l, 64 - 20 * t + 64 * h, 1)) for h in range(2)
    ]


def with_sides(centre, before, after):
    lane = lanes((8, 128))
    tile = jnp.where(lane < 64, centre, jnp.where(lane < 84, after, 0.0))
    return jnp.where(lane >= 108, before, tile)


def widen(own, row_one, row_two, one, two, index, even_x, even_y):
    out = [[], []]
    for v in range(2):
        if v == 0:
            mine = own[index]
        else:
            mine = outer_rows(row_one, row_two, index // 2, index % 2, even_x)
        halo = sides(one, two, index, v, even_y)
        for h in range(2):
            out[h].append(with_sides(roll(mine, 64 * h, 1), *halo[h]))
    return [jnp.concatenate(pair, axis=0) for pair in out]


def fix_ends(masked, level):
    R, C = ROWS[level], COLS[level]
    for f in range(F):
        for p in range(C):
            masked[f, 0, p + 1] = roll(masked[f, R, p + 1], 1, 0)
            masked[f, R + 1, p + 1] = roll(masked[f, 1, p + 1], -1, 0)
        for q in range(R):
            masked[f, q + 1, 0] = roll(masked[f, q + 1, C], 1, 1)
            masked[f, q + 1, C + 1] = roll(masked[f, q + 1, 1], -1, 1)


def put_masked(masked, level, f, q, p, value):
    masked[f, q + 1, p + 1] = value


def each_row(count, body):
    if count > 4:
        def step(q, _):
            body(q)
            return _

        lax.fori_loop(0, count, step, 0, unroll=count)
    else:
        for q in range(count):
            body(q)


def drive(level, K, x, masked, rhs, solid, q, p, rows=slice(None)):
    xs = [x[f, q, p, rows] for f in range(F)]
    weight = solid[q, p, rows]
    if level:
        weight = weight * SCALE[level]
    out = []
    for f in range(F):
        near = (masked[f, q, p + 1, rows] + masked[f, q + 2, p + 1, rows]) + (
            masked[f, q + 1, p, rows] + masked[f, q + 1, p + 2, rows]
        )
        total = rhs[f, q, p, rows] + weight * near
        mixed = None
        for b in range(F):
            if b != f:
                term = K[f, b] * xs[b]
                mixed = term if mixed is None else mixed + term
        out.append(total - mixed)
    return out, xs


def sweep(level, K, x, masked, target, rhs, solid, inverse, last=False):
    R, C = ROWS[level], COLS[level]

    def body(q):
        news = []
        for p in range(C):
            drives, xs = drive(level, K, x, masked, rhs, solid, q, p)
            news.append(
                [(1.0 - OMEGA) * xs[f] + inverse[f, q, p] * drives[f] for f in range(F)]
            )
        for p in range(C):
            m = None if last else solid[q, p]
            for f in range(F):
                x[f, q, p] = news[p][f]
                if not last:
                    put_masked(target, level, f, q, p, m * news[p][f])

    each_row(R, body)
    if not last:
        fix_ends(target, level)


def first(level, x, masked, rhs, solid, inverse):
    def body(q):
        for p in range(COLS[level]):
            m = solid[q, p]
            for f in range(F):
                new = inverse[f, q, p] * rhs[f, q, p]
                x[f, q, p] = new
                put_masked(masked, level, f, q, p, m * new)

    each_row(ROWS[level], body)
    fix_ends(masked, level)


def mask(level, x, masked, solid):
    def body(q):
        for p in range(COLS[level]):
            m = solid[q, p]
            for f in range(F):
                put_masked(masked, level, f, q, p, m * x[f, q, p])

    each_row(ROWS[level], body)
    fix_ends(masked, level)


def restrict(level, K, x, masked, rhs, solid, react, coarse):
    R, C = ROWS[level], COLS[level]
    wide = 2 if C > 1 else 1

    def body(half):
        for P_ in range(C // wide):
            sums = [None] * F
            for dq in range(2):
                for dp in range(wide):
                    q, p = 2 * half + dq, wide * P_ + dp
                    drives, xs = drive(level, K, x, masked, rhs, solid, q, p)
                    s = react[q, p]
                    for f in range(F):
                        e = drives[f] - (s + (4.0 * SCALE[level] + K[f, f])) * xs[f]
                        sums[f] = e if sums[f] is None else sums[f] + e
            for f in range(F):
                coarse[f, half, P_] = sums[f] * (0.5 / wide)

    each_row(R // 2, body)


def near_rows(value):
    outer = jnp.where(sublanes((8, 128)) < 4, value[8:16], value[16:24])
    return jnp.concatenate([value[0:8], outer], axis=0)


def prolong(level, x, masked, solid, source):
    def body(half):
        for dq in range(2):
            q = 2 * half + dq
            for p in range(COLS[level]):
                m = solid[q, p]
                for f in range(F):
                    fix = source[f, half, p // 2]
                    if fix.shape[0] == 24 and m.shape[0] == 16:
                        fix = near_rows(fix)
                    new = x[f, q, p] + fix
                    x[f, q, p] = new
                    put_masked(masked, level, f, q, p, m * new)

    each_row(ROWS[level] // 2, body)
    fix_ends(masked, level)


def invert(level, K, react, inverse):
    def body(q):
        for p in range(COLS[level]):
            s = react[q, p]
            for f in range(F):
                inverse[f, q, p] = OMEGA / (s + (4.0 * SCALE[level] + K[f, f]))

    each_row(ROWS[level], body)


def decimate():
    k = lax.broadcasted_iota(jnp.int32, (128, 128), 0)
    o = lax.broadcasted_iota(jnp.int32, (128, 128), 1)
    return jnp.where(o == (k // 2 + 10) % 64, 0.5, 0.0).astype(BF16)


def spread(half):
    o = lax.broadcasted_iota(jnp.int32, (128, 128), 0)
    k = lax.broadcasted_iota(jnp.int32, (128, 128), 1)
    return jnp.where(o == (k // 2 + 10) % 64 + 64 * half, 1.0, 0.0).astype(BF16)


def half_pair(a, b):
    return jnp.where(lanes((8, 128)) < 64, a, roll(b, 64, 1))


def descend(K, X, M, RHS, SOLID, REACT, INV):
    for level in range(3):
        a, b = M[level]
        if level:
            first(level, X[level], a, RHS[level], SOLID[level], INV[level])
            sweep(level, K, X[level], a, b, RHS[level], SOLID[level], INV[level])
        if level < 2:
            restrict(
                level, K, X[level], b, RHS[level], SOLID[level], REACT[level], RHS[level + 1]
            )


def coarse_rhs(K, X, M, RHS, SOLID, REACT, three_rhs):
    restrict(2, K, X[2], M[2][1], RHS[2], SOLID[2], REACT[2], three_rhs)
    return [three_rhs[f, 0, 0, 0:8] for f in range(F)]


def levels_one_two(state_one, state_two):
    out = []
    for level, (x, r, s, m) in ((1, state_one), (2, state_two)):
        keys = []
        for q in range(ROWS[level]):
            for p in range(COLS[level]):
                for f in range(F):
                    keys.append((x, (f, q, p)))
                    keys.append((r, (f, q, p)))
                keys.append((s, (q, p)))
                keys.append((m, (q, p)))
        out.append(keys)
    return out


TAKE = ((3, 2), (2, 4))


def pack_middle(keys, middle):
    sub = sublanes((8, 128))
    place = 0
    for (start, size), members in zip(TAKE, keys):
        each = 8 // size
        for g in range(0, len(members), each):
            tile = None
            for u in range(each):
                ref, index = members[g + u]
                part = roll(ref[index][0:8], size * u - start, 0)
                tile = part if tile is None else jnp.where(sub >= size * u, part, tile)
            middle[place] = tile
            place += 1


def grow(keys, tall_keys, near, far, even):
    sub = sublanes((8, 128))
    place = 0
    for (start, size), members, targets in zip(TAKE, keys, tall_keys):
        each = 8 // size
        for g in range(0, len(members), each):
            after, before = meet(near[place], far[place], even)
            for u in range(each):
                ref, index = members[g + u]
                tile = ref[index]
                inner, outer = tile[0:8], tile[8:16]
                later = roll(after, start - size * u, 0)
                sooner = roll(before, start - size * u, 0)
                later = jnp.where(sub < start, outer, jnp.where(sub < start + size, later, 0.0))
                sooner = jnp.where(
                    sub >= start + size, outer, jnp.where(sub >= start, sooner, 0.0)
                )
                target, index = targets[g + u]
                target[index] = jnp.concatenate([inner, later, sooner], axis=0)
            place += 1


def down_one(K, own, row_one, row_two, one, two, *refs):
    there, payload = refs[: STATE + 1], refs[STATE + 1]
    here = refs[STATE + 2 : 2 * STATE + 3]
    ma0, mb0, ma1, mb1, ma2, mb2, three_rhs, spread_out, sent, spread_sent = refs[2 * STATE + 3 :]
    x0, r0, s0, m0, i0, x1, r1, s1, m1, i1, x2, r2, s2, m2, i2, middle = here
    moves = []

    def send(*which):
        for n in which:
            move = pltpu.make_async_copy(here[n], there[n], sent.at[n])
            move.start()
            moves.append(move)

    halo = (own, row_one, row_two, one, two)
    even = (is_even("gx"), is_even("gy"))
    for a in range(6):
        for q in range(8):
            for h in range(2):
                pair = widen(*halo, a * 16 + q * 2 + h, *even)
                for e in range(2):
                    if a < 4:
                        r0[a, q, 2 * h + e] = pair[e]
                    elif a == 4:
                        s0[q, 2 * h + e] = pair[e]
                    else:
                        m0[q, 2 * h + e] = pair[e]
    send(1, 2, 3)
    for q in range(4):
        m1[q, 0], m1[q, 1] = widen(*halo, 96 + q, *even)
    m2[0, 0], m2[1, 0] = widen(*halo, 100, *even)
    m3 = widen(*halo, 101, *even)[0]
    for q in range(4):
        for p in range(2):
            s1[q, p] = 0.25 * (
                (s0[2 * q, 2 * p] + s0[2 * q, 2 * p + 1])
                + (s0[2 * q + 1, 2 * p] + s0[2 * q + 1, 2 * p + 1])
            )
    for q in range(2):
        s2[q, 0] = 0.25 * (
            (s1[2 * q, 0] + s1[2 * q, 1]) + (s1[2 * q + 1, 0] + s1[2 * q + 1, 1])
        )
    X, RHS, SOLID, REACT, INV = (x0, x1, x2), (r0, r1, r2), (m0, m1, m2), (s0, s1, s2), (i0, i1, i2)
    M = ((ma0, mb0), (ma1, mb1), (ma2, mb2))
    for level in range(3):
        invert(level, K, REACT[level], INV[level])
    send(4, 7, 8, 9, 12, 13, 14)
    first(0, x0, ma0, r0, m0, i0)
    sweep(0, K, x0, ma0, mb0, r0, m0, i0)
    send(0)
    descend(K, X, M, RHS, SOLID, REACT, INV)
    pack_middle(levels_one_two((x1, r1, s1, m1), (x2, r2, s2, m2)), middle)
    send(15, 5, 6, 10, 11)
    rest = coarse_rhs(K, X, M, RHS, SOLID, REACT, three_rhs)
    s3 = 0.5 * (s2[0, 0, 0:8] + s2[1, 0, 0:8])
    y = exact_dot(jnp.concatenate(rest + [m3[0:8], s3], axis=0), decimate())
    y = [y[8 * n : 8 * n + 8] for n in range(6)]
    tiles = [half_pair(y[2 * n], y[2 * n + 1]) for n in range(3)]
    for d in range(payload.shape[0]):
        for n in range(3):
            spread_out[d, n] = tiles[n]
    move = pltpu.make_async_copy(spread_out, payload, spread_sent)
    move.start()
    moves.append(move)
    for move in moves:
        move.wait()


def down_two(
    K, x0i, one, two, r0, s0, m0, i0, s1, m1, i1, s2, m2, i2,
    x0, x1, r1, x2, r2, payload,
    ma0, mb0, ma1, mb1, ma2, mb2, three_rhs,
):
    even = is_even("gy")
    for a in range(F):
        for q in range(8):
            for h in range(2):
                halo = [sides(one, two, a * 16 + q * 2 + h, v, even) for v in range(2)]
                for e in range(2):
                    mine = x0i[a, q, 2 * h + e]
                    x0[a, q, 2 * h + e] = jnp.concatenate(
                        [with_sides(mine[8 * v : 8 * v + 8], *halo[v][e]) for v in range(2)],
                        axis=0,
                    )
    X, RHS, SOLID, REACT, INV = (x0, x1, x2), (r0, r1, r2), (m0, m1, m2), (s0, s1, s2), (i0, i1, i2)
    M = ((ma0, mb0), (ma1, mb1), (ma2, mb2))
    mask(0, x0, mb0, m0)
    sweep(0, K, x0, mb0, ma0, r0, m0, i0)
    sweep(0, K, x0, ma0, mb0, r0, m0, i0)
    descend(K, X, M, RHS, SOLID, REACT, INV)
    rest = coarse_rhs(K, X, M, RHS, SOLID, REACT, three_rhs)
    y = exact_dot(jnp.concatenate(rest + rest[0:2], axis=0), decimate())
    y = [y[8 * n : 8 * n + 8] for n in range(4)]
    tiles = [half_pair(y[0], y[1]), half_pair(y[2], y[3])]
    for d in range(payload.shape[0]):
        for n in range(2):
            payload[d, n] = tiles[n]


def solve_coarsest(K, gathered, statics, natural, x, ma, mb, rhs, solid, react, inverse, wide, correct):
    low = lanes((8, 128)) < 64
    top = sublanes((8, 128)) == 0
    bottom = sublanes((8, 128)) == 7
    c = SCALE[3]
    blocks = gathered.shape[0]
    for d in range(blocks):
        natural[0, pl.ds(8 * d, 8), :] = gathered[d, 0]
        natural[1, pl.ds(8 * d, 8), :] = gathered[d, 1]
        natural[2, pl.ds(8 * d, 8), :] = statics[d, 2]
    diagonal = [jnp.where(low, 4.0 * c + K[2 * n, 2 * n], 4.0 * c + K[2 * n + 1, 2 * n + 1]) for n in range(2)]
    weights = [
        (jnp.where(low, K[0, 1], K[1, 0]), jnp.where(low, K[0, 2], K[1, 3]), jnp.where(low, K[0, 3], K[1, 2])),
        (jnp.where(low, K[2, 3], K[3, 2]), jnp.where(low, K[2, 0], K[3, 1]), jnp.where(low, K[2, 1], K[3, 0])),
    ]
    for t in range(blocks):
        pick = pl.ds(t, 8, stride=blocks)
        both = natural[2, pick, :]
        turned = roll(both, 64, 1)
        m = jnp.where(low, both, turned)
        s = jnp.where(low, turned, both)
        solid[t] = m
        react[t] = s
        for n in range(2):
            r = natural[n, pick, :]
            i = OMEGA / (s + diagonal[n])
            rhs[n, t] = r
            inverse[n, t] = i
            x[n, t] = i * r
            ma[n, t + 1] = m * (i * r)

    def ends(masked):
        for n in range(2):
            masked[n, 0] = jnp.where(top, 0.0, roll(masked[n, blocks], 1, 0))
            masked[n, blocks + 1] = jnp.where(bottom, 0.0, roll(masked[n, 1], -1, 0))

    def drives(t, masked):
        weight = c * solid[t]
        xs = [x[0, t], x[1, t]]
        turned = [roll(v, 64, 1) for v in xs]
        out = []
        for n in range(2):
            here = masked[n, t + 1]
            near = (masked[n, t] + masked[n, t + 2]) + (roll(here, 1, 1) + roll(here, -1, 1))
            u, v, w = weights[n]
            mixed = u * turned[n] + v * xs[1 - n] + w * turned[1 - n]
            out.append(rhs[n, t] + weight * near - mixed)
        return out, xs

    ends(ma)
    for index in range(5):
        source, target = (ma, mb) if index % 2 == 0 else (mb, ma)

        def body(t, _):
            out, xs = drives(t, source)
            m = solid[t]
            for n in range(2):
                new = (1.0 - OMEGA) * xs[n] + inverse[n, t] * out[n]
                x[n, t] = new
                target[n, t + 1] = m * new
            return _

        lax.fori_loop(0, blocks, body, 0, unroll=blocks)
        ends(target)

    def gather_sums(t, sums):
        out, xs = drives(t, mb)
        s = react[t]
        sums = list(sums)
        for n in range(2):
            g = s + diagonal[n]
            sums[n] = sums[n] + (out[n] - g * xs[n])
            sums[2 + n] = sums[2 + n] + g
        return tuple(sums)

    zero = jnp.zeros((8, 128), F32)
    sums = lax.fori_loop(0, blocks, gather_sums, (zero,) * 4, unroll=blocks)
    sums = [jnp.sum(v, axis=0, keepdims=True) for v in sums]
    for n in range(2):
        wide[n, pl.ds(0, 8), :] = zero
        wide[n, pl.ds(8 * blocks + 8, 8), :] = zero
        mean = sums[n] / sums[2 + n]
        for t in range(blocks):
            wide[n, pl.ds(8 + t, 8, stride=blocks), :] = x[n, t] + mean
    start = pl.multiple_of(lax.axis_index("gx") * 8, 8)
    low = sublanes((8, 128)) < 4
    height = correct.shape[-2]
    rows = []
    for n in range(2):
        mine = wide[n, pl.ds(start + 8, 8), :]
        after = wide[n, pl.ds(start + 16, 8), :]
        before = wide[n, pl.ds(start, 8), :]
        rows += [mine, after, before] if height == 24 else [mine, jnp.where(low, after, before)]
    rows = jnp.concatenate(rows, axis=0)
    for half in range(2):
        y = exact_dot(rows, spread(half))
        correct[half, 0, 0] = y[0:height]
        correct[2 + half, 0, 0] = y[height : 2 * height]


def rise(level, K, X, M, RHS, SOLID, INV, source, last):
    a, b = M[level]
    prolong(level, X[level], a, SOLID[level], source)
    sweep(level, K, X[level], a, b, RHS[level], SOLID[level], INV[level])
    sweep(level, K, X[level], b, a, RHS[level], SOLID[level], INV[level], last=last)
    return X[level]


def ascend(K, X, M, RHS, SOLID, INV, correct):
    source = correct
    for level in (2, 1, 0):
        source = rise(level, K, X, M, RHS, SOLID, INV, source, level > 0)


def copy_state(sources, targets):
    for source, target in zip(sources, targets):
        target[...] = source[...]


def up_one(K, gathered, *refs):
    there, refs = refs[:GIVEN], refs[GIVEN:]
    kept, one, two = refs[:KEPT], refs[KEPT], refs[KEPT + 1]
    refs = refs[KEPT + 2 :]
    here, refs = kept + refs[: GIVEN - KEPT], refs[GIVEN - KEPT :]
    x1, r1, s1, m1, i1, x2, r2, s2, m2, i2, ma0, mb0, ma1, mb1, ma2, mb2 = refs[:16]
    natural, x3, ma3, mb3, r3, m3, s3, i3, wide, correct, arrived = refs[16:]
    moves = [
        pltpu.make_async_copy(there[n], here[n], arrived.at[n]) for n in range(GIVEN)
    ]
    for move in moves[::-1]:
        move.start()
    r0, m0, i0, s0, x0, i1s, i2s, s1s, m1s, s2s, m2s, x1s, r1s, x2s, r2s, near, far = here
    solve_coarsest(K, gathered, gathered, natural, x3, ma3, mb3, r3, m3, s3, i3, wide, correct)
    for move in moves[5:]:
        move.wait()
    grow(
        levels_one_two((x1s, r1s, s1s, m1s), (x2s, r2s, s2s, m2s)),
        levels_one_two((x1, r1, s1, m1), (x2, r2, s2, m2)),
        near, far, is_even("gx"),
    )
    invert(1, K, s1, i1)
    invert(2, K, s2, i2)
    M = ((ma0, mb0), (ma1, mb1), (ma2, mb2))
    X, RHS, SOLID, INV = (x0, x1, x2), (r0, r1, r2), (m0, m1, m2), (i0, i1, i2)
    source = rise(2, K, X, M, RHS, SOLID, INV, correct, True)
    source = rise(1, K, X, M, RHS, SOLID, INV, source, True)
    for move in moves[:5]:
        move.wait()
    rise(0, K, X, M, RHS, SOLID, INV, source, True)

    def pick(index, v):
        f, q, h = index // 16, index // 2 % 8, index % 2
        part = slice(8 * v, 8 * v + 8)
        return half_pair(x0[f, q, 2 * h, part], x0[f, q, 2 * h + 1, part])

    pack_sides(pick, XTILES, one, two, is_even("gy"))


def up_two(
    K, gathered, statics, x0i, r0, s0, m0, i0, x1i, r1, m1, i1, x2i, r2, m2, i2,
    displacement, residual,
    x0, x1, x2, ma0, mb0, ma1, mb1, ma2, mb2,
    natural, x3, ma3, mb3, r3, m3, s3, i3, wide, correct, stage,
):
    copy_state((x0i, x1i, x2i), (x0, x1, x2))
    solve_coarsest(K, gathered, statics, natural, x3, ma3, mb3, r3, m3, s3, i3, wide, correct)
    M = ((ma0, mb0), (ma1, mb1), (ma2, mb2))
    ascend(K, (x0, x1, x2), M, (r0, r1, r2), (m0, m1, m2), (i0, i1, i2), correct)
    mine = slice(0, 8)
    for q in range(8):
        for h in range(2):
            outs = []
            for p in (2 * h, 2 * h + 1):
                drives, xs = drive(0, K, x0, ma0, r0, m0, q, p, mine)
                s = s0[q, p, mine]
                rest = [drives[f] - (s + (4.0 + K[f, f])) * xs[f] for f in range(F)]
                outs.append(xs + rest)
            for a in range(2 * F):
                stage[a, h, pl.ds(q, 8, stride=8), :] = half_pair(outs[0][a], outs[1][a])
    matrix = join_matrix(256, 4)
    for f in range(F):
        for out, a in ((displacement, f), (residual, F + f)):
            out[f] = exact_dot(jnp.concatenate([stage[a, 0], stage[a, 1]], axis=1), matrix)


def sds(*shape):
    return jax.ShapeDtypeStruct(shape, F32)


def field(level, height=16):
    return (F, ROWS[level], COLS[level], height, 128)


def plane(level, height=16):
    return (ROWS[level], COLS[level], height, 128)


def masked_scratch(height=16):
    out = []
    for level in range(3):
        tall = height if level else 16
        shape = (F, ROWS[level] + 2, COLS[level] + 2, tall, 128)
        out += [pltpu.VMEM(shape, F32), pltpu.VMEM(shape, F32)]
    return out


def coarsest_scratch(blocks, height=16):
    return [
        pltpu.VMEM((3, 8 * blocks, 128), F32),
        pltpu.VMEM((2, blocks, 8, 128), F32),
        pltpu.VMEM((2, blocks + 2, 8, 128), F32),
        pltpu.VMEM((2, blocks + 2, 8, 128), F32),
        pltpu.VMEM((2, blocks, 8, 128), F32),
        pltpu.VMEM((blocks, 8, 128), F32),
        pltpu.VMEM((blocks, 8, 128), F32),
        pltpu.VMEM((2, blocks, 8, 128), F32),
        pltpu.VMEM((2, 8 * blocks + 16, 128), F32),
        pltpu.VMEM((F, 1, 1, height, 128), F32),
    ]


def call(body, outs, scratch, args, smem=True, hbm=0):
    specs = [pl.BlockSpec(memory_space=pltpu.VMEM)] * (len(args) - hbm)
    specs += [pl.BlockSpec(memory_space=pltpu.HBM)] * hbm
    if smem:
        specs[0] = pl.BlockSpec(memory_space=pltpu.SMEM)
    args = args[: len(args) - hbm] + tuple(
        pltpu.with_memory_space_constraint(array, pltpu.HBM) for array in args[len(args) - hbm :]
    )
    kept = [isinstance(out, jax.ShapeDtypeStruct) for out in outs]
    return pl.pallas_call(
        body,
        out_shape=outs,
        in_specs=specs,
        out_specs=[
            pl.BlockSpec(memory_space=pltpu.VMEM if inside else pltpu.HBM) for inside in kept
        ],
        scratch_shapes=scratch,
        compiler_params=pltpu.CompilerParams(vmem_limit_bytes=30 * 1024 * 1024),
    )(*args)


def swap(axis, first, second):
    count = lax.axis_size(axis)
    near = [(i, i ^ 1) for i in range(count) if i ^ 1 < count]
    far = [(i, ((i - 1) ^ 1) + 1) for i in range(1, count) if ((i - 1) ^ 1) + 1 < count]
    return lax.ppermute(first, axis, near), lax.ppermute(second, axis, far)


def shards(source, reaction, coupling, solid0, solid1, solid2, solid3):
    blocks = lax.axis_size("gx")
    arrays = (source, reaction, solid0, solid1, solid2, solid3)
    packed = call(
        pack_kernel,
        [sds(TILES, 8, 128), sds(TILES // 2, 8, 128), sds(TILES // 2, 8, 128)],
        [pltpu.VMEM(array.shape, array.dtype) for array in arrays]
        + [
            pltpu.VMEM((6, 2, 64, 128), F32),
            pltpu.VMEM((32, 128), F32),
            pltpu.SemaphoreType.DMA((6,)),
        ],
        arrays,
        smem=False,
        hbm=6,
    )
    own, one, two = packed
    rows = swap("gx", one, two)
    side = call(
        functools.partial(side_kernel, TILES),
        [sds(TILES // 3, 2, 8, 128)] * 2,
        [],
        (own,) + rows,
        smem=False,
    )
    halo = (own,) + rows + swap("gy", *side)
    shapes = []
    for level in range(3):
        shapes += [field(level)] * 2 + [plane(level)] * 2 + [field(level)]
    shapes.append((MIDDLE, 8, 128))
    state = call(
        down_one,
        [pltpu.HBM(shape, F32) for shape in shapes + [(blocks, 3, 8, 128)]],
        [pltpu.VMEM(shape, F32) for shape in shapes]
        + masked_scratch()
        + [
            pltpu.VMEM((F, 1, 1, 16, 128), F32),
            pltpu.VMEM((blocks, 3, 8, 128), F32),
            pltpu.SemaphoreType.DMA((STATE + 1,)),
            pltpu.SemaphoreType.DMA,
        ],
        (coupling,) + halo,
    )
    x0, r0, s0, m0, i0, x1, r1, s1, m1, i1, x2, r2, s2, m2, i2, middle, payload = state
    near, far = swap("gx", middle, middle)
    statics = lax.all_to_all(payload, "gx", 0, 0)
    inner = [pltpu.VMEM(field(level), F32) for level in range(3)]
    tall = []
    for level in (1, 2):
        tall += [pltpu.VMEM(field(level, 24), F32)] * 2
        tall += [pltpu.VMEM(plane(level, 24), F32)] * 2
        tall += [pltpu.VMEM(field(level, 24), F32)]
    given = (r0, m0, i0, s0, x0, i1, i2, s1, m1, s2, m2, x1, r1, x2, r2, near, far)
    r0, m0, i0, s0, x0, i1, i2, s1, m1, s2, m2, one, two = call(
        up_one,
        [sds(*array.shape) for array in given[:KEPT]]
        + [sds(-(-XTILES // 3), 2, 8, 128)] * 2,
        [pltpu.VMEM(array.shape, F32) for array in given[KEPT:]]
        + tall
        + masked_scratch(24)
        + coarsest_scratch(blocks, 24)
        + [pltpu.SemaphoreType.DMA((GIVEN,))],
        (coupling, statics) + given,
        hbm=GIVEN,
    )
    x0, x1, r1, x2, r2, payload = call(
        down_two,
        [sds(*field(0)), sds(*field(1)), sds(*field(1)), sds(*field(2)), sds(*field(2)),
         sds(blocks, 2, 8, 128)],
        masked_scratch() + [pltpu.VMEM((F, 1, 1, 16, 128), F32)],
        (coupling, x0) + swap("gy", one, two) + (r0, s0, m0, i0, s1, m1, i1, s2, m2, i2),
    )
    gathered = lax.all_to_all(payload, "gx", 0, 0)
    displacement, residual = call(
        up_two,
        [sds(F, 64, 256), sds(F, 64, 256)],
        inner + masked_scratch() + coarsest_scratch(blocks)
        + [pltpu.VMEM((2 * F, 2, 64, 128), F32)],
        (coupling, gathered, statics, x0, r0, s0, m0, i0, x1, r1, m1, i1, x2, r2, m2, i2),
    )
    return displacement, residual


def solution(mesh):
    placed = (
        P(None, "gx", "gy"),
        P("gx", "gy"),
        P(),
        P("gx", "gy"),
        P("gx", "gy"),
        P("gx", "gy"),
        P("gx", "gy"),
    )
    return jax.shard_map(
        shards,
        mesh=mesh,
        in_specs=placed,
        out_specs=(P(None, "gx", "gy"), P(None, "gx", "gy")),
        check_vma=False,
    )
```

```python
import functools

import jax
import jax.numpy as jnp
from jax import lax
from jax.experimental import pallas as pl
from jax.experimental.pallas import tpu as pltpu
from jax.sharding import PartitionSpec as P


F = 4
ROWS = (8, 4, 2)
COLS = (4, 2, 1)
SCALE = (1.0, 0.25, 0.0625, 0.015625)
OMEGA = 0.6
TILES = 102
XTILES = 64
MIDDLE = 30
STATE = 12
GIVEN = 14
KEPT = 8
F32 = jnp.float32
BF16 = jnp.bfloat16


def lanes(shape):
    return lax.broadcasted_iota(jnp.int32, shape, len(shape) - 1)


def sublanes(shape):
    return lax.broadcasted_iota(jnp.int32, shape, len(shape) - 2)


def roll(value, shift, axis):
    size = value.shape[axis]
    shift = shift % size
    return value if shift == 0 else pltpu.roll(value, shift, axis)


def three(value):
    high = value.astype(BF16)
    rest = value - high.astype(F32)
    mid = rest.astype(BF16)
    low = (rest - mid.astype(F32)).astype(BF16)
    return high, mid, low


def exact_dot(value, matrix):
    parts = [jnp.dot(part, matrix, preferred_element_type=F32) for part in three(value)]
    return parts[0] + (parts[1] + parts[2])


def split_matrix(size, stride):
    c = lax.broadcasted_iota(jnp.int32, (size, size), 0)
    o = lax.broadcasted_iota(jnp.int32, (size, size), 1)
    return jnp.where(o == (c % stride) * (size // stride) + c // stride, 1.0, 0.0).astype(BF16)


def join_matrix(size, stride):
    o = lax.broadcasted_iota(jnp.int32, (size, size), 0)
    c = lax.broadcasted_iota(jnp.int32, (size, size), 1)
    return jnp.where(o == (c % stride) * (size // stride) + c // stride, 1.0, 0.0).astype(BF16)


def is_even(axis):
    return lax.broadcast(lax.rem(lax.axis_index(axis), 2), (8, 128)) == 0


def meet(after, before, even):
    return jnp.where(even, after, before), jnp.where(even, before, after)


def pack_rows(own, one, two, count):
    low = sublanes((8, 128)) < 4
    even = is_even("gx")

    def body(n, _):
        a = own[2 * n]
        b = own[2 * n + 1]
        up = jnp.where(low, a, roll(b, 4, 0))
        dn = jnp.where(low, roll(a, 4, 0), b)
        one[n], two[n] = meet(dn, up, even)
        return _

    lax.fori_loop(0, count // 2, body, 0, unroll=3)


def outer_rows(one, two, n, odd, even):
    low = sublanes((8, 128)) < 4
    up, dn = meet(one[n], two[n], even)
    if odd:
        return jnp.where(low, roll(up, 4, 0), dn)
    return jnp.where(low, up, roll(dn, 4, 0))


def pack_kernel(
    source_in, reaction_in, solid0_in, solid1_in, solid2_in, solid3_in, own, one, two,
    source, reaction, solid0, solid1, solid2, solid3, stage, small, arrived,
):
    moves = [
        pltpu.make_async_copy(there, here, arrived.at[n])
        for n, (there, here) in enumerate(
            (
                (source_in, source),
                (reaction_in, reaction),
                (solid0_in, solid0),
                (solid1_in, solid1),
                (solid2_in, solid2),
                (solid3_in, solid3),
            )
        )
    ]
    for move in moves:
        move.start()
    matrix = split_matrix(256, 4)
    for move in moves:
        move.wait()
    for a in range(6):
        if a < 4:
            value = exact_dot(source[a], matrix)
        elif a == 4:
            value = exact_dot(reaction[...], matrix)
        else:
            value = jnp.dot(
                solid0[...].astype(F32).astype(BF16), matrix, preferred_element_type=F32
            )
        for h in range(2):
            stage[a, h] = value[:, 128 * h : 128 * h + 128]
    for a in range(6):
        for q in range(8):
            for h in range(2):
                own[a * 16 + q * 2 + h] = stage[a, h, pl.ds(q, 8, stride=8), :]
    small[...] = jnp.dot(
        solid1[...].astype(F32).astype(BF16),
        split_matrix(128, 2),
        preferred_element_type=F32,
    )
    for q in range(4):
        own[96 + q] = small[pl.ds(q, 8, stride=4), :]
    c = lax.broadcasted_iota(jnp.int32, (64, 128), 0)
    o = lax.broadcasted_iota(jnp.int32, (64, 128), 1)
    wide = jnp.where(o % 64 == c, 1.0, 0.0).astype(BF16)
    small[pl.ds(0, 16), :] = jnp.dot(
        solid2[...].astype(F32).astype(BF16), wide, preferred_element_type=F32
    )
    own[100] = jnp.where(
        lanes((8, 128)) < 64,
        small[pl.ds(0, 8, stride=2), :],
        small[pl.ds(1, 8, stride=2), :],
    )
    c = lax.broadcasted_iota(jnp.int32, (32, 128), 0)
    o = lax.broadcasted_iota(jnp.int32, (32, 128), 1)
    twice = jnp.where((o % 64) // 2 == c, 1.0, 0.0)
    own[101] = jnp.dot(
        solid3[...].astype(F32), twice, preferred_element_type=F32,
        precision=lax.Precision.HIGHEST,
    )
    pack_rows(own, one, two, TILES)


def pack_sides(pick, count, one, two, even):
    lane = lanes((8, 128)) % 64
    for g in range(-(-count // 3)):
        members = min(3, count - 3 * g)
        for v in range(2):
            tiles = [pick(3 * g + t, v) for t in range(members)]
            r, l = tiles[0], tiles[0]
            for t in range(1, members):
                r = jnp.where(lane < 64 - 20 * t, roll(tiles[t], -20 * t, 1), r)
                l = jnp.where(lane >= 20 * t, roll(tiles[t], 20 * t, 1), l)
            one[g, v], two[g, v] = meet(r, l, even)


def side_kernel(count, own, up_one, up_two, one, two):
    even = is_even("gx")

    def pick(index, v):
        if v == 0:
            return own[index]
        return outer_rows(up_one, up_two, index // 2, index % 2, even)

    pack_sides(pick, count, one, two, is_even("gy"))


def sides(one, two, index, v, even):
    g, t = index // 3, index % 3
    l, r = meet(one[g, v], two[g, v], even)
    return [
        (roll(r, 64 + 20 * t + 64 * h, 1), roll(l, 64 - 20 * t + 64 * h, 1)) for h in range(2)
    ]


def with_sides(centre, before, after):
    lane = lanes((8, 128))
    tile = jnp.where(lane < 64, centre, jnp.where(lane < 84, after, 0.0))
    return jnp.where(lane >= 108, before, tile)


def widen(own, row_one, row_two, one, two, index, even_x, even_y):
    out = [[], []]
    for v in range(2):
        if v == 0:
            mine = own[index]
        else:
            mine = outer_rows(row_one, row_two, index // 2, index % 2, even_x)
        halo = sides(one, two, index, v, even_y)
        for h in range(2):
            out[h].append(with_sides(roll(mine, 64 * h, 1), *halo[h]))
    return [jnp.concatenate(pair, axis=0) for pair in out]


def fix_ends(masked, level):
    R, C = ROWS[level], COLS[level]
    for f in range(F):
        for p in range(C):
            masked[f, 0, p + 1] = roll(masked[f, R, p + 1], 1, 0)
            masked[f, R + 1, p + 1] = roll(masked[f, 1, p + 1], -1, 0)
        for q in range(R):
            masked[f, q + 1, 0] = roll(masked[f, q + 1, C], 1, 1)
            masked[f, q + 1, C + 1] = roll(masked[f, q + 1, 1], -1, 1)


def put_masked(masked, level, f, q, p, value):
    masked[f, q + 1, p + 1] = value


def each_row(count, body):
    if count > 4:
        def step(q, _):
            body(q)
            return _

        lax.fori_loop(0, count, step, 0, unroll=count)
    else:
        for q in range(count):
            body(q)


def drive(level, K, x, masked, rhs, solid, q, p, rows=slice(None)):
    xs = [x[f, q, p, rows] for f in range(F)]
    weight = solid[q, p, rows]
    if level:
        weight = weight * SCALE[level]
    out = []
    for f in range(F):
        near = (masked[f, q, p + 1, rows] + masked[f, q + 2, p + 1, rows]) + (
            masked[f, q + 1, p, rows] + masked[f, q + 1, p + 2, rows]
        )
        total = rhs[f, q, p, rows] + weight * near
        mixed = None
        for b in range(F):
            if b != f:
                term = K[f, b] * xs[b]
                mixed = term if mixed is None else mixed + term
        out.append(total - mixed)
    return out, xs


def sweep(level, K, x, masked, target, rhs, solid, inverse, last=False):
    R, C = ROWS[level], COLS[level]

    def body(q):
        news = []
        for p in range(C):
            drives, xs = drive(level, K, x, masked, rhs, solid, q, p)
            news.append(
                [(1.0 - OMEGA) * xs[f] + inverse[f, q, p] * drives[f] for f in range(F)]
            )
        for p in range(C):
            m = None if last else solid[q, p]
            for f in range(F):
                x[f, q, p] = news[p][f]
                if not last:
                    put_masked(target, level, f, q, p, m * news[p][f])

    each_row(R, body)
    if not last:
        fix_ends(target, level)


def first(level, x, masked, rhs, solid, inverse):
    def body(q):
        for p in range(COLS[level]):
            m = solid[q, p]
            for f in range(F):
                new = inverse[f, q, p] * rhs[f, q, p]
                x[f, q, p] = new
                put_masked(masked, level, f, q, p, m * new)

    each_row(ROWS[level], body)
    fix_ends(masked, level)


def mask(level, x, masked, solid):
    def body(q):
        for p in range(COLS[level]):
            m = solid[q, p]
            for f in range(F):
                put_masked(masked, level, f, q, p, m * x[f, q, p])

    each_row(ROWS[level], body)
    fix_ends(masked, level)


def restrict(level, K, x, masked, rhs, solid, react, coarse):
    R, C = ROWS[level], COLS[level]
    wide = 2 if C > 1 else 1

    def body(half):
        for P_ in range(C // wide):
            sums = [None] * F
            for dq in range(2):
                for dp in range(wide):
                    q, p = 2 * half + dq, wide * P_ + dp
                    drives, xs = drive(level, K, x, masked, rhs, solid, q, p)
                    s = react[q, p]
                    for f in range(F):
                        e = drives[f] - (s + (4.0 * SCALE[level] + K[f, f])) * xs[f]
                        sums[f] = e if sums[f] is None else sums[f] + e
            for f in range(F):
                coarse[f, half, P_] = sums[f] * (0.5 / wide)

    each_row(R // 2, body)


def near_rows(value):
    outer = jnp.where(sublanes((8, 128)) < 4, value[8:16], value[16:24])
    return jnp.concatenate([value[0:8], outer], axis=0)


def prolong(level, x, masked, solid, source):
    def body(half):
        for dq in range(2):
            q = 2 * half + dq
            for p in range(COLS[level]):
                m = solid[q, p]
                for f in range(F):
                    fix = source[f, half, p // 2]
                    if fix.shape[0] == 24 and m.shape[0] == 16:
                        fix = near_rows(fix)
                    new = x[f, q, p] + fix
                    x[f, q, p] = new
                    put_masked(masked, level, f, q, p, m * new)

    each_row(ROWS[level] // 2, body)
    fix_ends(masked, level)


def invert(level, K, react, inverse):
    def body(q):
        for p in range(COLS[level]):
            s = react[q, p]
            for f in range(F):
                inverse[f, q, p] = OMEGA / (s + (4.0 * SCALE[level] + K[f, f]))

    each_row(ROWS[level], body)


def decimate():
    k = lax.broadcasted_iota(jnp.int32, (128, 128), 0)
    o = lax.broadcasted_iota(jnp.int32, (128, 128), 1)
    return jnp.where(o == (k // 2 + 10) % 64, 0.5, 0.0).astype(BF16)


def spread(half):
    o = lax.broadcasted_iota(jnp.int32, (128, 128), 0)
    k = lax.broadcasted_iota(jnp.int32, (128, 128), 1)
    return jnp.where(o == (k // 2 + 10) % 64 + 64 * half, 1.0, 0.0).astype(BF16)


def half_pair(a, b):
    return jnp.where(lanes((8, 128)) < 64, a, roll(b, 64, 1))


def descend(K, X, M, RHS, SOLID, REACT, INV):
    for level in range(3):
        a, b = M[level]
        if level:
            first(level, X[level], a, RHS[level], SOLID[level], INV[level])
            sweep(level, K, X[level], a, b, RHS[level], SOLID[level], INV[level])
        if level < 2:
            restrict(
                level, K, X[level], b, RHS[level], SOLID[level], REACT[level], RHS[level + 1]
            )


def coarse_rhs(K, X, M, RHS, SOLID, REACT, three_rhs):
    restrict(2, K, X[2], M[2][1], RHS[2], SOLID[2], REACT[2], three_rhs)
    return [three_rhs[f, 0, 0, 0:8] for f in range(F)]


def levels_one_two(state_one, state_two):
    out = []
    for level, (x, r, s, m) in ((1, state_one), (2, state_two)):
        keys = []
        for q in range(ROWS[level]):
            for p in range(COLS[level]):
                for f in range(F):
                    keys.append((x, (f, q, p)))
                    keys.append((r, (f, q, p)))
                keys.append((s, (q, p)))
                keys.append((m, (q, p)))
        out.append(keys)
    return out


TAKE = ((3, 2), (2, 4))


def pack_middle(keys, middle):
    sub = sublanes((8, 128))
    place = 0
    for (start, size), members in zip(TAKE, keys):
        each = 8 // size
        for g in range(0, len(members), each):
            tile = None
            for u in range(each):
                ref, index = members[g + u]
                part = roll(ref[index][0:8], size * u - start, 0)
                tile = part if tile is None else jnp.where(sub >= size * u, part, tile)
            middle[place] = tile
            place += 1


def grow(keys, tall_keys, near, far, even):
    sub = sublanes((8, 128))
    place = 0
    for (start, size), members, targets in zip(TAKE, keys, tall_keys):
        each = 8 // size
        for g in range(0, len(members), each):
            after, before = meet(near[place], far[place], even)
            for u in range(each):
                ref, index = members[g + u]
                tile = ref[index]
                inner, outer = tile[0:8], tile[8:16]
                later = roll(after, start - size * u, 0)
                sooner = roll(before, start - size * u, 0)
                later = jnp.where(sub < start, outer, jnp.where(sub < start + size, later, 0.0))
                sooner = jnp.where(
                    sub >= start + size, outer, jnp.where(sub >= start, sooner, 0.0)
                )
                target, index = targets[g + u]
                target[index] = jnp.concatenate([inner, later, sooner], axis=0)
            place += 1


def down_one(K, own, row_one, row_two, one, two, *refs):
    there, payload = refs[: STATE + 1], refs[STATE + 1]
    here = refs[STATE + 2 : 2 * STATE + 3]
    i0, i1, i2, ma0, mb0, ma1, mb1, ma2, mb2 = refs[2 * STATE + 3 : 2 * STATE + 12]
    three_rhs, spread_out, sent, spread_sent = refs[2 * STATE + 12 :]
    x0, r0, s0, m0, x1, r1, s1, m1, x2, r2, s2, m2, middle = here
    moves = []

    def send(*which):
        for n in which:
            move = pltpu.make_async_copy(here[n], there[n], sent.at[n])
            move.start()
            moves.append(move)

    halo = (own, row_one, row_two, one, two)
    even = (is_even("gx"), is_even("gy"))
    for a in range(6):
        for q in range(8):
            for h in range(2):
                pair = widen(*halo, a * 16 + q * 2 + h, *even)
                for e in range(2):
                    if a < 4:
                        r0[a, q, 2 * h + e] = pair[e]
                    elif a == 4:
                        s0[q, 2 * h + e] = pair[e]
                    else:
                        m0[q, 2 * h + e] = pair[e]
    send(1, 2, 3)
    for q in range(4):
        m1[q, 0], m1[q, 1] = widen(*halo, 96 + q, *even)
    m2[0, 0], m2[1, 0] = widen(*halo, 100, *even)
    m3 = widen(*halo, 101, *even)[0]
    for q in range(4):
        for p in range(2):
            s1[q, p] = 0.25 * (
                (s0[2 * q, 2 * p] + s0[2 * q, 2 * p + 1])
                + (s0[2 * q + 1, 2 * p] + s0[2 * q + 1, 2 * p + 1])
            )
    for q in range(2):
        s2[q, 0] = 0.25 * (
            (s1[2 * q, 0] + s1[2 * q, 1]) + (s1[2 * q + 1, 0] + s1[2 * q + 1, 1])
        )
    X, RHS, SOLID, REACT, INV = (x0, x1, x2), (r0, r1, r2), (m0, m1, m2), (s0, s1, s2), (i0, i1, i2)
    M = ((ma0, mb0), (ma1, mb1), (ma2, mb2))
    for level in range(3):
        invert(level, K, REACT[level], INV[level])
    send(6, 7, 10, 11)
    first(0, x0, ma0, r0, m0, i0)
    sweep(0, K, x0, ma0, mb0, r0, m0, i0)
    send(0)
    descend(K, X, M, RHS, SOLID, REACT, INV)
    pack_middle(levels_one_two((x1, r1, s1, m1), (x2, r2, s2, m2)), middle)
    send(12, 4, 5, 8, 9)
    rest = coarse_rhs(K, X, M, RHS, SOLID, REACT, three_rhs)
    s3 = 0.5 * (s2[0, 0, 0:8] + s2[1, 0, 0:8])
    y = exact_dot(jnp.concatenate(rest + [m3[0:8], s3], axis=0), decimate())
    y = [y[8 * n : 8 * n + 8] for n in range(6)]
    tiles = [half_pair(y[2 * n], y[2 * n + 1]) for n in range(3)]
    for d in range(payload.shape[0]):
        for n in range(3):
            spread_out[d, n] = tiles[n]
    move = pltpu.make_async_copy(spread_out, payload, spread_sent)
    move.start()
    moves.append(move)
    for move in moves:
        move.wait()


def down_two(
    K, x0i, one, two, r0, s0, m0, i0, s1, m1, i1, s2, m2, i2,
    x0, x1, r1, x2, r2, payload,
    ma0, mb0, ma1, mb1, ma2, mb2, three_rhs,
):
    even = is_even("gy")
    for a in range(F):
        for q in range(8):
            for h in range(2):
                halo = [sides(one, two, a * 16 + q * 2 + h, v, even) for v in range(2)]
                for e in range(2):
                    mine = x0i[a, q, 2 * h + e]
                    x0[a, q, 2 * h + e] = jnp.concatenate(
                        [with_sides(mine[8 * v : 8 * v + 8], *halo[v][e]) for v in range(2)],
                        axis=0,
                    )
    X, RHS, SOLID, REACT, INV = (x0, x1, x2), (r0, r1, r2), (m0, m1, m2), (s0, s1, s2), (i0, i1, i2)
    M = ((ma0, mb0), (ma1, mb1), (ma2, mb2))
    mask(0, x0, mb0, m0)
    sweep(0, K, x0, mb0, ma0, r0, m0, i0)
    sweep(0, K, x0, ma0, mb0, r0, m0, i0)
    descend(K, X, M, RHS, SOLID, REACT, INV)
    rest = coarse_rhs(K, X, M, RHS, SOLID, REACT, three_rhs)
    y = exact_dot(jnp.concatenate(rest + rest[0:2], axis=0), decimate())
    y = [y[8 * n : 8 * n + 8] for n in range(4)]
    tiles = [half_pair(y[0], y[1]), half_pair(y[2], y[3])]
    for d in range(payload.shape[0]):
        for n in range(2):
            payload[d, n] = tiles[n]


def solve_coarsest(K, gathered, statics, natural, x, ma, mb, rhs, solid, react, inverse, wide, correct):
    low = lanes((8, 128)) < 64
    top = sublanes((8, 128)) == 0
    bottom = sublanes((8, 128)) == 7
    c = SCALE[3]
    blocks = gathered.shape[0]
    for d in range(blocks):
        natural[0, pl.ds(8 * d, 8), :] = gathered[d, 0]
        natural[1, pl.ds(8 * d, 8), :] = gathered[d, 1]
        natural[2, pl.ds(8 * d, 8), :] = statics[d, 2]
    diagonal = [jnp.where(low, 4.0 * c + K[2 * n, 2 * n], 4.0 * c + K[2 * n + 1, 2 * n + 1]) for n in range(2)]
    weights = [
        (jnp.where(low, K[0, 1], K[1, 0]), jnp.where(low, K[0, 2], K[1, 3]), jnp.where(low, K[0, 3], K[1, 2])),
        (jnp.where(low, K[2, 3], K[3, 2]), jnp.where(low, K[2, 0], K[3, 1]), jnp.where(low, K[2, 1], K[3, 0])),
    ]
    for t in range(blocks):
        pick = pl.ds(t, 8, stride=blocks)
        both = natural[2, pick, :]
        turned = roll(both, 64, 1)
        m = jnp.where(low, both, turned)
        s = jnp.where(low, turned, both)
        solid[t] = m
        react[t] = s
        for n in range(2):
            r = natural[n, pick, :]
            i = OMEGA / (s + diagonal[n])
            rhs[n, t] = r
            inverse[n, t] = i
            x[n, t] = i * r
            ma[n, t + 1] = m * (i * r)

    def ends(masked):
        for n in range(2):
            masked[n, 0] = jnp.where(top, 0.0, roll(masked[n, blocks], 1, 0))
            masked[n, blocks + 1] = jnp.where(bottom, 0.0, roll(masked[n, 1], -1, 0))

    def drives(t, masked):
        weight = c * solid[t]
        xs = [x[0, t], x[1, t]]
        turned = [roll(v, 64, 1) for v in xs]
        out = []
        for n in range(2):
            here = masked[n, t + 1]
            near = (masked[n, t] + masked[n, t + 2]) + (roll(here, 1, 1) + roll(here, -1, 1))
            u, v, w = weights[n]
            mixed = u * turned[n] + v * xs[1 - n] + w * turned[1 - n]
            out.append(rhs[n, t] + weight * near - mixed)
        return out, xs

    ends(ma)
    for index in range(5):
        source, target = (ma, mb) if index % 2 == 0 else (mb, ma)

        def body(t, _):
            out, xs = drives(t, source)
            m = solid[t]
            for n in range(2):
                new = (1.0 - OMEGA) * xs[n] + inverse[n, t] * out[n]
                x[n, t] = new
                target[n, t + 1] = m * new
            return _

        lax.fori_loop(0, blocks, body, 0, unroll=blocks)
        ends(target)

    def gather_sums(t, sums):
        out, xs = drives(t, mb)
        s = react[t]
        sums = list(sums)
        for n in range(2):
            g = s + diagonal[n]
            sums[n] = sums[n] + (out[n] - g * xs[n])
            sums[2 + n] = sums[2 + n] + g
        return tuple(sums)

    zero = jnp.zeros((8, 128), F32)
    sums = lax.fori_loop(0, blocks, gather_sums, (zero,) * 4, unroll=blocks)
    sums = [jnp.sum(v, axis=0, keepdims=True) for v in sums]
    for n in range(2):
        wide[n, pl.ds(0, 8), :] = zero
        wide[n, pl.ds(8 * blocks + 8, 8), :] = zero
        mean = sums[n] / sums[2 + n]
        for t in range(blocks):
            wide[n, pl.ds(8 + t, 8, stride=blocks), :] = x[n, t] + mean
    start = pl.multiple_of(lax.axis_index("gx") * 8, 8)
    low = sublanes((8, 128)) < 4
    height = correct.shape[-2]
    rows = []
    for n in range(2):
        mine = wide[n, pl.ds(start + 8, 8), :]
        after = wide[n, pl.ds(start + 16, 8), :]
        before = wide[n, pl.ds(start, 8), :]
        rows += [mine, after, before] if height == 24 else [mine, jnp.where(low, after, before)]
    rows = jnp.concatenate(rows, axis=0)
    for half in range(2):
        y = exact_dot(rows, spread(half))
        correct[half, 0, 0] = y[0:height]
        correct[2 + half, 0, 0] = y[height : 2 * height]


def rise(level, K, X, M, RHS, SOLID, INV, source, last):
    a, b = M[level]
    prolong(level, X[level], a, SOLID[level], source)
    sweep(level, K, X[level], a, b, RHS[level], SOLID[level], INV[level])
    sweep(level, K, X[level], b, a, RHS[level], SOLID[level], INV[level], last=last)
    return X[level]


def ascend(K, X, M, RHS, SOLID, INV, correct):
    source = correct
    for level in (2, 1, 0):
        source = rise(level, K, X, M, RHS, SOLID, INV, source, level > 0)


def copy_state(sources, targets):
    for source, target in zip(sources, targets):
        target[...] = source[...]


def up_one(K, gathered, *refs):
    there, refs = refs[:GIVEN], refs[GIVEN:]
    kept, (i0, i1s, i2s, one, two) = refs[:KEPT], refs[KEPT : KEPT + 5]
    refs = refs[KEPT + 5 :]
    here, refs = kept + refs[: GIVEN - KEPT], refs[GIVEN - KEPT :]
    x1, r1, s1, m1, i1, x2, r2, s2, m2, i2, ma0, mb0, ma1, mb1, ma2, mb2 = refs[:16]
    natural, x3, ma3, mb3, r3, m3, s3, i3, wide, correct, arrived = refs[16:]
    moves = [
        pltpu.make_async_copy(there[n], here[n], arrived.at[n]) for n in range(GIVEN)
    ]
    for move in moves[::-1]:
        move.start()
    r0, m0, x0, s0, s1s, m1s, s2s, m2s, x1s, r1s, x2s, r2s, near, far = here
    solve_coarsest(K, gathered, gathered, natural, x3, ma3, mb3, r3, m3, s3, i3, wide, correct)
    for move in moves[3:]:
        move.wait()
    grow(
        levels_one_two((x1s, r1s, s1s, m1s), (x2s, r2s, s2s, m2s)),
        levels_one_two((x1, r1, s1, m1), (x2, r2, s2, m2)),
        near, far, is_even("gx"),
    )
    invert(1, K, s1, i1)
    invert(2, K, s2, i2)
    invert(0, K, s0, i0)
    invert(1, K, s1s, i1s)
    invert(2, K, s2s, i2s)
    M = ((ma0, mb0), (ma1, mb1), (ma2, mb2))
    X, RHS, SOLID, INV = (x0, x1, x2), (r0, r1, r2), (m0, m1, m2), (i0, i1, i2)
    source = rise(2, K, X, M, RHS, SOLID, INV, correct, True)
    source = rise(1, K, X, M, RHS, SOLID, INV, source, True)
    for move in moves[:3]:
        move.wait()
    rise(0, K, X, M, RHS, SOLID, INV, source, True)

    def pick(index, v):
        f, q, h = index // 16, index // 2 % 8, index % 2
        part = slice(8 * v, 8 * v + 8)
        return half_pair(x0[f, q, 2 * h, part], x0[f, q, 2 * h + 1, part])

    pack_sides(pick, XTILES, one, two, is_even("gy"))


def up_two(
    K, gathered, statics, x0i, r0, s0, m0, i0, x1i, r1, m1, i1, x2i, r2, m2, i2,
    displacement, residual,
    x0, x1, x2, ma0, mb0, ma1, mb1, ma2, mb2,
    natural, x3, ma3, mb3, r3, m3, s3, i3, wide, correct, stage,
):
    copy_state((x0i, x1i, x2i), (x0, x1, x2))
    solve_coarsest(K, gathered, statics, natural, x3, ma3, mb3, r3, m3, s3, i3, wide, correct)
    M = ((ma0, mb0), (ma1, mb1), (ma2, mb2))
    ascend(K, (x0, x1, x2), M, (r0, r1, r2), (m0, m1, m2), (i0, i1, i2), correct)
    mine = slice(0, 8)
    for q in range(8):
        for h in range(2):
            outs = []
            for p in (2 * h, 2 * h + 1):
                drives, xs = drive(0, K, x0, ma0, r0, m0, q, p, mine)
                s = s0[q, p, mine]
                rest = [drives[f] - (s + (4.0 + K[f, f])) * xs[f] for f in range(F)]
                outs.append(xs + rest)
            for a in range(2 * F):
                stage[a, h, pl.ds(q, 8, stride=8), :] = half_pair(outs[0][a], outs[1][a])
    matrix = join_matrix(256, 4)
    for f in range(F):
        for out, a in ((displacement, f), (residual, F + f)):
            out[f] = exact_dot(jnp.concatenate([stage[a, 0], stage[a, 1]], axis=1), matrix)


def sds(*shape):
    return jax.ShapeDtypeStruct(shape, F32)


def field(level, height=16):
    return (F, ROWS[level], COLS[level], height, 128)


def plane(level, height=16):
    return (ROWS[level], COLS[level], height, 128)


def masked_scratch(height=16):
    out = []
    for level in range(3):
        tall = height if level else 16
        shape = (F, ROWS[level] + 2, COLS[level] + 2, tall, 128)
        out += [pltpu.VMEM(shape, F32), pltpu.VMEM(shape, F32)]
    return out


def coarsest_scratch(blocks, height=16):
    return [
        pltpu.VMEM((3, 8 * blocks, 128), F32),
        pltpu.VMEM((2, blocks, 8, 128), F32),
        pltpu.VMEM((2, blocks + 2, 8, 128), F32),
        pltpu.VMEM((2, blocks + 2, 8, 128), F32),
        pltpu.VMEM((2, blocks, 8, 128), F32),
        pltpu.VMEM((blocks, 8, 128), F32),
        pltpu.VMEM((blocks, 8, 128), F32),
        pltpu.VMEM((2, blocks, 8, 128), F32),
        pltpu.VMEM((2, 8 * blocks + 16, 128), F32),
        pltpu.VMEM((F, 1, 1, height, 128), F32),
    ]


def call(body, outs, scratch, args, smem=True, hbm=0):
    specs = [pl.BlockSpec(memory_space=pltpu.VMEM)] * (len(args) - hbm)
    specs += [pl.BlockSpec(memory_space=pltpu.HBM)] * hbm
    if smem:
        specs[0] = pl.BlockSpec(memory_space=pltpu.SMEM)
    args = args[: len(args) - hbm] + tuple(
        pltpu.with_memory_space_constraint(array, pltpu.HBM) for array in args[len(args) - hbm :]
    )
    kept = [isinstance(out, jax.ShapeDtypeStruct) for out in outs]
    return pl.pallas_call(
        body,
        out_shape=outs,
        in_specs=specs,
        out_specs=[
            pl.BlockSpec(memory_space=pltpu.VMEM if inside else pltpu.HBM) for inside in kept
        ],
        scratch_shapes=scratch,
        compiler_params=pltpu.CompilerParams(vmem_limit_bytes=30 * 1024 * 1024),
    )(*args)


def swap(axis, first, second):
    count = lax.axis_size(axis)
    near = [(i, i ^ 1) for i in range(count) if i ^ 1 < count]
    far = [(i, ((i - 1) ^ 1) + 1) for i in range(1, count) if ((i - 1) ^ 1) + 1 < count]
    return lax.ppermute(first, axis, near), lax.ppermute(second, axis, far)


def shards(source, reaction, coupling, solid0, solid1, solid2, solid3):
    blocks = lax.axis_size("gx")
    arrays = (source, reaction, solid0, solid1, solid2, solid3)
    packed = call(
        pack_kernel,
        [sds(TILES, 8, 128), sds(TILES // 2, 8, 128), sds(TILES // 2, 8, 128)],
        [pltpu.VMEM(array.shape, array.dtype) for array in arrays]
        + [
            pltpu.VMEM((6, 2, 64, 128), F32),
            pltpu.VMEM((32, 128), F32),
            pltpu.SemaphoreType.DMA((6,)),
        ],
        arrays,
        smem=False,
        hbm=6,
    )
    own, one, two = packed
    rows = swap("gx", one, two)
    side = call(
        functools.partial(side_kernel, TILES),
        [sds(TILES // 3, 2, 8, 128)] * 2,
        [],
        (own,) + rows,
        smem=False,
    )
    halo = (own,) + rows + swap("gy", *side)
    shapes = []
    for level in range(3):
        shapes += [field(level)] * 2 + [plane(level)] * 2
    shapes.append((MIDDLE, 8, 128))
    state = call(
        down_one,
        [pltpu.HBM(shape, F32) for shape in shapes + [(blocks, 3, 8, 128)]],
        [pltpu.VMEM(shape, F32) for shape in shapes]
        + [pltpu.VMEM(field(level), F32) for level in range(3)]
        + masked_scratch()
        + [
            pltpu.VMEM((F, 1, 1, 16, 128), F32),
            pltpu.VMEM((blocks, 3, 8, 128), F32),
            pltpu.SemaphoreType.DMA((STATE + 1,)),
            pltpu.SemaphoreType.DMA,
        ],
        (coupling,) + halo,
    )
    x0, r0, s0, m0, x1, r1, s1, m1, x2, r2, s2, m2, middle, payload = state
    near, far = swap("gx", middle, middle)
    statics = lax.all_to_all(payload, "gx", 0, 0)
    inner = [pltpu.VMEM(field(level), F32) for level in range(3)]
    tall = []
    for level in (1, 2):
        tall += [pltpu.VMEM(field(level, 24), F32)] * 2
        tall += [pltpu.VMEM(plane(level, 24), F32)] * 2
        tall += [pltpu.VMEM(field(level, 24), F32)]
    given = (r0, m0, x0, s0, s1, m1, s2, m2, x1, r1, x2, r2, near, far)
    r0, m0, x0, s0, s1, m1, s2, m2, i0, i1, i2, one, two = call(
        up_one,
        [sds(*array.shape) for array in given[:KEPT]]
        + [sds(*field(level)) for level in range(3)]
        + [sds(-(-XTILES // 3), 2, 8, 128)] * 2,
        [pltpu.VMEM(array.shape, F32) for array in given[KEPT:]]
        + tall
        + masked_scratch(24)
        + coarsest_scratch(blocks, 24)
        + [pltpu.SemaphoreType.DMA((GIVEN,))],
        (coupling, statics) + given,
        hbm=GIVEN,
    )
    x0, x1, r1, x2, r2, payload = call(
        down_two,
        [sds(*field(0)), sds(*field(1)), sds(*field(1)), sds(*field(2)), sds(*field(2)),
         sds(blocks, 2, 8, 128)],
        masked_scratch() + [pltpu.VMEM((F, 1, 1, 16, 128), F32)],
        (coupling, x0) + swap("gy", one, two) + (r0, s0, m0, i0, s1, m1, i1, s2, m2, i2),
    )
    gathered = lax.all_to_all(payload, "gx", 0, 0)
    displacement, residual = call(
        up_two,
        [sds(F, 64, 256), sds(F, 64, 256)],
        inner + masked_scratch() + coarsest_scratch(blocks)
        + [pltpu.VMEM((2 * F, 2, 64, 128), F32)],
        (coupling, gathered, statics, x0, r0, s0, m0, i0, x1, r1, m1, i1, x2, r2, m2, i2),
    )
    return displacement, residual


def solution(mesh):
    placed = (
        P(None, "gx", "gy"),
        P("gx", "gy"),
        P(),
        P("gx", "gy"),
        P("gx", "gy"),
        P("gx", "gy"),
        P("gx", "gy"),
    )
    return jax.shard_map(
        shards,
        mesh=mesh,
        in_specs=placed,
        out_specs=(P(None, "gx", "gy"), P(None, "gx", "gy")),
        check_vma=False,
    )
```

```python
import functools

import jax
import jax.numpy as jnp
from jax import lax
from jax.experimental import pallas as pl
from jax.experimental.pallas import tpu as pltpu
from jax.sharding import PartitionSpec as P


F = 4
ROWS = (8, 4, 2)
COLS = (4, 2, 1)
SCALE = (1.0, 0.25, 0.0625, 0.015625)
OMEGA = 0.6
TILES = 102
XTILES = 64
MIDDLE = 30
STATE = 12
GIVEN = 14
KEPT = 8
F32 = jnp.float32
BF16 = jnp.bfloat16


def lanes(shape):
    return lax.broadcasted_iota(jnp.int32, shape, len(shape) - 1)


def sublanes(shape):
    return lax.broadcasted_iota(jnp.int32, shape, len(shape) - 2)


def roll(value, shift, axis):
    size = value.shape[axis]
    shift = shift % size
    return value if shift == 0 else pltpu.roll(value, shift, axis)


def three(value):
    high = value.astype(BF16)
    rest = value - high.astype(F32)
    mid = rest.astype(BF16)
    low = (rest - mid.astype(F32)).astype(BF16)
    return high, mid, low


def exact_dot(value, matrix):
    parts = [jnp.dot(part, matrix, preferred_element_type=F32) for part in three(value)]
    return parts[0] + (parts[1] + parts[2])


def split_matrix(size, stride):
    c = lax.broadcasted_iota(jnp.int32, (size, size), 0)
    o = lax.broadcasted_iota(jnp.int32, (size, size), 1)
    return jnp.where(o == (c % stride) * (size // stride) + c // stride, 1.0, 0.0).astype(BF16)


def join_matrix(size, stride):
    o = lax.broadcasted_iota(jnp.int32, (size, size), 0)
    c = lax.broadcasted_iota(jnp.int32, (size, size), 1)
    return jnp.where(o == (c % stride) * (size // stride) + c // stride, 1.0, 0.0).astype(BF16)


def is_even(axis):
    return lax.broadcast(lax.rem(lax.axis_index(axis), 2), (8, 128)) == 0


def meet(after, before, even):
    return jnp.where(even, after, before), jnp.where(even, before, after)


def pack_rows(own, one, two, count):
    low = sublanes((8, 128)) < 4
    even = is_even("gx")

    def body(n, _):
        a = own[2 * n]
        b = own[2 * n + 1]
        up = jnp.where(low, a, roll(b, 4, 0))
        dn = jnp.where(low, roll(a, 4, 0), b)
        one[n], two[n] = meet(dn, up, even)
        return _

    lax.fori_loop(0, count // 2, body, 0, unroll=3)


def outer_rows(one, two, n, odd, even):
    low = sublanes((8, 128)) < 4
    up, dn = meet(one[n], two[n], even)
    if odd:
        return jnp.where(low, roll(up, 4, 0), dn)
    return jnp.where(low, up, roll(dn, 4, 0))


def pack_kernel(
    source_in, reaction_in, solid0_in, solid1_in, solid2_in, solid3_in, own, one, two,
    source, reaction, solid0, solid1, solid2, solid3, stage, small, arrived,
):
    moves = [
        pltpu.make_async_copy(there, here, arrived.at[n])
        for n, (there, here) in enumerate(
            (
                (source_in, source),
                (reaction_in, reaction),
                (solid0_in, solid0),
                (solid1_in, solid1),
                (solid2_in, solid2),
                (solid3_in, solid3),
            )
        )
    ]
    for move in moves:
        move.start()
    matrix = split_matrix(256, 4)
    for move in moves:
        move.wait()
    for a in range(6):
        if a < 4:
            value = exact_dot(source[a], matrix)
        elif a == 4:
            value = exact_dot(reaction[...], matrix)
        else:
            value = jnp.dot(
                solid0[...].astype(F32).astype(BF16), matrix, preferred_element_type=F32
            )
        for h in range(2):
            stage[a, h] = value[:, 128 * h : 128 * h + 128]
    for a in range(6):
        for q in range(8):
            for h in range(2):
                own[a * 16 + q * 2 + h] = stage[a, h, pl.ds(q, 8, stride=8), :]
    small[...] = jnp.dot(
        solid1[...].astype(F32).astype(BF16),
        split_matrix(128, 2),
        preferred_element_type=F32,
    )
    for q in range(4):
        own[96 + q] = small[pl.ds(q, 8, stride=4), :]
    c = lax.broadcasted_iota(jnp.int32, (64, 128), 0)
    o = lax.broadcasted_iota(jnp.int32, (64, 128), 1)
    wide = jnp.where(o % 64 == c, 1.0, 0.0).astype(BF16)
    small[pl.ds(0, 16), :] = jnp.dot(
        solid2[...].astype(F32).astype(BF16), wide, preferred_element_type=F32
    )
    own[100] = jnp.where(
        lanes((8, 128)) < 64,
        small[pl.ds(0, 8, stride=2), :],
        small[pl.ds(1, 8, stride=2), :],
    )
    c = lax.broadcasted_iota(jnp.int32, (32, 128), 0)
    o = lax.broadcasted_iota(jnp.int32, (32, 128), 1)
    twice = jnp.where((o % 64) // 2 == c, 1.0, 0.0)
    own[101] = jnp.dot(
        solid3[...].astype(F32), twice, preferred_element_type=F32,
        precision=lax.Precision.HIGHEST,
    )
    pack_rows(own, one, two, TILES)


def pack_sides(pick, count, one, two, even):
    lane = lanes((8, 128)) % 64
    for g in range(-(-count // 3)):
        members = min(3, count - 3 * g)
        for v in range(2):
            tiles = [pick(3 * g + t, v) for t in range(members)]
            r, l = tiles[0], tiles[0]
            for t in range(1, members):
                r = jnp.where(lane < 64 - 20 * t, roll(tiles[t], -20 * t, 1), r)
                l = jnp.where(lane >= 20 * t, roll(tiles[t], 20 * t, 1), l)
            one[g, v], two[g, v] = meet(r, l, even)


def side_kernel(count, own, up_one, up_two, one, two):
    even = is_even("gx")

    def pick(index, v):
        if v == 0:
            return own[index]
        return outer_rows(up_one, up_two, index // 2, index % 2, even)

    pack_sides(pick, count, one, two, is_even("gy"))


def sides(one, two, index, v, even):
    g, t = index // 3, index % 3
    l, r = meet(one[g, v], two[g, v], even)
    return [
        (roll(r, 64 + 20 * t + 64 * h, 1), roll(l, 64 - 20 * t + 64 * h, 1)) for h in range(2)
    ]


def with_sides(centre, before, after):
    lane = lanes((8, 128))
    tile = jnp.where(lane < 64, centre, jnp.where(lane < 84, after, 0.0))
    return jnp.where(lane >= 108, before, tile)


def widen(own, row_one, row_two, one, two, index, even_x, even_y):
    out = [[], []]
    for v in range(2):
        if v == 0:
            mine = own[index]
        else:
            mine = outer_rows(row_one, row_two, index // 2, index % 2, even_x)
        halo = sides(one, two, index, v, even_y)
        for h in range(2):
            out[h].append(with_sides(roll(mine, 64 * h, 1), *halo[h]))
    return [jnp.concatenate(pair, axis=0) for pair in out]


def fix_ends(masked, level):
    R, C = ROWS[level], COLS[level]
    for f in range(F):
        for p in range(C):
            masked[f, 0, p + 1] = roll(masked[f, R, p + 1], 1, 0)
            masked[f, R + 1, p + 1] = roll(masked[f, 1, p + 1], -1, 0)
        for q in range(R):
            masked[f, q + 1, 0] = roll(masked[f, q + 1, C], 1, 1)
            masked[f, q + 1, C + 1] = roll(masked[f, q + 1, 1], -1, 1)


def put_masked(masked, level, f, q, p, value):
    masked[f, q + 1, p + 1] = value


def each_row(count, body):
    if count > 4:
        def step(q, _):
            body(q)
            return _

        lax.fori_loop(0, count, step, 0, unroll=count)
    else:
        for q in range(count):
            body(q)


def drive(level, K, x, masked, rhs, solid, q, p, rows=slice(None)):
    xs = [x[f, q, p, rows] for f in range(F)]
    weight = solid[q, p, rows]
    if level:
        weight = weight * SCALE[level]
    out = []
    for f in range(F):
        near = (masked[f, q, p + 1, rows] + masked[f, q + 2, p + 1, rows]) + (
            masked[f, q + 1, p, rows] + masked[f, q + 1, p + 2, rows]
        )
        total = rhs[f, q, p, rows] + weight * near
        mixed = None
        for b in range(F):
            if b != f:
                term = K[f, b] * xs[b]
                mixed = term if mixed is None else mixed + term
        out.append(total - mixed)
    return out, xs


def sweep(level, K, x, masked, target, rhs, solid, inverse, last=False):
    R, C = ROWS[level], COLS[level]

    def body(q):
        news = []
        for p in range(C):
            drives, xs = drive(level, K, x, masked, rhs, solid, q, p)
            news.append(
                [(1.0 - OMEGA) * xs[f] + inverse[f, q, p] * drives[f] for f in range(F)]
            )
        for p in range(C):
            m = None if last else solid[q, p]
            for f in range(F):
                x[f, q, p] = news[p][f]
                if not last:
                    put_masked(target, level, f, q, p, m * news[p][f])

    each_row(R, body)
    if not last:
        fix_ends(target, level)


def first(level, x, masked, rhs, solid, inverse):
    def body(q):
        for p in range(COLS[level]):
            m = solid[q, p]
            for f in range(F):
                new = inverse[f, q, p] * rhs[f, q, p]
                x[f, q, p] = new
                put_masked(masked, level, f, q, p, m * new)

    each_row(ROWS[level], body)
    fix_ends(masked, level)


def mask(level, x, masked, solid):
    def body(q):
        for p in range(COLS[level]):
            m = solid[q, p]
            for f in range(F):
                put_masked(masked, level, f, q, p, m * x[f, q, p])

    each_row(ROWS[level], body)
    fix_ends(masked, level)


def restrict(level, K, x, masked, rhs, solid, react, coarse):
    R, C = ROWS[level], COLS[level]
    wide = 2 if C > 1 else 1

    def body(half):
        for P_ in range(C // wide):
            sums = [None] * F
            for dq in range(2):
                for dp in range(wide):
                    q, p = 2 * half + dq, wide * P_ + dp
                    drives, xs = drive(level, K, x, masked, rhs, solid, q, p)
                    s = react[q, p]
                    for f in range(F):
                        e = drives[f] - (s + (4.0 * SCALE[level] + K[f, f])) * xs[f]
                        sums[f] = e if sums[f] is None else sums[f] + e
            for f in range(F):
                coarse[f, half, P_] = sums[f] * (0.5 / wide)

    each_row(R // 2, body)


def near_rows(value):
    outer = jnp.where(sublanes((8, 128)) < 4, value[8:16], value[16:24])
    return jnp.concatenate([value[0:8], outer], axis=0)


def prolong(level, x, masked, solid, source):
    def body(half):
        for dq in range(2):
            q = 2 * half + dq
            for p in range(COLS[level]):
                m = solid[q, p]
                for f in range(F):
                    fix = source[f, half, p // 2]
                    if fix.shape[0] == 24 and m.shape[0] == 16:
                        fix = near_rows(fix)
                    new = x[f, q, p] + fix
                    x[f, q, p] = new
                    put_masked(masked, level, f, q, p, m * new)

    each_row(ROWS[level] // 2, body)
    fix_ends(masked, level)


def invert(level, K, react, inverse):
    def body(q):
        for p in range(COLS[level]):
            s = react[q, p]
            for f in range(F):
                inverse[f, q, p] = OMEGA / (s + (4.0 * SCALE[level] + K[f, f]))

    each_row(ROWS[level], body)


def decimate():
    k = lax.broadcasted_iota(jnp.int32, (128, 128), 0)
    o = lax.broadcasted_iota(jnp.int32, (128, 128), 1)
    return jnp.where(o == (k // 2 + 10) % 64, 0.5, 0.0).astype(BF16)


def spread(half):
    o = lax.broadcasted_iota(jnp.int32, (128, 128), 0)
    k = lax.broadcasted_iota(jnp.int32, (128, 128), 1)
    return jnp.where(o == (k // 2 + 10) % 64 + 64 * half, 1.0, 0.0).astype(BF16)


def half_pair(a, b):
    return jnp.where(lanes((8, 128)) < 64, a, roll(b, 64, 1))


def descend(K, X, M, RHS, SOLID, REACT, INV):
    for level in range(3):
        a, b = M[level]
        if level:
            first(level, X[level], a, RHS[level], SOLID[level], INV[level])
            sweep(level, K, X[level], a, b, RHS[level], SOLID[level], INV[level])
        if level < 2:
            restrict(
                level, K, X[level], b, RHS[level], SOLID[level], REACT[level], RHS[level + 1]
            )


def coarse_rhs(K, X, M, RHS, SOLID, REACT, three_rhs):
    restrict(2, K, X[2], M[2][1], RHS[2], SOLID[2], REACT[2], three_rhs)
    return [three_rhs[f, 0, 0, 0:8] for f in range(F)]


def levels_one_two(state_one, state_two):
    out = []
    for level, (x, r, s, m) in ((1, state_one), (2, state_two)):
        keys = []
        for q in range(ROWS[level]):
            for p in range(COLS[level]):
                for f in range(F):
                    keys.append((x, (f, q, p)))
                    keys.append((r, (f, q, p)))
                keys.append((s, (q, p)))
                keys.append((m, (q, p)))
        out.append(keys)
    return out


TAKE = ((3, 2), (2, 4))


def pack_middle(keys, middle):
    sub = sublanes((8, 128))
    place = 0
    for (start, size), members in zip(TAKE, keys):
        each = 8 // size
        for g in range(0, len(members), each):
            tile = None
            for u in range(each):
                ref, index = members[g + u]
                part = roll(ref[index][0:8], size * u - start, 0)
                tile = part if tile is None else jnp.where(sub >= size * u, part, tile)
            middle[place] = tile
            place += 1


def grow(keys, tall_keys, near, far, even):
    sub = sublanes((8, 128))
    place = 0
    for (start, size), members, targets in zip(TAKE, keys, tall_keys):
        each = 8 // size
        for g in range(0, len(members), each):
            after, before = meet(near[place], far[place], even)
            for u in range(each):
                ref, index = members[g + u]
                tile = ref[index]
                inner, outer = tile[0:8], tile[8:16]
                later = roll(after, start - size * u, 0)
                sooner = roll(before, start - size * u, 0)
                later = jnp.where(sub < start, outer, jnp.where(sub < start + size, later, 0.0))
                sooner = jnp.where(
                    sub >= start + size, outer, jnp.where(sub >= start, sooner, 0.0)
                )
                target, index = targets[g + u]
                target[index] = jnp.concatenate([inner, later, sooner], axis=0)
            place += 1


def down_one(K, own, row_one, row_two, one, two, *refs):
    there, payload = refs[: STATE + 1], refs[STATE + 1]
    here = refs[STATE + 2 : 2 * STATE + 3]
    i0, i1, i2, ma0, mb0, ma1, mb1, ma2, mb2 = refs[2 * STATE + 3 : 2 * STATE + 12]
    three_rhs, spread_out, sent, spread_sent = refs[2 * STATE + 12 :]
    x0, r0, s0, m0, x1, r1, s1, m1, x2, r2, s2, m2, middle = here
    moves = []

    def send(*which):
        for n in which:
            move = pltpu.make_async_copy(here[n], there[n], sent.at[n])
            move.start()
            moves.append(move)

    halo = (own, row_one, row_two, one, two)
    even = (is_even("gx"), is_even("gy"))
    for a in range(6):
        for q in range(8):
            for h in range(2):
                pair = widen(*halo, a * 16 + q * 2 + h, *even)
                for e in range(2):
                    if a < 4:
                        r0[a, q, 2 * h + e] = pair[e]
                    elif a == 4:
                        s0[q, 2 * h + e] = pair[e]
                    else:
                        m0[q, 2 * h + e] = pair[e]
    send(1, 2, 3)
    for q in range(4):
        m1[q, 0], m1[q, 1] = widen(*halo, 96 + q, *even)
    m2[0, 0], m2[1, 0] = widen(*halo, 100, *even)
    m3 = widen(*halo, 101, *even)[0]
    for q in range(4):
        for p in range(2):
            s1[q, p] = 0.25 * (
                (s0[2 * q, 2 * p] + s0[2 * q, 2 * p + 1])
                + (s0[2 * q + 1, 2 * p] + s0[2 * q + 1, 2 * p + 1])
            )
    for q in range(2):
        s2[q, 0] = 0.25 * (
            (s1[2 * q, 0] + s1[2 * q, 1]) + (s1[2 * q + 1, 0] + s1[2 * q + 1, 1])
        )
    X, RHS, SOLID, REACT, INV = (x0, x1, x2), (r0, r1, r2), (m0, m1, m2), (s0, s1, s2), (i0, i1, i2)
    M = ((ma0, mb0), (ma1, mb1), (ma2, mb2))
    for level in range(3):
        invert(level, K, REACT[level], INV[level])
    send(6, 7, 10, 11)
    first(0, x0, ma0, r0, m0, i0)
    sweep(0, K, x0, ma0, mb0, r0, m0, i0)
    send(0)
    descend(K, X, M, RHS, SOLID, REACT, INV)
    pack_middle(levels_one_two((x1, r1, s1, m1), (x2, r2, s2, m2)), middle)
    send(12, 4, 5, 8, 9)
    rest = coarse_rhs(K, X, M, RHS, SOLID, REACT, three_rhs)
    s3 = 0.5 * (s2[0, 0, 0:8] + s2[1, 0, 0:8])
    y = exact_dot(jnp.concatenate(rest + [m3[0:8], s3], axis=0), decimate())
    y = [y[8 * n : 8 * n + 8] for n in range(6)]
    tiles = [half_pair(y[2 * n], y[2 * n + 1]) for n in range(3)]
    for d in range(payload.shape[0]):
        for n in range(3):
            spread_out[d, n] = tiles[n]
    move = pltpu.make_async_copy(spread_out, payload, spread_sent)
    move.start()
    moves.append(move)
    for move in moves:
        move.wait()


def down_two(
    K, x0i, one, two, r0, s0, m0, i0, s1, m1, i1, s2, m2, i2,
    x0, x1, r1, x2, r2, payload,
    ma0, mb0, ma1, mb1, ma2, mb2, three_rhs,
):
    even = is_even("gy")
    for a in range(F):
        for q in range(8):
            for h in range(2):
                halo = [sides(one, two, a * 16 + q * 2 + h, v, even) for v in range(2)]
                for e in range(2):
                    mine = x0i[a, q, 2 * h + e]
                    x0[a, q, 2 * h + e] = jnp.concatenate(
                        [with_sides(mine[8 * v : 8 * v + 8], *halo[v][e]) for v in range(2)],
                        axis=0,
                    )
    X, RHS, SOLID, REACT, INV = (x0, x1, x2), (r0, r1, r2), (m0, m1, m2), (s0, s1, s2), (i0, i1, i2)
    M = ((ma0, mb0), (ma1, mb1), (ma2, mb2))
    mask(0, x0, mb0, m0)
    sweep(0, K, x0, mb0, ma0, r0, m0, i0)
    sweep(0, K, x0, ma0, mb0, r0, m0, i0)
    descend(K, X, M, RHS, SOLID, REACT, INV)
    rest = coarse_rhs(K, X, M, RHS, SOLID, REACT, three_rhs)
    y = exact_dot(jnp.concatenate(rest + rest[0:2], axis=0), decimate())
    y = [y[8 * n : 8 * n + 8] for n in range(4)]
    tiles = [half_pair(y[0], y[1]), half_pair(y[2], y[3])]
    for d in range(payload.shape[0]):
        for n in range(2):
            payload[d, n] = tiles[n]


def solve_coarsest(K, gathered, statics, natural, x, ma, mb, rhs, solid, react, inverse, wide, correct):
    low = lanes((8, 128)) < 64
    top = sublanes((8, 128)) == 0
    bottom = sublanes((8, 128)) == 7
    c = SCALE[3]
    blocks = gathered.shape[0]
    for d in range(blocks):
        natural[0, pl.ds(8 * d, 8), :] = gathered[d, 0]
        natural[1, pl.ds(8 * d, 8), :] = gathered[d, 1]
        natural[2, pl.ds(8 * d, 8), :] = statics[d, 2]
    diagonal = [jnp.where(low, 4.0 * c + K[2 * n, 2 * n], 4.0 * c + K[2 * n + 1, 2 * n + 1]) for n in range(2)]
    weights = [
        (jnp.where(low, K[0, 1], K[1, 0]), jnp.where(low, K[0, 2], K[1, 3]), jnp.where(low, K[0, 3], K[1, 2])),
        (jnp.where(low, K[2, 3], K[3, 2]), jnp.where(low, K[2, 0], K[3, 1]), jnp.where(low, K[2, 1], K[3, 0])),
    ]
    for t in range(blocks):
        pick = pl.ds(t, 8, stride=blocks)
        both = natural[2, pick, :]
        turned = roll(both, 64, 1)
        m = jnp.where(low, both, turned)
        s = jnp.where(low, turned, both)
        solid[t] = m
        react[t] = s
        for n in range(2):
            r = natural[n, pick, :]
            i = OMEGA / (s + diagonal[n])
            rhs[n, t] = r
            inverse[n, t] = i
            x[n, t] = i * r
            ma[n, t + 1] = m * (i * r)

    def ends(masked):
        for n in range(2):
            masked[n, 0] = jnp.where(top, 0.0, roll(masked[n, blocks], 1, 0))
            masked[n, blocks + 1] = jnp.where(bottom, 0.0, roll(masked[n, 1], -1, 0))

    def drives(t, masked):
        weight = c * solid[t]
        xs = [x[0, t], x[1, t]]
        turned = [roll(v, 64, 1) for v in xs]
        out = []
        for n in range(2):
            here = masked[n, t + 1]
            near = (masked[n, t] + masked[n, t + 2]) + (roll(here, 1, 1) + roll(here, -1, 1))
            u, v, w = weights[n]
            mixed = u * turned[n] + v * xs[1 - n] + w * turned[1 - n]
            out.append(rhs[n, t] + weight * near - mixed)
        return out, xs

    ends(ma)
    for index in range(5):
        source, target = (ma, mb) if index % 2 == 0 else (mb, ma)

        def body(t, _):
            out, xs = drives(t, source)
            m = solid[t]
            for n in range(2):
                new = (1.0 - OMEGA) * xs[n] + inverse[n, t] * out[n]
                x[n, t] = new
                target[n, t + 1] = m * new
            return _

        lax.fori_loop(0, blocks, body, 0, unroll=blocks)
        ends(target)

    def gather_sums(t, sums):
        out, xs = drives(t, mb)
        s = react[t]
        sums = list(sums)
        for n in range(2):
            g = s + diagonal[n]
            sums[n] = sums[n] + (out[n] - g * xs[n])
            sums[2 + n] = sums[2 + n] + g
        return tuple(sums)

    zero = jnp.zeros((8, 128), F32)
    sums = lax.fori_loop(0, blocks, gather_sums, (zero,) * 4, unroll=blocks)
    sums = [jnp.sum(v, axis=0, keepdims=True) for v in sums]
    for n in range(2):
        wide[n, pl.ds(0, 8), :] = zero
        wide[n, pl.ds(8 * blocks + 8, 8), :] = zero
        mean = sums[n] / sums[2 + n]
        for t in range(blocks):
            wide[n, pl.ds(8 + t, 8, stride=blocks), :] = x[n, t] + mean
    start = pl.multiple_of(lax.axis_index("gx") * 8, 8)
    low = sublanes((8, 128)) < 4
    height = correct.shape[-2]
    rows = []
    for n in range(2):
        mine = wide[n, pl.ds(start + 8, 8), :]
        after = wide[n, pl.ds(start + 16, 8), :]
        before = wide[n, pl.ds(start, 8), :]
        rows += [mine, after, before] if height == 24 else [mine, jnp.where(low, after, before)]
    rows = jnp.concatenate(rows, axis=0)
    for half in range(2):
        y = exact_dot(rows, spread(half))
        correct[half, 0, 0] = y[0:height]
        correct[2 + half, 0, 0] = y[height : 2 * height]


def rise(level, K, X, M, RHS, SOLID, INV, source, last):
    a, b = M[level]
    prolong(level, X[level], a, SOLID[level], source)
    sweep(level, K, X[level], a, b, RHS[level], SOLID[level], INV[level])
    sweep(level, K, X[level], b, a, RHS[level], SOLID[level], INV[level], last=last)
    return X[level]


def ascend(K, X, M, RHS, SOLID, INV, correct):
    source = correct
    for level in (2, 1, 0):
        source = rise(level, K, X, M, RHS, SOLID, INV, source, level > 0)


def copy_state(sources, targets):
    for source, target in zip(sources, targets):
        target[...] = source[...]


def up_one(K, gathered, *refs):
    there, refs = refs[:GIVEN], refs[GIVEN:]
    kept, (i0, i1s, i2s, one, two) = refs[:KEPT], refs[KEPT : KEPT + 5]
    refs = refs[KEPT + 5 :]
    here, refs = kept + refs[: GIVEN - KEPT], refs[GIVEN - KEPT :]
    x1, r1, s1, m1, i1, x2, r2, s2, m2, i2, ma0, mb0, ma1, mb1, ma2, mb2 = refs[:16]
    natural, x3, ma3, mb3, r3, m3, s3, i3, wide, correct, pairs, arrived = refs[16:]
    moves = [
        pltpu.make_async_copy(there[n], here[n], arrived.at[n]) for n in range(GIVEN)
    ]
    for move in moves[::-1]:
        move.start()
    r0, m0, x0, s0, s1s, m1s, s2s, m2s, x1s, r1s, x2s, r2s, near, far = here
    solve_coarsest(K, gathered, gathered, natural, x3, ma3, mb3, r3, m3, s3, i3, wide, correct)
    for move in moves[3:]:
        move.wait()
    grow(
        levels_one_two((x1s, r1s, s1s, m1s), (x2s, r2s, s2s, m2s)),
        levels_one_two((x1, r1, s1, m1), (x2, r2, s2, m2)),
        near, far, is_even("gx"),
    )
    invert(1, K, s1, i1)
    invert(2, K, s2, i2)
    invert(0, K, s0, i0)
    invert(1, K, s1s, i1s)
    invert(2, K, s2s, i2s)
    M = ((ma0, mb0), (ma1, mb1), (ma2, mb2))
    X, RHS, SOLID, INV = (x0, x1, x2), (r0, r1, r2), (m0, m1, m2), (i0, i1, i2)
    source = rise(2, K, X, M, RHS, SOLID, INV, correct, True)
    source = rise(1, K, X, M, RHS, SOLID, INV, source, True)
    for move in moves[:3]:
        move.wait()
    rise(0, K, X, M, RHS, SOLID, INV, source, True)

    for f in range(F):
        for q in range(8):
            for h in range(2):
                for v in range(2):
                    part = slice(8 * v, 8 * v + 8)
                    pairs[f * 16 + q * 2 + h, v] = half_pair(
                        x0[f, q, 2 * h, part], x0[f, q, 2 * h + 1, part]
                    )
    pack_sides(lambda index, v: pairs[index, v], XTILES, one, two, is_even("gy"))


def up_two(
    K, gathered, statics, x0i, r0, s0, m0, i0, x1i, r1, m1, i1, x2i, r2, m2, i2,
    displacement, residual,
    x0, x1, x2, ma0, mb0, ma1, mb1, ma2, mb2,
    natural, x3, ma3, mb3, r3, m3, s3, i3, wide, correct, stage, rest,
):
    copy_state((x0i, x1i, x2i), (x0, x1, x2))
    solve_coarsest(K, gathered, statics, natural, x3, ma3, mb3, r3, m3, s3, i3, wide, correct)
    M = ((ma0, mb0), (ma1, mb1), (ma2, mb2))
    ascend(K, (x0, x1, x2), M, (r0, r1, r2), (m0, m1, m2), (i0, i1, i2), correct)
    mine = slice(0, 8)
    for q in range(8):
        for p in range(4):
            drives, xs = drive(0, K, x0, ma0, r0, m0, q, p, mine)
            s = s0[q, p, mine]
            for f in range(F):
                rest[f, q, p] = drives[f] - (s + (4.0 + K[f, f])) * xs[f]
    for f in range(F):
        for q in range(8):
            for h in range(2):
                for a, v in ((f, x0), (F + f, rest)):
                    stage[a, h, pl.ds(q, 8, stride=8), :] = half_pair(
                        v[f, q, 2 * h, mine], v[f, q, 2 * h + 1, mine]
                    )
    matrix = join_matrix(256, 4)
    for f in range(F):
        for out, a in ((displacement, f), (residual, F + f)):
            out[f] = exact_dot(jnp.concatenate([stage[a, 0], stage[a, 1]], axis=1), matrix)


def sds(*shape):
    return jax.ShapeDtypeStruct(shape, F32)


def field(level, height=16):
    return (F, ROWS[level], COLS[level], height, 128)


def plane(level, height=16):
    return (ROWS[level], COLS[level], height, 128)


def masked_scratch(height=16):
    out = []
    for level in range(3):
        tall = height if level else 16
        shape = (F, ROWS[level] + 2, COLS[level] + 2, tall, 128)
        out += [pltpu.VMEM(shape, F32), pltpu.VMEM(shape, F32)]
    return out


def coarsest_scratch(blocks, height=16):
    return [
        pltpu.VMEM((3, 8 * blocks, 128), F32),
        pltpu.VMEM((2, blocks, 8, 128), F32),
        pltpu.VMEM((2, blocks + 2, 8, 128), F32),
        pltpu.VMEM((2, blocks + 2, 8, 128), F32),
        pltpu.VMEM((2, blocks, 8, 128), F32),
        pltpu.VMEM((blocks, 8, 128), F32),
        pltpu.VMEM((blocks, 8, 128), F32),
        pltpu.VMEM((2, blocks, 8, 128), F32),
        pltpu.VMEM((2, 8 * blocks + 16, 128), F32),
        pltpu.VMEM((F, 1, 1, height, 128), F32),
    ]


def call(body, outs, scratch, args, smem=True, hbm=0):
    specs = [pl.BlockSpec(memory_space=pltpu.VMEM)] * (len(args) - hbm)
    specs += [pl.BlockSpec(memory_space=pltpu.HBM)] * hbm
    if smem:
        specs[0] = pl.BlockSpec(memory_space=pltpu.SMEM)
    args = args[: len(args) - hbm] + tuple(
        pltpu.with_memory_space_constraint(array, pltpu.HBM) for array in args[len(args) - hbm :]
    )
    kept = [isinstance(out, jax.ShapeDtypeStruct) for out in outs]
    return pl.pallas_call(
        body,
        out_shape=outs,
        in_specs=specs,
        out_specs=[
            pl.BlockSpec(memory_space=pltpu.VMEM if inside else pltpu.HBM) for inside in kept
        ],
        scratch_shapes=scratch,
        compiler_params=pltpu.CompilerParams(vmem_limit_bytes=30 * 1024 * 1024),
    )(*args)


def swap(axis, first, second):
    count = lax.axis_size(axis)
    near = [(i, i ^ 1) for i in range(count) if i ^ 1 < count]
    far = [(i, ((i - 1) ^ 1) + 1) for i in range(1, count) if ((i - 1) ^ 1) + 1 < count]
    return lax.ppermute(first, axis, near), lax.ppermute(second, axis, far)


def shards(source, reaction, coupling, solid0, solid1, solid2, solid3):
    blocks = lax.axis_size("gx")
    arrays = (source, reaction, solid0, solid1, solid2, solid3)
    packed = call(
        pack_kernel,
        [sds(TILES, 8, 128), sds(TILES // 2, 8, 128), sds(TILES // 2, 8, 128)],
        [pltpu.VMEM(array.shape, array.dtype) for array in arrays]
        + [
            pltpu.VMEM((6, 2, 64, 128), F32),
            pltpu.VMEM((32, 128), F32),
            pltpu.SemaphoreType.DMA((6,)),
        ],
        arrays,
        smem=False,
        hbm=6,
    )
    own, one, two = packed
    rows = swap("gx", one, two)
    side = call(
        functools.partial(side_kernel, TILES),
        [sds(TILES // 3, 2, 8, 128)] * 2,
        [],
        (own,) + rows,
        smem=False,
    )
    halo = (own,) + rows + swap("gy", *side)
    shapes = []
    for level in range(3):
        shapes += [field(level)] * 2 + [plane(level)] * 2
    shapes.append((MIDDLE, 8, 128))
    state = call(
        down_one,
        [pltpu.HBM(shape, F32) for shape in shapes + [(blocks, 3, 8, 128)]],
        [pltpu.VMEM(shape, F32) for shape in shapes]
        + [pltpu.VMEM(field(level), F32) for level in range(3)]
        + masked_scratch()
        + [
            pltpu.VMEM((F, 1, 1, 16, 128), F32),
            pltpu.VMEM((blocks, 3, 8, 128), F32),
            pltpu.SemaphoreType.DMA((STATE + 1,)),
            pltpu.SemaphoreType.DMA,
        ],
        (coupling,) + halo,
    )
    x0, r0, s0, m0, x1, r1, s1, m1, x2, r2, s2, m2, middle, payload = state
    near, far = swap("gx", middle, middle)
    statics = lax.all_to_all(payload, "gx", 0, 0)
    inner = [pltpu.VMEM(field(level), F32) for level in range(3)]
    tall = []
    for level in (1, 2):
        tall += [pltpu.VMEM(field(level, 24), F32)] * 2
        tall += [pltpu.VMEM(plane(level, 24), F32)] * 2
        tall += [pltpu.VMEM(field(level, 24), F32)]
    given = (r0, m0, x0, s0, s1, m1, s2, m2, x1, r1, x2, r2, near, far)
    r0, m0, x0, s0, s1, m1, s2, m2, i0, i1, i2, one, two = call(
        up_one,
        [sds(*array.shape) for array in given[:KEPT]]
        + [sds(*field(level)) for level in range(3)]
        + [sds(-(-XTILES // 3), 2, 8, 128)] * 2,
        [pltpu.VMEM(array.shape, F32) for array in given[KEPT:]]
        + tall
        + masked_scratch(24)
        + coarsest_scratch(blocks, 24)
        + [pltpu.VMEM((XTILES, 2, 8, 128), F32), pltpu.SemaphoreType.DMA((GIVEN,))],
        (coupling, statics) + given,
        hbm=GIVEN,
    )
    x0, x1, r1, x2, r2, payload = call(
        down_two,
        [sds(*field(0)), sds(*field(1)), sds(*field(1)), sds(*field(2)), sds(*field(2)),
         sds(blocks, 2, 8, 128)],
        masked_scratch() + [pltpu.VMEM((F, 1, 1, 16, 128), F32)],
        (coupling, x0) + swap("gy", one, two) + (r0, s0, m0, i0, s1, m1, i1, s2, m2, i2),
    )
    gathered = lax.all_to_all(payload, "gx", 0, 0)
    displacement, residual = call(
        up_two,
        [sds(F, 64, 256), sds(F, 64, 256)],
        inner + masked_scratch() + coarsest_scratch(blocks)
        + [pltpu.VMEM((2 * F, 2, 64, 128), F32), pltpu.VMEM((F, 8, 4, 8, 128), F32)],
        (coupling, gathered, statics, x0, r0, s0, m0, i0, x1, r1, m1, i1, x2, r2, m2, i2),
    )
    return displacement, residual


def solution(mesh):
    placed = (
        P(None, "gx", "gy"),
        P("gx", "gy"),
        P(),
        P("gx", "gy"),
        P("gx", "gy"),
        P("gx", "gy"),
        P("gx", "gy"),
    )
    return jax.shard_map(
        shards,
        mesh=mesh,
        in_specs=placed,
        out_specs=(P(None, "gx", "gy"), P(None, "gx", "gy")),
        check_vma=False,
    )
```
